32 devices in a mesh: dp: 8 (over y, x, core), expert: 4 (over z).
Axes of the slice: x: 2, y: 2, z: 4, core: 2. Of those that a mesh axis runs over, the one named last changes fastest.
Arguments:
- tokens: bfloat16 [12608, 768], P(('dp', 'expert')), may hold values from -6 to 6
- routes: int32 [12608, 2], P(('dp', 'expert')), may hold values from 0 to 15, all different within a row; in each aligned block of 197 rows (0 to 196, 197 to 393, ...) at most 41 rows name the same one
- gain_one: float32 [768], replicated, may hold values from 0.5 to 1.5
- shift_one: float32 [768], replicated, may hold values from -1 to 1
- w_qkv: bfloat16 [768, 2304], replicated, may hold values from -0.21875 to 0.21875
- qv_bias: float32 [2, 768], replicated, may hold values from -1 to 1
- w_out: bfloat16 [768, 768], replicated, may hold values from -2.5 to 2.5
- out_bias: float32 [768], replicated, may hold values from -1 to 1
- gain_two: float32 [768], replicated, may hold values from 0.5 to 1.5
- shift_two: float32 [768], replicated, may hold values from -1 to 1
- w_route: bfloat16 [768, 16], replicated, may hold values from -0.15625 to 0.15625
- w_in: bfloat16 [16, 768, 3072], P('expert'), may hold values from -0.21875 to 0.21875
- b_in: float32 [16, 3072], P('expert'), may hold values from -1 to 1
- w_back: bfloat16 [16, 3072, 768], P('expert'), may hold values from -3.5 to 3.5
- b_back: float32 [16, 768], P('expert'), may hold values from -15 to 15
- d_out: bfloat16 [12608, 768], P(('dp', 'expert')), may hold values from -6 to 6
Outputs:
- block_out: bfloat16 [12608, 768], P(('dp', 'expert'))
- input_grad: float32 [12608, 768], P(('dp', 'expert'))
- gain_one_grad: float32 [768], replicated
- shift_one_grad: float32 [768], replicated
- w_qkv_grad: float32 [768, 2304], replicated
- qv_bias_grad: float32 [2, 768], replicated
- w_out_grad: float32 [768, 768], replicated
- out_bias_grad: float32 [768], replicated
- gain_two_grad: float32 [768], replicated
- shift_two_grad: float32 [768], replicated
- w_route_grad: float32 [768, 16], replicated
- w_in_grad: float32 [16, 768, 3072], P('expert', 'dp')
- b_in_grad: float32 [16, 3072], P('expert', 'dp')
- w_back_grad: float32 [16, 3072, 768], P('expert', 'dp')
- b_back_grad: float32 [16, 768], P('expert', 'dp')
The draws below stay inside these ranges and needn't reach their ends.
Inputs may be any that keep to these rules, and one draw needn't show every extreme that they name: `routes`: within each aligned block of 197 rows (one device's tokens of one micro-batch) the two experts of a row differ, and no expert is named by more than 41 rows; some expert is named by exactly 41 rows of a block.
All inputs are finite; a program needn't handle non-finite values.
Results may differ from the reference program's by a relative error of at most 0.015.
Values may be sent and summed in bfloat16 or wider, within the bound.
A program may use at most 320 MiB of HBM per device.

```python
import math
from functools import partial
import jax
import jax.numpy as jnp
import numpy as np
from jax import lax

D = 768
HEADS = 12
HEAD_DIM = 64
FF = 3072
SEQ = 197
TOP = 2
EXPERTS = 16
ROWS_MB = 197
TOKENS = 12608
CAP = 41


def block_levels(own_key, dims, split, low, top_value):
    level, own = 1.0, jax.random.fold_in(own_key, 6)
    for dim, blocks in split:
        draws = jnp.exp(jax.random.uniform(jax.random.fold_in(own, dim), (blocks,), jnp.float32, low / len(split), top_value / len(split)))
        level = level * jnp.repeat(draws, dims[dim] // blocks).reshape([-1 if axis == dim else 1 for axis in range(len(dims))])
    return level


def shared_out(key, own, number, rows, count, top, bound, skew):
    sequence = jax.random.permutation(key, count)
    packed, usual = portions_of(count, rows * top, bound, skew, True), portions_of(count, rows * top, bound, skew, False)
    places = jnp.arange(count)

    def named(lengths, rotation):
        used = int((lengths > 0).sum())
        fixed = max(1, used // 4)
        shifted = fixed + (places - fixed + rotation * (used - fixed)) % max(1, count - fixed)
        return jnp.zeros((count,), jnp.int32).at[sequence[jnp.where(places < fixed, places, shifted)]].set(jnp.asarray(lengths, jnp.int32))

    lengths = jnp.where(number % 4 == 0, named(packed, number // 4), named(usual, number - number // 4 - 1))
    mixed = jax.random.permutation(jax.random.fold_in(own, 3), count)
    source_of, sink = mixed[0:count // 2 * 2:2], mixed[1:count // 2 * 2:2]
    slack = jnp.minimum(lengths[source_of] - 1, bound - lengths[sink]) // 2
    slack = jnp.where((source_of == sequence[0]) | (sink == sequence[0]) | (lengths[sink] == 0), 0, jnp.maximum(slack, 0))
    shifted = jax.random.randint(jax.random.fold_in(own, 4), (count // 2,), 0, 1 << 20) % (slack + 1)
    lengths = lengths.at[source_of].add(-shifted).at[sink].add(shifted)
    labels = jnp.searchsorted(jnp.cumsum(lengths), jnp.arange(rows * top), side="right").astype(jnp.int32)
    grid = labels.reshape(top, rows).T
    grid = grid[jax.random.permutation(jax.random.fold_in(own, 1), rows)]
    rotation = jax.random.randint(jax.random.fold_in(own, 2), (rows, 1), 0, top)
    return jnp.take_along_axis(grid, (jnp.arange(top)[None, :] + rotation) % top, axis=1)


def portions_of(number_of, total, bound, lean, full):
    loads = [(1 << 20) // math.isqrt(rank ** lean) + 1 for rank in range(1, number_of + 1)]
    largest = bound if full else min(bound, max(-(-total // number_of), total * loads[0] // sum(loads)))
    least = 1 if total - largest >= number_of - 1 else 0
    counts, spare = [largest] + [least] * (number_of - 1), total - largest - least * (number_of - 1)
    while spare > 0:
        candidates = [i for i in range(1, number_of) if counts[i] < largest] or [i for i in range(1, number_of) if counts[i] < bound]
        whole, remaining = sum([loads[i] for i in candidates]), spare
        for i in candidates:
            more = min(bound - counts[i], max(1, remaining * loads[i] // whole), spare)
            counts[i] = counts[i] + more
            spare = spare - more
    return np.array(counts)


def noise(stream_key, extent, width, most, cuts=(), kind=jnp.bfloat16):
    entries = jax.random.normal(stream_key, extent, jnp.float32) * width
    if len(cuts) > 0:
        entries = block_levels(stream_key, extent, cuts, -0.22, 0.18) * entries
    return jnp.clip(entries, min=-most, max=most).astype(kind)


def setup_inputs(seed: int = 0) -> dict:
    streams_of = jax.random.split(jax.random.key(seed), 17)
    tokens = noise(streams_of[0], (TOKENS, D), 1.0, 6.0, ((0, 32),))
    routes_keys = jax.random.split(jax.random.fold_in(streams_of[1], 1), TOKENS // ROWS_MB)
    routes_turns = jax.random.permutation(jax.random.fold_in(streams_of[1], 3), TOKENS // ROWS_MB)
    routes = jax.vmap(lambda own, number: shared_out(jax.random.fold_in(streams_of[1], 2), own, number, ROWS_MB, EXPERTS, TOP, CAP, 2))(routes_keys, routes_turns).reshape((TOKENS, TOP))
    gain_one = jnp.clip(1.0 + 0.1 * jax.random.normal(streams_of[2], (D,), jnp.float32), 0.5, 1.5)
    shift_one = noise(streams_of[3], (D,), 0.2, 1.0, (), jnp.float32)
    w_qkv = noise(streams_of[4], (D, 3 * D), D ** -0.5, 0.21875)
    qv_bias = noise(streams_of[5], (2, D), 0.2, 1.0, (), jnp.float32)
    w_out = noise(streams_of[6], (D, D), (max(1, D // 128)) ** -0.5, 2.5)
    out_bias = noise(streams_of[7], (D,), 0.2, 1.0, (), jnp.float32)
    gain_two = jnp.clip(1.0 + 0.1 * jax.random.normal(streams_of[8], (D,), jnp.float32), 0.5, 1.5)
    shift_two = noise(streams_of[9], (D,), 0.2, 1.0, (), jnp.float32)
    w_route = noise(streams_of[10], (D, EXPERTS), (2 * D) ** -0.5, 0.15625)
    w_in = noise(streams_of[11], (EXPERTS, D, FF), D ** -0.5, 0.21875, ((0, 4),))
    b_in = noise(streams_of[12], (EXPERTS, FF), 0.2, 1.0, ((0, 4),), jnp.float32)
    w_back = noise(streams_of[13], (EXPERTS, FF, D), (max(1, FF // 1024)) ** -0.5, 3.5, ((0, 4),))
    b_back = noise(streams_of[14], (EXPERTS, D), 3.0, 15.0, ((0, 4),), jnp.float32)
    d_out = noise(streams_of[15], (TOKENS, D), 1.0, 6.0, ((0, 32),))
    return dict(tokens=tokens, routes=routes, gain_one=gain_one, shift_one=shift_one, w_qkv=w_qkv, qv_bias=qv_bias, w_out=w_out, out_bias=out_bias, gain_two=gain_two, shift_two=shift_two, w_route=w_route, w_in=w_in, b_in=b_in, w_back=w_back, b_back=b_back, d_out=d_out)


HIGH = lax.Precision.HIGHEST
EPSILON = 1e-06

@jax.custom_vjp
def low(v):
    return lax.optimization_barrier(v.astype(jnp.bfloat16)).astype(jnp.float32)

@jax.custom_vjp
def low_back(v):
    return v

def low_keep(v):
    return (low(v), None)

def low_pass(kept, grad):
    return (grad,)

def back_keep(v):
    return (v, None)

def back_low(kept, grad):
    return (low(grad),)
low.defvjp(low_keep, low_pass)
low_back.defvjp(back_keep, back_low)

def layer_norm(value, gain, shift):
    center = value - lax.optimization_barrier(jnp.mean(value, axis=-1, keepdims=True))
    spread = lax.optimization_barrier(jnp.mean(center * center, axis=-1, keepdims=True))
    return center * lax.rsqrt(spread + EPSILON) * gain + shift

def attend(image):
    query, key_rows, value = image
    scores = low_back(jnp.einsum('shd,thd->hst', query, key_rows, precision=HIGH) * HEAD_DIM ** (-0.5))
    probs = jax.nn.softmax(scores, axis=-1)
    return jnp.einsum('hst,thd->shd', low(probs), value, precision=HIGH)

def expert_rows(parts):
    rows_in, weight_in, bias_in, weight_back, bias_back = parts
    hidden = low_back(jnp.dot(rows_in, weight_in, precision=HIGH) + bias_in)
    active = low(jax.nn.gelu(hidden))
    return low(low_back(jnp.dot(active, weight_back, precision=HIGH) + bias_back))

def slot_positions(routes):
    block_count = TOKENS // ROWS_MB
    chosen = routes.reshape(block_count, ROWS_MB * TOP)
    table = (chosen[:, :, None] == jnp.arange(EXPERTS, dtype=jnp.int32)[None, None, :]).astype(jnp.int32)
    before = jnp.cumsum(table, axis=1) - table
    slot = lax.optimization_barrier(jnp.sum(before * table, axis=2))
    base = (jnp.arange(block_count, dtype=jnp.int32) * CAP)[:, None]
    return (chosen.reshape(-1).astype(jnp.int32), (slot + base).reshape(-1).astype(jnp.int32))

def forward(expert_id, position, routes, x, gain_one, shift_one, w_qkv, qv_bias, w_out, out_bias, gain_two, shift_two, w_route, w_in, b_in, w_back, b_back):
    image_count = TOKENS // SEQ
    block_count = TOKENS // ROWS_MB
    normed = low(layer_norm(x, gain_one, shift_one))
    bias = jnp.concatenate([qv_bias[0], jnp.zeros_like(qv_bias[0]), qv_bias[1]])
    qkv = low(low_back(jnp.dot(normed, w_qkv, precision=HIGH) + bias))
    images = qkv.reshape(image_count, SEQ, 3, HEADS, HEAD_DIM)
    mixed = lax.map(jax.checkpoint(attend), (images[:, :, 0], images[:, :, 1], images[:, :, 2]))
    mixed = low(low_back(mixed.reshape(TOKENS, D)))
    resid = x + low_back(jnp.dot(mixed, w_out, precision=HIGH) + out_bias)
    inner = low(layer_norm(resid, gain_two, shift_two))
    logits = jnp.dot(inner, w_route, precision=HIGH)
    route_probs = jax.nn.softmax(logits, axis=-1)
    gates = jnp.take_along_axis(route_probs, routes, axis=1)
    source = jnp.repeat(inner, TOP, axis=0)
    buffer = jnp.zeros((EXPERTS, block_count * CAP, D), jnp.float32).at[expert_id, position].set(source)
    results = lax.map(jax.checkpoint(expert_rows), (low_back(buffer), w_in, b_in, w_back, b_back))
    picked = results[expert_id, position].reshape(TOKENS, TOP, D)
    return resid + lax.optimization_barrier(jnp.sum(gates[:, :, None] * picked, axis=1))

def reference(tokens, routes, gain_one, shift_one, w_qkv, qv_bias, w_out, out_bias, gain_two, shift_two, w_route, w_in, b_in, w_back, b_back, d_out):
    expert_id, position = slot_positions(routes)
    params = tuple((p.astype(jnp.float32) for p in (gain_one, shift_one, w_qkv, qv_bias, w_out, out_bias, gain_two, shift_two, w_route, w_in, b_in, w_back, b_back)))
    func = partial(forward, expert_id, position, routes)
    result, pull = jax.vjp(func, tokens.astype(jnp.float32), *params)
    grads = pull(d_out.astype(jnp.float32))
    return (result.astype(jnp.bfloat16), grads[0], grads[1], grads[2], grads[3], grads[4], grads[5], grads[6], grads[7], grads[8], grads[9], grads[10], grads[11], grads[12], grads[13])
```

```python
import jax
import jax.numpy as jnp
from jax import lax
from jax.experimental import pallas as pl
from jax.experimental.pallas import tpu as pltpu
from jax.sharding import PartitionSpec as P

HEADS = 12
HEAD_DIM = 64
SEQ = 197
TOP = 2
MB = 2
ROWS_MB = 197
D = 768


HIGH = lax.Precision.HIGHEST
EPSILON = 1e-06


def layer_norm(value, gain, shift):
    center = value - jnp.mean(value, axis=-1, keepdims=True)
    spread = jnp.mean(center * center, axis=-1, keepdims=True)
    return center * lax.rsqrt(spread + EPSILON) * gain + shift


def route_soft(logits):
    return jax.nn.softmax(logits, axis=-1)


def general_body(
    tokens,
    routes,
    gain_one,
    shift_one,
    w_qkv,
    qv_bias,
    w_out,
    out_bias,
    gain_two,
    shift_two,
    w_route,
    w_in,
    b_in,
    w_back,
    b_back,
    d_out,
):
    groups = lax.axis_size("expert")
    local = w_in.shape[0]
    experts = groups * local
    width = tokens.shape[1]
    rows = ROWS_MB
    cap = 5 * rows * TOP // (3 * experts)
    images = rows // SEQ
    scale = HEAD_DIM ** (-0.5)
    expert_ids = jnp.arange(experts, dtype=jnp.int32)
    w_route_wide = w_route.astype(jnp.float32)
    acc_gain_one = jnp.zeros_like(gain_one)
    acc_shift_one = jnp.zeros_like(shift_one)
    acc_qkv = jnp.zeros(w_qkv.shape, jnp.float32)
    acc_qv = jnp.zeros_like(qv_bias)
    acc_out = jnp.zeros(w_out.shape, jnp.float32)
    acc_out_bias = jnp.zeros_like(out_bias)
    acc_gain_two = jnp.zeros_like(gain_two)
    acc_shift_two = jnp.zeros_like(shift_two)
    acc_route = jnp.zeros(w_route.shape, jnp.float32)
    acc_expert = None
    outputs = []
    input_grads = []
    for part in range(MB):
        x = tokens[part * rows : (part + 1) * rows].astype(jnp.float32)
        route = routes[part * rows : (part + 1) * rows]
        cotan = d_out[part * rows : (part + 1) * rows].astype(jnp.float32)
        normed, ln_one_pull = jax.vjp(layer_norm, x, gain_one, shift_one)
        normed_low = normed.astype(jnp.bfloat16)
        bias = jnp.concatenate([qv_bias[0], jnp.zeros_like(qv_bias[0]), qv_bias[1]])
        qkv = (jnp.dot(normed_low, w_qkv, preferred_element_type=jnp.float32) + bias).astype(
            jnp.bfloat16
        )
        query = qkv[:, :width].reshape(images, SEQ, HEADS, HEAD_DIM)
        keys = qkv[:, width : 2 * width].reshape(images, SEQ, HEADS, HEAD_DIM)
        values = qkv[:, 2 * width :].reshape(images, SEQ, HEADS, HEAD_DIM)
        scores = (
            jnp.einsum("ishd,ithd->ihst", query, keys, preferred_element_type=jnp.float32) * scale
        )
        log_total = jax.nn.logsumexp(scores, axis=-1, keepdims=True)
        probs_low = jnp.exp(scores - log_total).astype(jnp.bfloat16)
        mixed = jnp.einsum("ihst,ithd->ishd", probs_low, values, preferred_element_type=jnp.float32)
        mixed = mixed.reshape(rows, width).astype(jnp.bfloat16)
        resid = x + jnp.dot(mixed, w_out, preferred_element_type=jnp.float32) + out_bias
        inner, ln_two_pull = jax.vjp(layer_norm, resid, gain_two, shift_two)
        inner_low = inner.astype(jnp.bfloat16)
        logits = jnp.dot(inner_low, w_route, preferred_element_type=jnp.float32)
        route_probs, soft_pull = jax.vjp(route_soft, logits)
        choose = (route[:, :, None] == expert_ids[None, None, :]).astype(jnp.float32)
        gates = jnp.einsum("rke,re->rk", choose, route_probs, precision=HIGH)
        flat_ids = route.reshape(-1)
        table = (flat_ids[:, None] == expert_ids[None, :]).astype(jnp.int32)
        order = jnp.arange(rows * TOP, dtype=jnp.int32)
        earlier = (order[None, :] < order[:, None]).astype(jnp.bfloat16)
        before = jnp.dot(
            earlier, table.astype(jnp.bfloat16), preferred_element_type=jnp.float32
        ).astype(jnp.int32)
        slot = jnp.sum(before * table, axis=1)
        dest = flat_ids * cap + slot
        sending = (
            jnp.zeros((experts * cap, width), jnp.bfloat16)
            .at[dest]
            .set(jnp.repeat(inner_low, TOP, axis=0))
        )
        sending = sending.reshape(groups, local, cap, width)
        received = lax.all_to_all(sending, "expert", split_axis=0, concat_axis=0, tiled=True)
        hidden = jnp.einsum("secd,edf->secf", received, w_in, preferred_element_type=jnp.float32)
        hidden = hidden + b_in[None, :, None, :]
        active = jax.nn.gelu(hidden).astype(jnp.bfloat16)
        result = jnp.einsum("secf,efd->secd", active, w_back, preferred_element_type=jnp.float32)
        result = (result + b_back[None, :, None, :]).astype(jnp.bfloat16)
        returned = lax.all_to_all(result, "expert", split_axis=0, concat_axis=0, tiled=True)
        returned, kept_rows, kept_hidden = (returned, received, hidden)
        picked = (
            returned.reshape(experts * cap, width)[dest]
            .reshape(rows, TOP, width)
            .astype(jnp.float32)
        )
        block = resid + jnp.sum(gates[:, :, None] * picked, axis=1)
        outputs.append(block.astype(jnp.bfloat16))
        grad_gate = jnp.sum(picked * cotan[:, None, :], axis=2)
        grad_picked = (gates[:, :, None] * cotan[:, None, :]).astype(jnp.bfloat16)
        grad_send = (
            jnp.zeros((experts * cap, width), jnp.bfloat16)
            .at[dest]
            .set(grad_picked.reshape(rows * TOP, width))
        )
        grad_send = grad_send.reshape(groups, local, cap, width)
        grad_recv = lax.all_to_all(grad_send, "expert", split_axis=0, concat_axis=0, tiled=True)
        active, gelu_pull = jax.vjp(jax.nn.gelu, kept_hidden)
        active_low = active.astype(jnp.bfloat16)
        grad_active = jnp.einsum(
            "secd,efd->secf", grad_recv, w_back, preferred_element_type=jnp.float32
        )
        grad_hidden = gelu_pull(grad_active)[0].astype(jnp.bfloat16)
        step_w_back = jnp.einsum(
            "secf,secd->efd", active_low, grad_recv, preferred_element_type=jnp.float32
        )
        step_b_back = jnp.sum(grad_recv.astype(jnp.float32), axis=(0, 2))
        step_w_in = jnp.einsum(
            "secd,secf->edf", kept_rows, grad_hidden, preferred_element_type=jnp.float32
        )
        step_b_in = jnp.sum(grad_hidden.astype(jnp.float32), axis=(0, 2))
        grad_rows = jnp.einsum(
            "secf,edf->secd", grad_hidden, w_in, preferred_element_type=jnp.float32
        )
        grad_rows = grad_rows.astype(jnp.bfloat16)
        grad_back = lax.all_to_all(grad_rows, "expert", split_axis=0, concat_axis=0, tiled=True)
        shares = (step_w_in, step_b_in, step_w_back, step_b_back)
        if acc_expert is None:
            acc_expert = shares
        else:
            acc_expert = tuple((a + b for a, b in zip(acc_expert, shares)))
        grad_inner = jnp.sum(
            grad_back.reshape(experts * cap, width)[dest]
            .reshape(rows, TOP, width)
            .astype(jnp.float32),
            axis=1,
        )
        grad_probs = jnp.einsum("rk,rke->re", grad_gate, choose, precision=HIGH)
        grad_logits = soft_pull(grad_probs)[0]
        acc_route = acc_route + jnp.einsum(
            "rd,re->de", inner_low.astype(jnp.float32), grad_logits, precision=HIGH
        )
        grad_inner = grad_inner + jnp.einsum("re,de->rd", grad_logits, w_route_wide, precision=HIGH)
        grad_ln_two, grad_gain_two, grad_shift_two = ln_two_pull(grad_inner)
        acc_gain_two = acc_gain_two + grad_gain_two
        acc_shift_two = acc_shift_two + grad_shift_two
        grad_resid = cotan + grad_ln_two
        grad_att = grad_resid.astype(jnp.bfloat16)
        acc_out = acc_out + jnp.einsum(
            "rd,re->de", mixed, grad_att, preferred_element_type=jnp.float32
        )
        acc_out_bias = acc_out_bias + jnp.sum(grad_att.astype(jnp.float32), axis=0)
        grad_mixed = jnp.einsum("re,de->rd", grad_att, w_out, preferred_element_type=jnp.float32)
        grad_mixed = grad_mixed.astype(jnp.bfloat16).reshape(images, SEQ, HEADS, HEAD_DIM)
        again = (
            jnp.einsum("ishd,ithd->ihst", query, keys, preferred_element_type=jnp.float32) * scale
        )
        probs = jnp.exp(again - log_total)
        grad_probs_att = jnp.einsum(
            "ishd,ithd->ihst", grad_mixed, values, preferred_element_type=jnp.float32
        )
        row_total = jnp.sum(probs * grad_probs_att, axis=-1, keepdims=True)
        grad_scores = (probs * (grad_probs_att - row_total)).astype(jnp.bfloat16)
        grad_query = (
            jnp.einsum("ihst,ithd->ishd", grad_scores, keys, preferred_element_type=jnp.float32)
            * scale
        )
        grad_keys = (
            jnp.einsum("ihst,ishd->ithd", grad_scores, query, preferred_element_type=jnp.float32)
            * scale
        )
        grad_values = jnp.einsum(
            "ihst,ishd->ithd",
            probs.astype(jnp.bfloat16),
            grad_mixed,
            preferred_element_type=jnp.float32,
        )
        grad_qkv = jnp.concatenate(
            [
                grad_query.reshape(rows, width),
                grad_keys.reshape(rows, width),
                grad_values.reshape(rows, width),
            ],
            axis=1,
        ).astype(jnp.bfloat16)
        acc_qkv = acc_qkv + jnp.einsum(
            "rd,re->de", normed_low, grad_qkv, preferred_element_type=jnp.float32
        )
        column_sums = jnp.sum(grad_qkv.astype(jnp.float32), axis=0)
        acc_qv = acc_qv + jnp.stack([column_sums[:width], column_sums[2 * width :]])
        grad_normed = jnp.einsum("re,de->rd", grad_qkv, w_qkv, preferred_element_type=jnp.float32)
        grad_ln_one, grad_gain_one, grad_shift_one = ln_one_pull(grad_normed)
        acc_gain_one = acc_gain_one + grad_gain_one
        acc_shift_one = acc_shift_one + grad_shift_one
        input_grads.append(grad_resid + grad_ln_one)
    expert_grads = (
        lax.psum_scatter(
            acc_expert[0].astype(jnp.bfloat16), "dp", scatter_dimension=1, tiled=True
        ).astype(jnp.float32),
        lax.psum_scatter(
            acc_expert[1].astype(jnp.bfloat16), "dp", scatter_dimension=1, tiled=True
        ).astype(jnp.float32),
        lax.psum_scatter(
            acc_expert[2].astype(jnp.bfloat16), "dp", scatter_dimension=1, tiled=True
        ).astype(jnp.float32),
        lax.psum_scatter(
            acc_expert[3].astype(jnp.bfloat16), "dp", scatter_dimension=1, tiled=True
        ).astype(jnp.float32),
    )
    shared = (
        acc_gain_one,
        acc_shift_one,
        acc_qkv,
        acc_qv,
        acc_out,
        acc_out_bias,
        acc_gain_two,
        acc_shift_two,
        acc_route,
    )
    shared = lax.psum(
        (
            shared[0],
            shared[1],
            shared[2],
            shared[3],
            shared[4],
            shared[5],
            shared[6],
            shared[7],
            shared[8],
        ),
        ("dp", "expert"),
    )
    return (
        jnp.concatenate(outputs, axis=0),
        jnp.concatenate(input_grads, axis=0),
        shared[0],
        shared[1],
        shared[2],
        shared[3],
        shared[4],
        shared[5],
        shared[6],
        shared[7],
        shared[8],
        expert_grads[0],
        expert_grads[1],
        expert_grads[2],
        expert_grads[3],
    )


F32, BF16 = jnp.float32, jnp.bfloat16
NZ = 4
LOCAL = 4
PAIRS = HEADS // 2
T = 208
KEYS = 256
CAP_ROWS = 48
ROWS = NZ * CAP_ROWS
CHUNK = 768
MESH = pl.DeviceIdType.MESH
NT = (((1,), (1,)), ((), ()))
TN = (((0,), (0,)), ((), ()))


def dot(a, b, dims=(((1,), (0,)), ((), ()))):
    return lax.dot_general(a, b, dims, preferred_element_type=F32)


def normal(value):
    center = value - jnp.mean(value, axis=-1, keepdims=True)
    scale = lax.rsqrt(jnp.mean(center * center, axis=-1, keepdims=True) + EPSILON)
    return center * scale, scale


def half_mask(which):
    lane = lax.broadcasted_iota(jnp.int32, (1, 128), 1)
    return ((lane < 64) if which == 0 else (lane >= 64)).astype(F32).astype(BF16)


def attention_probs(scores):
    key = lax.broadcasted_iota(jnp.int32, scores.shape, 1)
    scores = jnp.where(key < SEQ, scores, -1e30)
    top = jnp.max(scores, axis=-1, keepdims=True)
    raised = jnp.exp(scores - top)
    return raised / jnp.sum(raised, axis=-1, keepdims=True)


def route_table(rt_ref, mb):
    row = lax.broadcasted_iota(jnp.int32, (32, T), 0)
    part = lax.rem(row, 8)
    expert = jnp.where(part < LOCAL, (row // 8) * LOCAL + part, -7)
    first = rt_ref[mb, 0:1, :]
    second = rt_ref[mb, 1:2, :]
    return jnp.logical_or(expert == first, expert == second), part < LOCAL


def route_softmax(logits, real):
    logits = jnp.where(real, logits, -1e30)
    raised = jnp.exp(logits - jnp.max(logits, axis=0, keepdims=True))
    raised = jnp.where(real, raised, 0.0)
    return raised / jnp.sum(raised, axis=0, keepdims=True)


def pick_matrix(slots):
    index = lax.broadcasted_iota(jnp.int32, (CAP_ROWS, T), 0).astype(F32)
    return jnp.concatenate(
        [(index == slots[e : e + 1, :]).astype(F32) for e in range(LOCAL)], axis=0
    )


def dispatch_kernel(
    tok, rt, g1, s1, wqkv, bqkv, wout, bout, g2, s2, wrt, b_in, b_back, dout, w_in, w_back,
    qkv_o, mixed_o, resid_o, rp_o, gg_o, bb_o, bi_o, x_o, gp_o, act_o, gh_o, pb_o, pg_o,
    gi, gd, sg, qkv_s, mixed_s, inner_s, xs, gs, cs, rgs, ggs, wb1, wb2, act_st, gh_st, acc_o, acc_g,
    os_, grs, pb_s, pg_s,
    send_sem, recv_sem, d_sem, w_sem, st_sem, x_sem, p_sem,
):
    dp = lax.axis_index("dp")
    z = lax.axis_index("expert")

    def item_ref(kind, source, mb):
        return (gd, sg, gi)[kind].at[source, mb]

    def hop(up, kind, mb, h):
        source = z - h if up else z + h
        target = z + 1 if up else z - 1
        index = (0 if up else 1, kind * MB + mb, h)
        return pltpu.make_async_remote_copy(
            src_ref=item_ref(kind, source, mb),
            dst_ref=item_ref(kind, source, mb),
            send_sem=send_sem.at[index],
            recv_sem=recv_sem.at[index],
            device_id=(dp, target),
            device_id_type=MESH,
        )

    def leaves(up, h):
        return jnp.logical_and(z - h >= 0, z + 1 < NZ) if up else jnp.logical_and(z + h < NZ, z >= 1)

    def arrives(up, h):
        return (z - h - 1 >= 0) if up else (z + h + 1 < NZ)

    def start(kind, mb, h):
        for up in (True, False):
            @pl.when(leaves(up, h))
            def _():
                hop(up, kind, mb, h).start()

    def pass_on(kind, mb, h):
        for up in (True, False):
            @pl.when(arrives(up, h))
            def _():
                source = z - h - 1 if up else z + h + 1
                index = (0 if up else 1, kind * MB + mb, h)
                ref = item_ref(kind, source, mb)
                pltpu.make_async_remote_copy(
                    src_ref=ref, dst_ref=ref, send_sem=send_sem.at[index], recv_sem=recv_sem.at[index],
                    device_id=(dp, z - 1 if up else z + 1), device_id_type=MESH,
                ).wait_recv()
            if h + 1 < NZ - 1:
                @pl.when(leaves(up, h + 1))
                def _():
                    hop(up, kind, mb, h + 1).start()

    def weights(n, slot):
        e = lax.rem(n, 16) // 4
        f = lax.rem(n, 4)
        cols = pl.ds(pl.multiple_of(f * CHUNK, CHUNK), CHUNK)
        return (
            pltpu.make_async_copy(w_in.at[e, :, cols], wb1.at[slot], w_sem.at[0, slot]),
            pltpu.make_async_copy(w_back.at[e, cols, :], wb2.at[slot], w_sem.at[1, slot]),
        )

    own = [pltpu.make_async_copy(dout.at[mb], gd.at[z, mb], d_sem.at[mb]) for mb in range(MB)]
    for copy in own:
        copy.start()
    barrier = pltpu.get_barrier_semaphore()
    for up in (True, False):
        @pl.when(leaves(up, 0))
        def _():
            pl.semaphore_signal(
                barrier, inc=1, device_id=(dp, z + 1 if up else z - 1), device_id_type=MESH
            )
    pl.semaphore_wait(
        barrier, (z >= 1).astype(jnp.int32) + (z + 1 < NZ).astype(jnp.int32)
    )
    for copy in own:
        copy.wait()
    start(0, 0, 0)
    for copy in weights(0, 0):
        copy.start()

    qkv_s[T:KEYS, :] = jnp.zeros((KEYS - T, 3 * D), BF16)
    bb_o[...] = jnp.zeros_like(bb_o)
    bi_o[...] = jnp.zeros_like(bi_o)

    def forward(mb, carry):
        x = tok[mb].astype(F32)
        normed = (normal(x)[0] * g1[...] + s1[...]).astype(BF16)
        for c in range(3):
            cols = slice(c * D, (c + 1) * D)
            qkv_s[0:T, cols] = (dot(normed, wqkv[:, cols]) + bqkv[:, cols]).astype(BF16)

        def heads(p, carry):
            at = [pl.ds(pl.multiple_of(c * D + p * 128, 128), 128) for c in range(3)]
            q, k, v = qkv_s[0:T, at[0]], qkv_s[:, at[1]], qkv_s[:, at[2]]
            mixed = jnp.zeros((T, 128), F32)
            for which in (0, 1):
                mask = half_mask(which)
                probs = attention_probs(dot(q, k * mask, NT) * HEAD_DIM ** (-0.5))
                mixed = mixed + dot(probs.astype(BF16), v * mask)
            mixed_s[:, at[0]] = mixed.astype(BF16)
            return carry

        lax.fori_loop(0, PAIRS, heads, 0)
        qkv_o[mb] = qkv_s[0:T, :]
        mixed_o[mb] = mixed_s[...]
        resid = x + dot(mixed_s[...], wout[...]) + bout[...]
        resid_o[mb] = resid
        inner = (normal(resid)[0] * g2[...] + s2[...]).astype(BF16)
        gi[z, mb] = inner
        table, real = route_table(rt, mb)
        probs = route_softmax(dot(wrt[...], inner, NT), real)
        rp_o[mb] = probs
        earlier = (
            lax.broadcasted_iota(jnp.int32, (T, T), 0) < lax.broadcasted_iota(jnp.int32, (T, T), 1)
        ).astype(F32).astype(BF16)
        before = dot(table.astype(F32).astype(BF16), earlier)
        slots = jnp.where(table, before, -1.0)
        gates = jnp.where(table, probs, 0.0)
        for p in range(NZ):
            sg[z, mb, 0, p] = slots[8 * p : 8 * p + 8, :]
            sg[z, mb, 1, p] = gates[8 * p : 8 * p + 8, :]

        @pl.when(mb == 0)
        def _():
            start(1, 0, 0)
            start(2, 0, 0)

        return carry

    lax.fori_loop(0, MB, forward, 0)
    for h in range(NZ - 1):
        for kind in range(3):
            pass_on(kind, 0, h)
    for kind in range(3):
        start(kind, 1, 0)

    def micro(mb, carry):
        @pl.when(mb == 1)
        def _():
            for kind in range(3):
                pass_on(kind, 1, 2)

        def spread(src, carry):
            pick = pick_matrix(sg[src, mb, 0, z])
            gate = sg[src, mb, 1, z]
            low = pick.astype(BF16)
            rows_x = dot(low, gi[src, mb]).astype(BF16)
            rows_c = dot(low, gd[src, mb])
            at = pl.ds(pl.multiple_of(mb * ROWS + src * CAP_ROWS, 16), CAP_ROWS)
            here = pl.ds(pl.multiple_of(src * CAP_ROWS, 16), CAP_ROWS)
            for e in range(LOCAL):
                part = slice(e * CAP_ROWS, (e + 1) * CAP_ROWS)
                gate_rows = jnp.sum(pick[part] * gate[e : e + 1, :], axis=1, keepdims=True)
                grad = (rows_c[part] * gate_rows).astype(BF16)
                xs[e, at, :] = rows_x[part]
                gs[e, at, :] = grad
                cs[e, here, :] = rows_c[part].astype(BF16)
                rgs[e, here, :] = jnp.broadcast_to(gate_rows, (CAP_ROWS, 128))
                bb_o[e] += jnp.sum(grad.astype(F32), axis=0, keepdims=True)
            return carry

        lax.fori_loop(0, NZ, spread, 0)
        rows = pl.ds(pl.multiple_of(mb * ROWS, 16), ROWS)

        def expert(e, carry):
            acc_o[...] = jnp.zeros_like(acc_o)
            acc_g[...] = jnp.zeros_like(acc_g)

            def step(f, carry):
                n = mb * 16 + e * 4 + f
                slot = lax.rem(n, 2)

                @pl.when(n + 1 < 16 * MB)
                def _():
                    for copy in weights(n + 1, 1 - slot):
                        copy.start()

                for copy in weights(n, slot):
                    copy.wait()
                hid = dot(xs[e, rows, :], wb1[slot]) + b_in[e * 4 + f]
                square = hid * hid
                bend = jnp.tanh(hid * (0.7978845608 + (0.7978845608 * 0.044715) * square))
                half = 0.5 + 0.5 * bend
                act = (hid * half).astype(BF16)
                slope = half + (0.5 * hid) * (1.0 - bend * bend) * (
                    0.7978845608 + (3 * 0.7978845608 * 0.044715) * square
                )

                @pl.when(n >= 2)
                def _():
                    for copy in stores(n - 2, slot):
                        copy.wait()

                act_st[slot] = act
                acc_o[...] += dot(act, wb2[slot])
                grad = (dot(gs[e, rows, :], wb2[slot], NT) * slope).astype(BF16)
                gh_st[slot] = grad
                acc_g[...] += dot(grad, wb1[slot], NT)
                bi_o[e * 4 + f] += jnp.sum(grad.astype(F32), axis=0, keepdims=True)
                for copy in stores(n, slot):
                    copy.start()
                return carry

            lax.fori_loop(0, 4, step, 0)
            out = (acc_o[...] + b_back[e]).astype(BF16).astype(F32)
            gg = jnp.sum(out * cs[e].astype(F32), axis=1, keepdims=True)
            scaled = (out * rgs[e][:, 0:1]).astype(BF16)
            back = acc_g[...].astype(BF16)
            at = pl.ds(pl.multiple_of(e * CAP_ROWS, 16), CAP_ROWS)
            for src in range(NZ):
                part = slice(src * CAP_ROWS, (src + 1) * CAP_ROWS)
                os_[src, at, :] = scaled[part]
                grs[src, at, :] = back[part]
                ggs[src, at, :] = jnp.broadcast_to(gg[part], (CAP_ROWS, 128))

            @pl.when(jnp.logical_and(mb == 0, e == 1))
            def _():
                for kind in range(3):
                    pass_on(kind, 1, 0)

            @pl.when(jnp.logical_and(mb == 0, e == 3))
            def _():
                for kind in range(3):
                    pass_on(kind, 1, 1)

            return carry

        def stores(n, slot):
            m = n // 16
            e = lax.rem(n, 16) // 4
            f = lax.rem(n, 4)
            at = (e, pl.ds(pl.multiple_of(m * ROWS, 16), ROWS), pl.ds(pl.multiple_of(f * CHUNK, CHUNK), CHUNK))
            return (
                pltpu.make_async_copy(act_st.at[slot], act_o.at[at], st_sem.at[0, slot]),
                pltpu.make_async_copy(gh_st.at[slot], gh_o.at[at], st_sem.at[1, slot]),
            )

        lax.fori_loop(0, LOCAL, expert, 0)

        @pl.when(mb == 1)
        def _():
            for slot in (0, 1):
                for copy in stores(16 * MB - 2 + slot, slot):
                    copy.wait()

        def gather(src, carry):
            pick = pick_matrix(sg[src, mb, 0, z])
            low = pick.astype(BF16)
            n = mb * NZ + src
            slot = lax.rem(n, 2)

            @pl.when(n >= 2)
            def _():
                for copy in parts(n - 2, slot):
                    copy.wait()

            pb_s[slot] = dot(low, os_[src], TN).astype(BF16)
            pg_s[slot] = dot(low, grs[src], TN).astype(BF16)
            for copy in parts(n, slot):
                copy.start()
            for e in range(LOCAL):
                part = slice(e * CAP_ROWS, (e + 1) * CAP_ROWS)
                gg_o[src, mb, e : e + 1, :] = jnp.sum(
                    pick[part] * ggs[src, part, 0:1], axis=0, keepdims=True
                )
            return carry

        def parts(n, slot):
            src, m = lax.rem(n, NZ), n // NZ
            return (
                pltpu.make_async_copy(pb_s.at[slot], pb_o.at[src, m], p_sem.at[0, slot]),
                pltpu.make_async_copy(pg_s.at[slot], pg_o.at[src, m], p_sem.at[1, slot]),
            )

        lax.fori_loop(0, NZ, gather, 0)

        @pl.when(mb == 1)
        def _():
            for slot in (0, 1):
                for copy in parts(NZ * MB - 2 + slot, slot):
                    copy.wait()

        return carry

    gg_o[...] = jnp.zeros_like(gg_o)
    lax.fori_loop(0, MB, micro, 0)
    last = (
        pltpu.make_async_copy(xs, x_o, x_sem.at[0]),
        pltpu.make_async_copy(gs, gp_o, x_sem.at[1]),
    )
    for copy in last:
        copy.start()
    for copy in last:
        copy.wait()
    for mb in range(MB):
        for kind in range(3):
            for h in range(NZ - 1):
                for up in (True, False):
                    @pl.when(leaves(up, h))
                    def _():
                        hop(up, kind, mb, h).wait_send()


def dispatch_call(tok, rt, g1, s1, wqkv, bqkv, wout, bout, g2, s2, wrt, b_in, b_back, dout, w_in, w_back):
    vm = pl.BlockSpec(memory_space=pltpu.VMEM)
    hb = pl.BlockSpec(memory_space=pl.ANY)
    S = jax.ShapeDtypeStruct
    D = 768
    rows = MB * ROWS
    outs = [
        (S((MB, T, 3 * D), BF16), vm),
        (S((MB, T, D), BF16), vm),
        (S((MB, T, D), F32), vm),
        (S((MB, 32, T), F32), vm),
        (S((NZ, MB, 8, T), F32), vm),
        (S((LOCAL, 1, D), F32), vm),
        (S((LOCAL * 4, 1, CHUNK), F32), vm),
        (S((LOCAL, rows, D), BF16), hb),
        (S((LOCAL, rows, D), BF16), hb),
        (S((LOCAL, rows, 4 * CHUNK), BF16), hb),
        (S((LOCAL, rows, 4 * CHUNK), BF16), hb),
        (S((NZ, MB, T, D), BF16), hb),
        (S((NZ, MB, T, D), BF16), hb),
    ]
    V = pltpu.VMEM
    DMA = pltpu.SemaphoreType.DMA
    return pl.pallas_call(
        dispatch_kernel,
        out_shape=[o[0] for o in outs],
        in_specs=[vm] * 13 + [hb] * 3,
        out_specs=[o[1] for o in outs],
        scratch_shapes=[
            V((NZ, MB, T, D), BF16), V((NZ, MB, T, D), BF16), V((NZ, MB, 2, NZ, 8, T), F32),
            V((KEYS, 3 * D), BF16), V((T, D), BF16), V((8, 128), F32),
            V((LOCAL, rows, D), BF16), V((LOCAL, rows, D), BF16), V((LOCAL, ROWS, D), BF16),
            V((LOCAL, ROWS, 128), F32), V((NZ, ROWS, 128), F32),
            V((2, D, CHUNK), BF16), V((2, CHUNK, D), BF16),
            V((2, ROWS, CHUNK), BF16), V((2, ROWS, CHUNK), BF16),
            V((ROWS, D), F32), V((ROWS, D), F32),
            V((NZ, ROWS, D), BF16), V((NZ, ROWS, D), BF16),
            V((2, T, D), BF16), V((2, T, D), BF16),
            DMA((2, 3 * MB, NZ - 1)), DMA((2, 3 * MB, NZ - 1)), DMA((MB,)), DMA((2, 2)), DMA((2, 2)),
            DMA((2,)), DMA((2, 2)),
        ],
        compiler_params=pltpu.CompilerParams(
            collective_id=1, has_side_effects=True, vmem_limit_bytes=58 << 20
        ),
        name="dispatch",
    )(tok, rt, g1, s1, wqkv, bqkv, wout, bout, g2, s2, wrt, b_in, b_back, dout, w_in, w_back)

def fast_body(
    tokens, routes, gain_one, shift_one, w_qkv, qv_bias, w_out, out_bias, gain_two, shift_two,
    w_route, w_in, b_in, w_back, b_back, d_out,
):
    def windows(a):
        return jnp.pad(a.reshape(MB, SEQ, a.shape[1]), ((0, 0), (0, T - SEQ), (0, 0)))

    tok, dout = windows(tokens), windows(d_out)
    rt = jnp.pad(
        jnp.transpose(routes.reshape(MB, SEQ, TOP), (0, 2, 1)),
        ((0, 0), (0, 8 - TOP), (0, T - SEQ)), constant_values=-1,
    )
    row = lambda a: a.reshape(1, -1)
    bqkv = jnp.concatenate([qv_bias[0], jnp.zeros_like(qv_bias[0]), qv_bias[1]])
    wrt = jnp.pad(w_route.T.reshape(NZ, LOCAL, D), ((0, 0), (0, 8 - LOCAL), (0, 0))).reshape(32, D)
    (qkv, mixed, resid, rp, gg, bb, bi, xr, gp, act, gh, pb, pg) = dispatch_call(
        tok, rt, row(gain_one), row(shift_one), w_qkv, row(bqkv), w_out, row(out_bias),
        row(gain_two), row(shift_two), wrt, b_in.reshape(16, 1, CHUNK), b_back.reshape(LOCAL, 1, D),
        dout, w_in, w_back,
    )
    scale = HEAD_DIM ** (-0.5)
    pb = lax.psum_scatter(pb.astype(F32), "expert", scatter_dimension=0, tiled=False)
    pg = lax.psum_scatter(pg.astype(F32), "expert", scatter_dimension=0, tiled=False)
    gg = lax.all_to_all(gg, "expert", 0, 0, tiled=True)
    grad_gate = jnp.transpose(gg, (1, 0, 2, 3)).reshape(MB, 32, T)
    block = (resid + pb).astype(BF16)[:, :SEQ].reshape(MB * SEQ, D)
    table = jnp.stack([route_table(rt, mb)[0] for mb in range(MB)])
    g = jnp.where(table, grad_gate, 0.0)
    gl = rp * (g - jnp.sum(rp * g, axis=1, keepdims=True))
    cot = dout.astype(F32)
    n2, r2 = normal(resid)
    inner = (n2 * gain_two + shift_two).astype(BF16)
    acc_route = jnp.einsum("bet,btd->ed", gl, inner.astype(F32), precision=HIGH)
    gi = pg + jnp.einsum("bet,ed->btd", gl, wrt.astype(F32), precision=HIGH)
    acc_gain_two = jnp.sum(gi * n2, axis=(0, 1))
    acc_shift_two = jnp.sum(gi, axis=(0, 1))
    u = gi * gain_two
    grad_resid = cot + r2 * (
        u - jnp.mean(u, -1, keepdims=True) - n2 * jnp.mean(u * n2, -1, keepdims=True)
    )
    ga = grad_resid.astype(BF16)
    acc_out = jnp.einsum("btd,bte->de", mixed, ga, preferred_element_type=F32)
    acc_out_bias = jnp.sum(ga.astype(F32), axis=(0, 1))
    gm = jnp.einsum("bte,de->btd", ga, w_out, preferred_element_type=F32).astype(BF16)
    gm = gm[:, :SEQ].reshape(MB, SEQ, HEADS, HEAD_DIM)
    query, keys, values = [
        qkv[:, :SEQ, i * D : (i + 1) * D].reshape(MB, SEQ, HEADS, HEAD_DIM) for i in range(3)
    ]
    again = jnp.einsum("ishd,ithd->ihst", query, keys, preferred_element_type=F32) * scale
    probs = jax.nn.softmax(again, axis=-1)
    gpa = jnp.einsum("ishd,ithd->ihst", gm, values, preferred_element_type=F32)
    gsc = (probs * (gpa - jnp.sum(probs * gpa, -1, keepdims=True))).astype(BF16)
    gq = jnp.einsum("ihst,ithd->ishd", gsc, keys, preferred_element_type=F32) * scale
    gk = jnp.einsum("ihst,ishd->ithd", gsc, query, preferred_element_type=F32) * scale
    gv = jnp.einsum("ihst,ishd->ithd", probs.astype(BF16), gm, preferred_element_type=F32)
    rows = MB * SEQ
    gqkv = jnp.concatenate([a.reshape(rows, D) for a in (gq, gk, gv)], axis=1).astype(BF16)
    x = tokens.astype(F32)
    n1, r1 = normal(x)
    normed = (n1 * gain_one + shift_one).astype(BF16)
    acc_qkv = jnp.einsum("rd,re->de", normed, gqkv, preferred_element_type=F32)
    cs = jnp.sum(gqkv.astype(F32), axis=0)
    acc_qv = jnp.stack([cs[:D], cs[2 * D :]])
    gn = jnp.einsum("re,de->rd", gqkv, w_qkv, preferred_element_type=F32)
    acc_gain_one = jnp.sum(gn * n1, axis=0)
    acc_shift_one = jnp.sum(gn, axis=0)
    w = gn * gain_one
    input_grad = grad_resid[:, :SEQ].reshape(rows, D) + r1 * (
        w - jnp.mean(w, -1, keepdims=True) - n1 * jnp.mean(w * n1, -1, keepdims=True)
    )
    wb = jnp.einsum("erf,erd->efd", act, gp, preferred_element_type=F32).astype(BF16)
    wi = jnp.einsum("erd,erf->edf", xr, gh, preferred_element_type=F32).astype(BF16)
    scat = lambda a: lax.psum_scatter(a, "dp", scatter_dimension=1, tiled=True).astype(F32)
    shared = lax.psum(
        (acc_gain_one, acc_shift_one, acc_qkv, acc_qv, acc_out, acc_out_bias, acc_gain_two,
         acc_shift_two, acc_route.reshape(NZ, 8, D)[:, :LOCAL].reshape(16, D).T),
        ("dp", "expert"),
    )
    return (block, input_grad, *shared, scat(wi), scat(bi.reshape(LOCAL, 4 * CHUNK)), scat(wb), scat(bb.reshape(LOCAL, D)))


def solution(mesh):
    fast = mesh.shape["dp"] == 8 and mesh.shape["expert"] == NZ
    return jax.shard_map(
        fast_body if fast else general_body,
        mesh=mesh,
        in_specs=(
            P(("dp", "expert"), None),
            P(("dp", "expert"), None),
            P(),
            P(),
            P(),
            P(),
            P(),
            P(),
            P(),
            P(),
            P(),
            P("expert", None, None),
            P("expert", None),
            P("expert", None, None),
            P("expert", None),
            P(("dp", "expert"), None),
        ),
        out_specs=(
            P(("dp", "expert"), None),
            P(("dp", "expert"), None),
            P(),
            P(),
            P(),
            P(),
            P(),
            P(),
            P(),
            P(),
            P(),
            P("expert", "dp", None),
            P("expert", "dp"),
            P("expert", "dp", None),
            P("expert", "dp"),
        ),
        check_vma=False,
    )
```

```python
import jax
import jax.numpy as jnp
from jax import lax
from jax.experimental import pallas as pl
from jax.experimental.pallas import tpu as pltpu
from jax.sharding import PartitionSpec as P

HEADS = 12
HEAD_DIM = 64
SEQ = 197
TOP = 2
MB = 2
ROWS_MB = 197
D = 768


HIGH = lax.Precision.HIGHEST
EPSILON = 1e-06


def layer_norm(value, gain, shift):
    center = value - jnp.mean(value, axis=-1, keepdims=True)
    spread = jnp.mean(center * center, axis=-1, keepdims=True)
    return center * lax.rsqrt(spread + EPSILON) * gain + shift


def route_soft(logits):
    return jax.nn.softmax(logits, axis=-1)


def general_body(
    tokens,
    routes,
    gain_one,
    shift_one,
    w_qkv,
    qv_bias,
    w_out,
    out_bias,
    gain_two,
    shift_two,
    w_route,
    w_in,
    b_in,
    w_back,
    b_back,
    d_out,
):
    groups = lax.axis_size("expert")
    local = w_in.shape[0]
    experts = groups * local
    width = tokens.shape[1]
    rows = ROWS_MB
    cap = 5 * rows * TOP // (3 * experts)
    images = rows // SEQ
    scale = HEAD_DIM ** (-0.5)
    expert_ids = jnp.arange(experts, dtype=jnp.int32)
    w_route_wide = w_route.astype(jnp.float32)
    acc_gain_one = jnp.zeros_like(gain_one)
    acc_shift_one = jnp.zeros_like(shift_one)
    acc_qkv = jnp.zeros(w_qkv.shape, jnp.float32)
    acc_qv = jnp.zeros_like(qv_bias)
    acc_out = jnp.zeros(w_out.shape, jnp.float32)
    acc_out_bias = jnp.zeros_like(out_bias)
    acc_gain_two = jnp.zeros_like(gain_two)
    acc_shift_two = jnp.zeros_like(shift_two)
    acc_route = jnp.zeros(w_route.shape, jnp.float32)
    acc_expert = None
    outputs = []
    input_grads = []
    for part in range(MB):
        x = tokens[part * rows : (part + 1) * rows].astype(jnp.float32)
        route = routes[part * rows : (part + 1) * rows]
        cotan = d_out[part * rows : (part + 1) * rows].astype(jnp.float32)
        normed, ln_one_pull = jax.vjp(layer_norm, x, gain_one, shift_one)
        normed_low = normed.astype(jnp.bfloat16)
        bias = jnp.concatenate([qv_bias[0], jnp.zeros_like(qv_bias[0]), qv_bias[1]])
        qkv = (jnp.dot(normed_low, w_qkv, preferred_element_type=jnp.float32) + bias).astype(
            jnp.bfloat16
        )
        query = qkv[:, :width].reshape(images, SEQ, HEADS, HEAD_DIM)
        keys = qkv[:, width : 2 * width].reshape(images, SEQ, HEADS, HEAD_DIM)
        values = qkv[:, 2 * width :].reshape(images, SEQ, HEADS, HEAD_DIM)
        scores = (
            jnp.einsum("ishd,ithd->ihst", query, keys, preferred_element_type=jnp.float32) * scale
        )
        log_total = jax.nn.logsumexp(scores, axis=-1, keepdims=True)
        probs_low = jnp.exp(scores - log_total).astype(jnp.bfloat16)
        mixed = jnp.einsum("ihst,ithd->ishd", probs_low, values, preferred_element_type=jnp.float32)
        mixed = mixed.reshape(rows, width).astype(jnp.bfloat16)
        resid = x + jnp.dot(mixed, w_out, preferred_element_type=jnp.float32) + out_bias
        inner, ln_two_pull = jax.vjp(layer_norm, resid, gain_two, shift_two)
        inner_low = inner.astype(jnp.bfloat16)
        logits = jnp.dot(inner_low, w_route, preferred_element_type=jnp.float32)
        route_probs, soft_pull = jax.vjp(route_soft, logits)
        choose = (route[:, :, None] == expert_ids[None, None, :]).astype(jnp.float32)
        gates = jnp.einsum("rke,re->rk", choose, route_probs, precision=HIGH)
        flat_ids = route.reshape(-1)
        table = (flat_ids[:, None] == expert_ids[None, :]).astype(jnp.int32)
        order = jnp.arange(rows * TOP, dtype=jnp.int32)
        earlier = (order[None, :] < order[:, None]).astype(jnp.bfloat16)
        before = jnp.dot(
            earlier, table.astype(jnp.bfloat16), preferred_element_type=jnp.float32
        ).astype(jnp.int32)
        slot = jnp.sum(before * table, axis=1)
        dest = flat_ids * cap + slot
        sending = (
            jnp.zeros((experts * cap, width), jnp.bfloat16)
            .at[dest]
            .set(jnp.repeat(inner_low, TOP, axis=0))
        )
        sending = sending.reshape(groups, local, cap, width)
        received = lax.all_to_all(sending, "expert", split_axis=0, concat_axis=0, tiled=True)
        hidden = jnp.einsum("secd,edf->secf", received, w_in, preferred_element_type=jnp.float32)
        hidden = hidden + b_in[None, :, None, :]
        active = jax.nn.gelu(hidden).astype(jnp.bfloat16)
        result = jnp.einsum("secf,efd->secd", active, w_back, preferred_element_type=jnp.float32)
        result = (result + b_back[None, :, None, :]).astype(jnp.bfloat16)
        returned = lax.all_to_all(result, "expert", split_axis=0, concat_axis=0, tiled=True)
        returned, kept_rows, kept_hidden = (returned, received, hidden)
        picked = (
            returned.reshape(experts * cap, width)[dest]
            .reshape(rows, TOP, width)
            .astype(jnp.float32)
        )
        block = resid + jnp.sum(gates[:, :, None] * picked, axis=1)
        outputs.append(block.astype(jnp.bfloat16))
        grad_gate = jnp.sum(picked * cotan[:, None, :], axis=2)
        grad_picked = (gates[:, :, None] * cotan[:, None, :]).astype(jnp.bfloat16)
        grad_send = (
            jnp.zeros((experts * cap, width), jnp.bfloat16)
            .at[dest]
            .set(grad_picked.reshape(rows * TOP, width))
        )
        grad_send = grad_send.reshape(groups, local, cap, width)
        grad_recv = lax.all_to_all(grad_send, "expert", split_axis=0, concat_axis=0, tiled=True)
        active, gelu_pull = jax.vjp(jax.nn.gelu, kept_hidden)
        active_low = active.astype(jnp.bfloat16)
        grad_active = jnp.einsum(
            "secd,efd->secf", grad_recv, w_back, preferred_element_type=jnp.float32
        )
        grad_hidden = gelu_pull(grad_active)[0].astype(jnp.bfloat16)
        step_w_back = jnp.einsum(
            "secf,secd->efd", active_low, grad_recv, preferred_element_type=jnp.float32
        )
        step_b_back = jnp.sum(grad_recv.astype(jnp.float32), axis=(0, 2))
        step_w_in = jnp.einsum(
            "secd,secf->edf", kept_rows, grad_hidden, preferred_element_type=jnp.float32
        )
        step_b_in = jnp.sum(grad_hidden.astype(jnp.float32), axis=(0, 2))
        grad_rows = jnp.einsum(
            "secf,edf->secd", grad_hidden, w_in, preferred_element_type=jnp.float32
        )
        grad_rows = grad_rows.astype(jnp.bfloat16)
        grad_back = lax.all_to_all(grad_rows, "expert", split_axis=0, concat_axis=0, tiled=True)
        shares = (step_w_in, step_b_in, step_w_back, step_b_back)
        if acc_expert is None:
            acc_expert = shares
        else:
            acc_expert = tuple((a + b for a, b in zip(acc_expert, shares)))
        grad_inner = jnp.sum(
            grad_back.reshape(experts * cap, width)[dest]
            .reshape(rows, TOP, width)
            .astype(jnp.float32),
            axis=1,
        )
        grad_probs = jnp.einsum("rk,rke->re", grad_gate, choose, precision=HIGH)
        grad_logits = soft_pull(grad_probs)[0]
        acc_route = acc_route + jnp.einsum(
            "rd,re->de", inner_low.astype(jnp.float32), grad_logits, precision=HIGH
        )
        grad_inner = grad_inner + jnp.einsum("re,de->rd", grad_logits, w_route_wide, precision=HIGH)
        grad_ln_two, grad_gain_two, grad_shift_two = ln_two_pull(grad_inner)
        acc_gain_two = acc_gain_two + grad_gain_two
        acc_shift_two = acc_shift_two + grad_shift_two
        grad_resid = cotan + grad_ln_two
        grad_att = grad_resid.astype(jnp.bfloat16)
        acc_out = acc_out + jnp.einsum(
            "rd,re->de", mixed, grad_att, preferred_element_type=jnp.float32
        )
        acc_out_bias = acc_out_bias + jnp.sum(grad_att.astype(jnp.float32), axis=0)
        grad_mixed = jnp.einsum("re,de->rd", grad_att, w_out, preferred_element_type=jnp.float32)
        grad_mixed = grad_mixed.astype(jnp.bfloat16).reshape(images, SEQ, HEADS, HEAD_DIM)
        again = (
            jnp.einsum("ishd,ithd->ihst", query, keys, preferred_element_type=jnp.float32) * scale
        )
        probs = jnp.exp(again - log_total)
        grad_probs_att = jnp.einsum(
            "ishd,ithd->ihst", grad_mixed, values, preferred_element_type=jnp.float32
        )
        row_total = jnp.sum(probs * grad_probs_att, axis=-1, keepdims=True)
        grad_scores = (probs * (grad_probs_att - row_total)).astype(jnp.bfloat16)
        grad_query = (
            jnp.einsum("ihst,ithd->ishd", grad_scores, keys, preferred_element_type=jnp.float32)
            * scale
        )
        grad_keys = (
            jnp.einsum("ihst,ishd->ithd", grad_scores, query, preferred_element_type=jnp.float32)
            * scale
        )
        grad_values = jnp.einsum(
            "ihst,ishd->ithd",
            probs.astype(jnp.bfloat16),
            grad_mixed,
            preferred_element_type=jnp.float32,
        )
        grad_qkv = jnp.concatenate(
            [
                grad_query.reshape(rows, width),
                grad_keys.reshape(rows, width),
                grad_values.reshape(rows, width),
            ],
            axis=1,
        ).astype(jnp.bfloat16)
        acc_qkv = acc_qkv + jnp.einsum(
            "rd,re->de", normed_low, grad_qkv, preferred_element_type=jnp.float32
        )
        column_sums = jnp.sum(grad_qkv.astype(jnp.float32), axis=0)
        acc_qv = acc_qv + jnp.stack([column_sums[:width], column_sums[2 * width :]])
        grad_normed = jnp.einsum("re,de->rd", grad_qkv, w_qkv, preferred_element_type=jnp.float32)
        grad_ln_one, grad_gain_one, grad_shift_one = ln_one_pull(grad_normed)
        acc_gain_one = acc_gain_one + grad_gain_one
        acc_shift_one = acc_shift_one + grad_shift_one
        input_grads.append(grad_resid + grad_ln_one)
    expert_grads = (
        lax.psum_scatter(
            acc_expert[0].astype(jnp.bfloat16), "dp", scatter_dimension=1, tiled=True
        ).astype(jnp.float32),
        lax.psum_scatter(
            acc_expert[1].astype(jnp.bfloat16), "dp", scatter_dimension=1, tiled=True
        ).astype(jnp.float32),
        lax.psum_scatter(
            acc_expert[2].astype(jnp.bfloat16), "dp", scatter_dimension=1, tiled=True
        ).astype(jnp.float32),
        lax.psum_scatter(
            acc_expert[3].astype(jnp.bfloat16), "dp", scatter_dimension=1, tiled=True
        ).astype(jnp.float32),
    )
    shared = (
        acc_gain_one,
        acc_shift_one,
        acc_qkv,
        acc_qv,
        acc_out,
        acc_out_bias,
        acc_gain_two,
        acc_shift_two,
        acc_route,
    )
    shared = lax.psum(
        (
            shared[0],
            shared[1],
            shared[2],
            shared[3],
            shared[4],
            shared[5],
            shared[6],
            shared[7],
            shared[8],
        ),
        ("dp", "expert"),
    )
    return (
        jnp.concatenate(outputs, axis=0),
        jnp.concatenate(input_grads, axis=0),
        shared[0],
        shared[1],
        shared[2],
        shared[3],
        shared[4],
        shared[5],
        shared[6],
        shared[7],
        shared[8],
        expert_grads[0],
        expert_grads[1],
        expert_grads[2],
        expert_grads[3],
    )


F32, BF16 = jnp.float32, jnp.bfloat16
NZ = 4
LOCAL = 4
PAIRS = HEADS // 2
T = 208
KEYS = 256
CAP_ROWS = 48
ROWS = NZ * CAP_ROWS
CHUNK = 768
MESH = pl.DeviceIdType.MESH
NT = (((1,), (1,)), ((), ()))
TN = (((0,), (0,)), ((), ()))


def dot(a, b, dims=(((1,), (0,)), ((), ()))):
    return lax.dot_general(a, b, dims, preferred_element_type=F32)


def normal(value):
    center = value - jnp.mean(value, axis=-1, keepdims=True)
    scale = lax.rsqrt(jnp.mean(center * center, axis=-1, keepdims=True) + EPSILON)
    return center * scale, scale


def half_mask(which):
    lane = lax.broadcasted_iota(jnp.int32, (1, 128), 1)
    return ((lane < 64) if which == 0 else (lane >= 64)).astype(F32).astype(BF16)


def attention_probs(scores):
    key = lax.broadcasted_iota(jnp.int32, scores.shape, 1)
    scores = jnp.where(key < SEQ, scores, -1e30)
    top = jnp.max(scores, axis=-1, keepdims=True)
    raised = jnp.exp(scores - top)
    return raised / jnp.sum(raised, axis=-1, keepdims=True)


def route_table(rt_ref, mb):
    row = lax.broadcasted_iota(jnp.int32, (32, T), 0)
    part = lax.rem(row, 8)
    expert = jnp.where(part < LOCAL, (row // 8) * LOCAL + part, -7)
    first = rt_ref[mb, 0:1, :]
    second = rt_ref[mb, 1:2, :]
    return jnp.logical_or(expert == first, expert == second), part < LOCAL


def route_softmax(logits, real):
    logits = jnp.where(real, logits, -1e30)
    raised = jnp.exp(logits - jnp.max(logits, axis=0, keepdims=True))
    raised = jnp.where(real, raised, 0.0)
    return raised / jnp.sum(raised, axis=0, keepdims=True)


def pick_matrix(slots):
    index = lax.broadcasted_iota(jnp.int32, (CAP_ROWS, T), 0).astype(F32)
    return jnp.concatenate(
        [(index == slots[e : e + 1, :]).astype(F32) for e in range(LOCAL)], axis=0
    )


def dispatch_kernel(
    tok, rt, vec, wqkv, wout, wrt, b_in, b_back, dout, w_in, w_back,
    qkv_o, mixed_o, resid_o, rp_o, gg_o, bb_o, bi_o, x_o, gp_o, act_o, gh_o, pb_o, pg_o, home_o,
    gi, gd, sg, qkv_s, mixed_s, inner_s, xs, gs, cs, rgs, ggs, wb1, wb2, act_st, gh_st, acc_o, acc_g,
    os_, grs, pb_s, pg_s,
    send_sem, recv_sem, d_sem, w_sem, st_sem, x_sem, p_sem, h_send, h_recv,
):
    dp = lax.axis_index("dp")
    z = lax.axis_index("expert")

    def item_ref(kind, source, mb):
        return (gd, sg, gi)[kind].at[source, mb]

    def hop(up, kind, mb, h):
        source = z - h if up else z + h
        target = z + 1 if up else z - 1
        index = (0 if up else 1, kind * MB + mb, h)
        return pltpu.make_async_remote_copy(
            src_ref=item_ref(kind, source, mb),
            dst_ref=item_ref(kind, source, mb),
            send_sem=send_sem.at[index],
            recv_sem=recv_sem.at[index],
            device_id=(dp, target),
            device_id_type=MESH,
        )

    def leaves(up, h):
        return jnp.logical_and(z - h >= 0, z + 1 < NZ) if up else jnp.logical_and(z + h < NZ, z >= 1)

    def arrives(up, h):
        return (z - h - 1 >= 0) if up else (z + h + 1 < NZ)

    def start(kind, mb, h):
        for up in (True, False):
            @pl.when(leaves(up, h))
            def _():
                hop(up, kind, mb, h).start()

    def pass_on(kind, mb, h):
        for up in (True, False):
            @pl.when(arrives(up, h))
            def _():
                source = z - h - 1 if up else z + h + 1
                index = (0 if up else 1, kind * MB + mb, h)
                ref = item_ref(kind, source, mb)
                pltpu.make_async_remote_copy(
                    src_ref=ref, dst_ref=ref, send_sem=send_sem.at[index], recv_sem=recv_sem.at[index],
                    device_id=(dp, z - 1 if up else z + 1), device_id_type=MESH,
                ).wait_recv()
            if h + 1 < NZ - 1:
                @pl.when(leaves(up, h + 1))
                def _():
                    hop(up, kind, mb, h + 1).start()

    def weights(n, slot):
        e = lax.rem(n, 16) // 4
        f = lax.rem(n, 4)
        cols = pl.ds(pl.multiple_of(f * CHUNK, CHUNK), CHUNK)
        return (
            pltpu.make_async_copy(w_in.at[e, :, cols], wb1.at[slot], w_sem.at[0, slot]),
            pltpu.make_async_copy(w_back.at[e, cols, :], wb2.at[slot], w_sem.at[1, slot]),
        )

    own = [pltpu.make_async_copy(dout.at[mb], gd.at[z, mb], d_sem.at[mb]) for mb in range(MB)]
    for copy in own:
        copy.start()
    barrier = pltpu.get_barrier_semaphore()
    for d in range(1, NZ):
        pl.semaphore_signal(barrier, inc=1, device_id=(dp, lax.rem(z + d, NZ)), device_id_type=MESH)
    pl.semaphore_wait(barrier, NZ - 1)
    for copy in own:
        copy.wait()
    start(0, 0, 0)
    for copy in weights(0, 0):
        copy.start()

    qkv_s[T:KEYS, :] = jnp.zeros((KEYS - T, 3 * D), BF16)
    bb_o[...] = jnp.zeros_like(bb_o)
    bi_o[...] = jnp.zeros_like(bi_o)

    def forward(mb, carry):
        x = tok[mb].astype(F32)
        normed = (normal(x)[0] * vec[0:1] + vec[1:2]).astype(BF16)
        for c in range(3):
            cols = slice(c * D, (c + 1) * D)
            part = dot(normed, wqkv[:, cols])
            if c != 1:
                row = 5 if c == 0 else 6
                part = part + vec[row : row + 1]
            qkv_s[0:T, cols] = part.astype(BF16)

        def heads(p, carry):
            at = [pl.ds(pl.multiple_of(c * D + p * 128, 128), 128) for c in range(3)]
            q, k, v = qkv_s[0:T, at[0]], qkv_s[:, at[1]], qkv_s[:, at[2]]
            mixed = jnp.zeros((T, 128), F32)
            for which in (0, 1):
                mask = half_mask(which)
                probs = attention_probs(dot(q, k * mask, NT) * HEAD_DIM ** (-0.5))
                mixed = mixed + dot(probs.astype(BF16), v * mask)
            mixed_s[:, at[0]] = mixed.astype(BF16)
            return carry

        lax.fori_loop(0, PAIRS, heads, 0)
        qkv_o[mb] = qkv_s[0:T, :]
        mixed_o[mb] = mixed_s[...]
        resid = x + dot(mixed_s[...], wout[...]) + vec[4:5]
        resid_o[mb] = resid
        inner = (normal(resid)[0] * vec[2:3] + vec[3:4]).astype(BF16)
        gi[z, mb] = inner
        table, real = route_table(rt, mb)
        probs = route_softmax(dot(wrt[...], inner, NT), real)
        rp_o[mb] = probs
        earlier = (
            lax.broadcasted_iota(jnp.int32, (T, T), 0) < lax.broadcasted_iota(jnp.int32, (T, T), 1)
        ).astype(F32).astype(BF16)
        before = dot(table.astype(F32).astype(BF16), earlier)
        slots = jnp.where(table, before, -1.0)
        gates = jnp.where(table, probs, 0.0)
        for p in range(NZ):
            sg[z, mb, 0, p] = slots[8 * p : 8 * p + 8, :]
            sg[z, mb, 1, p] = gates[8 * p : 8 * p + 8, :]

        @pl.when(mb == 0)
        def _():
            start(1, 0, 0)
            start(2, 0, 0)

        return carry

    lax.fori_loop(0, MB, forward, 0)
    for h in range(NZ - 1):
        for kind in range(3):
            pass_on(kind, 0, h)
    for kind in range(3):
        start(kind, 1, 0)

    def micro(mb, carry):
        @pl.when(mb == 1)
        def _():
            for kind in range(3):
                pass_on(kind, 1, 2)

        def spread(src, carry):
            pick = pick_matrix(sg[src, mb, 0, z])
            gate = sg[src, mb, 1, z]
            low = pick.astype(BF16)
            rows_x = dot(low, gi[src, mb]).astype(BF16)
            rows_c = dot(low, gd[src, mb])
            at = pl.ds(pl.multiple_of(mb * ROWS + src * CAP_ROWS, 16), CAP_ROWS)
            here = pl.ds(pl.multiple_of(src * CAP_ROWS, 16), CAP_ROWS)
            for e in range(LOCAL):
                part = slice(e * CAP_ROWS, (e + 1) * CAP_ROWS)
                gate_rows = jnp.sum(pick[part] * gate[e : e + 1, :], axis=1, keepdims=True)
                grad = (rows_c[part] * gate_rows).astype(BF16)
                xs[e, at, :] = rows_x[part]
                gs[e, at, :] = grad
                cs[e, here, :] = rows_c[part].astype(BF16)
                rgs[e, here, :] = jnp.broadcast_to(gate_rows, (CAP_ROWS, 128))
                bb_o[e : e + 1, :] += jnp.sum(grad.astype(F32), axis=0, keepdims=True)
            return carry

        lax.fori_loop(0, NZ, spread, 0)
        rows = pl.ds(pl.multiple_of(mb * ROWS, 16), ROWS)

        def expert(e, carry):
            acc_o[...] = jnp.zeros_like(acc_o)
            acc_g[...] = jnp.zeros_like(acc_g)

            def step(f, carry):
                n = mb * 16 + e * 4 + f
                slot = lax.rem(n, 2)
                cols = pl.ds(pl.multiple_of(f * CHUNK, CHUNK), CHUNK)

                @pl.when(n + 1 < 16 * MB)
                def _():
                    for copy in weights(n + 1, 1 - slot):
                        copy.start()

                for copy in weights(n, slot):
                    copy.wait()
                hid = dot(xs[e, rows, :], wb1[slot]) + b_in[pl.ds(e, 1), cols]
                square = hid * hid
                bend = jnp.tanh(hid * (0.7978845608 + (0.7978845608 * 0.044715) * square))
                half = 0.5 + 0.5 * bend
                act = (hid * half).astype(BF16)
                slope = half + (0.5 * hid) * (1.0 - bend * bend) * (
                    0.7978845608 + (3 * 0.7978845608 * 0.044715) * square
                )

                @pl.when(n >= 2)
                def _():
                    for copy in stores(n - 2, slot):
                        copy.wait()

                act_st[slot] = act
                acc_o[...] += dot(act, wb2[slot])
                grad = (dot(gs[e, rows, :], wb2[slot], NT) * slope).astype(BF16)
                gh_st[slot] = grad
                acc_g[...] += dot(grad, wb1[slot], NT)
                bi_o[pl.ds(e, 1), cols] += jnp.sum(grad.astype(F32), axis=0, keepdims=True)
                for copy in stores(n, slot):
                    copy.start()
                return carry

            lax.fori_loop(0, 4, step, 0)
            out = (acc_o[...] + b_back[pl.ds(e, 1), :]).astype(BF16).astype(F32)
            gg = jnp.sum(out * cs[e].astype(F32), axis=1, keepdims=True)
            scaled = (out * rgs[e][:, 0:1]).astype(BF16)
            back = acc_g[...].astype(BF16)
            at = pl.ds(pl.multiple_of(e * CAP_ROWS, 16), CAP_ROWS)
            for src in range(NZ):
                part = slice(src * CAP_ROWS, (src + 1) * CAP_ROWS)
                os_[src, at, :] = scaled[part]
                grs[src, at, :] = back[part]
                ggs[src, at, :] = jnp.broadcast_to(gg[part], (CAP_ROWS, 128))

            @pl.when(jnp.logical_and(mb == 0, e == 1))
            def _():
                for kind in range(3):
                    pass_on(kind, 1, 0)

            @pl.when(jnp.logical_and(mb == 0, e == 3))
            def _():
                for kind in range(3):
                    pass_on(kind, 1, 1)

            return carry

        def stores(n, slot):
            m = n // 16
            e = lax.rem(n, 16) // 4
            f = lax.rem(n, 4)
            at = (e, pl.ds(pl.multiple_of(m * ROWS, 16), ROWS), pl.ds(pl.multiple_of(f * CHUNK, CHUNK), CHUNK))
            return (
                pltpu.make_async_copy(act_st.at[slot], act_o.at[at], st_sem.at[0, slot]),
                pltpu.make_async_copy(gh_st.at[slot], gh_o.at[at], st_sem.at[1, slot]),
            )

        lax.fori_loop(0, LOCAL, expert, 0)

        @pl.when(mb == 1)
        def _():
            for slot in (0, 1):
                for copy in stores(16 * MB - 2 + slot, slot):
                    copy.wait()

        @pl.when(mb == 1)
        def _():
            for src in range(NZ):
                kept(0, src).wait()
            for d in range(1, NZ):
                sent_home(d).wait_send()
            own_home().wait()

        def gather(src, carry):
            pick = pick_matrix(sg[src, mb, 0, z])
            low = pick.astype(BF16)
            pb_s[src] = dot(low, os_[src], TN).astype(BF16)
            pg_s[src] = dot(low, grs[src], TN).astype(BF16)
            kept(mb, src).start()
            for e in range(LOCAL):
                part = slice(e * CAP_ROWS, (e + 1) * CAP_ROWS)
                gg_o[src, mb, e : e + 1, :] = jnp.sum(
                    pick[part] * ggs[src, part, 0:1], axis=0, keepdims=True
                )

            @pl.when(mb == 1)
            def _():
                kept_grad(src).start()

            return carry

        lax.fori_loop(0, NZ, gather, 0)

        @pl.when(mb == 0)
        def _():
            for d in range(1, NZ):
                sent_home(d).start()
            own_home().start()

        @pl.when(mb == 1)
        def _():
            for src in range(NZ):
                kept(1, src).wait()
                kept_grad(src).wait()

        return carry

    def kept(mb, src):
        return pltpu.make_async_copy(pb_s.at[src], pb_o.at[mb, src], p_sem.at[0, src])

    def kept_grad(src):
        return pltpu.make_async_copy(pg_s.at[src], pg_o.at[src], p_sem.at[1, src])

    def sent_home(d):
        target = lax.rem(z + d, NZ)
        return pltpu.make_async_remote_copy(
            src_ref=pg_s.at[target], dst_ref=home_o.at[z], send_sem=h_send.at[d - 1], recv_sem=h_recv.at[d - 1],
            device_id=(dp, target), device_id_type=MESH,
        )

    def own_home():
        return pltpu.make_async_copy(pg_s.at[z], home_o.at[z], d_sem.at[0])

    gg_o[...] = jnp.zeros_like(gg_o)
    lax.fori_loop(0, MB, micro, 0)
    last = (
        pltpu.make_async_copy(xs, x_o, x_sem.at[0]),
        pltpu.make_async_copy(gs, gp_o, x_sem.at[1]),
    )
    for copy in last:
        copy.start()
    for copy in last:
        copy.wait()
    for d in range(1, NZ):
        source = lax.rem(z + NZ - d, NZ)
        pltpu.make_async_remote_copy(
            src_ref=home_o.at[source], dst_ref=home_o.at[source], send_sem=h_send.at[d - 1],
            recv_sem=h_recv.at[d - 1], device_id=(dp, source), device_id_type=MESH,
        ).wait_recv()
    for mb in range(MB):
        for kind in range(3):
            for h in range(NZ - 1):
                for up in (True, False):
                    @pl.when(leaves(up, h))
                    def _():
                        hop(up, kind, mb, h).wait_send()


def dispatch_call(*operands):
    vm = pl.BlockSpec(memory_space=pltpu.VMEM)
    hb = pl.BlockSpec(memory_space=pl.ANY)
    S = jax.ShapeDtypeStruct
    rows = MB * ROWS
    outs = [
        (S((MB, T, 3 * D), BF16), vm),
        (S((MB, T, D), BF16), vm),
        (S((MB, T, D), F32), vm),
        (S((MB, 32, T), F32), vm),
        (S((NZ, MB, 8, T), F32), vm),
        (S((LOCAL, D), F32), vm),
        (S((LOCAL, 4 * CHUNK), F32), vm),
        (S((LOCAL, rows, D), BF16), hb),
        (S((LOCAL, rows, D), BF16), hb),
        (S((LOCAL, rows, 4 * CHUNK), BF16), hb),
        (S((LOCAL, rows, 4 * CHUNK), BF16), hb),
        (S((MB, NZ, T, D), BF16), hb),
        (S((NZ, T, D), BF16), hb),
        (S((NZ, T, D), BF16), hb),
    ]
    V = pltpu.VMEM
    DMA = pltpu.SemaphoreType.DMA
    return pl.pallas_call(
        dispatch_kernel,
        out_shape=[o[0] for o in outs],
        in_specs=[vm] * 8 + [hb] * 3,
        out_specs=[o[1] for o in outs],
        scratch_shapes=[
            V((NZ, MB, T, D), BF16), V((NZ, MB, T, D), BF16), V((NZ, MB, 2, NZ, 8, T), F32),
            V((KEYS, 3 * D), BF16), V((T, D), BF16), V((8, 128), F32),
            V((LOCAL, rows, D), BF16), V((LOCAL, rows, D), BF16), V((LOCAL, ROWS, D), BF16),
            V((LOCAL, ROWS, 128), F32), V((NZ, ROWS, 128), F32),
            V((2, D, CHUNK), BF16), V((2, CHUNK, D), BF16),
            V((2, ROWS, CHUNK), BF16), V((2, ROWS, CHUNK), BF16),
            V((ROWS, D), F32), V((ROWS, D), F32),
            V((NZ, ROWS, D), BF16), V((NZ, ROWS, D), BF16),
            V((NZ, T, D), BF16), V((NZ, T, D), BF16),
            DMA((2, 3 * MB, NZ - 1)), DMA((2, 3 * MB, NZ - 1)), DMA((MB,)), DMA((2, 2)), DMA((2, 2)),
            DMA((2,)), DMA((2, NZ)), DMA((NZ - 1,)), DMA((NZ - 1,)),
        ],
        compiler_params=pltpu.CompilerParams(
            collective_id=1, has_side_effects=True, vmem_limit_bytes=58 << 20
        ),
        name="dispatch",
    )(*operands)


HIDDEN = 4 * CHUNK
PART = HIDDEN // 8
BAND = D // 8
SHARE = 400
EXTRA = 128
TOTAL = 8 * SHARE


def add_low(a, b):
    return (a.astype(F32) + b.astype(F32)).astype(BF16)


def grads_kernel(
    vec, rt, wrt, bb, bi, rp,
    tok, dout, wqkv, wout, qkv, mixed, resid, gg, xr, gp, act, gh, pb, pg, pg0,
    block_o, ig_o, ar_o, wi_o, wb_o, land_o,
    core_b, core_i, st1_b, st1_i, st2_b, st2_i, ar_core, ar_z, ar_xy1, ar_xy2, ar_t,
    ggr, quad,
    c_send, c_recv, s1_send, s1_recv, s2_send, s2_recv, r_send, r_recv, g_send, g_recv,
    ac_send, ac_recv, az_send, az_recv, ax_send, ax_recv, zz_send, zz_recv, cc_send, cc_recv,
    l_sem, o_sem, f_sem,
):
    dp = lax.axis_index("dp")
    z = lax.axis_index("expert")
    y, x, c = dp // 4, lax.rem(dp // 2, 2), lax.rem(dp, 2)
    yx = y * 2 + x
    partner = (yx * 2 + (1 - c), z)
    flips = ((y * 2 + (1 - x)), ((1 - y) * 2 + x))
    across = (1 - y) * 2 + (1 - x)

    def remote(src, dst, ssem, rsem, target):
        return pltpu.make_async_remote_copy(
            src_ref=src, dst_ref=dst, send_sem=ssem, recv_sem=rsem, device_id=target, device_id_type=MESH
        )

    barrier = pltpu.get_barrier_semaphore()
    for target in [partner, (flips[0] * 2 + c, z), (flips[1] * 2 + c, z)]:
        pl.semaphore_signal(barrier, inc=1, device_id=target, device_id_type=MESH)
    for d in range(1, NZ):
        pl.semaphore_signal(barrier, inc=1, device_id=(dp, lax.rem(z + d, NZ)), device_id_type=MESH)
    pl.semaphore_wait(barrier, 6)

    def gate_copy(d):
        return remote(gg.at[lax.rem(z + d, NZ)], ggr.at[z], g_send.at[d - 1], g_recv.at[d - 1], (dp, lax.rem(z + d, NZ)))

    for d in range(1, NZ):
        gate_copy(d).start()
    own_gate = pltpu.make_async_copy(gg.at[z], ggr.at[z], l_sem.at[0])
    own_gate.start()

    def home(item, d):
        target = lax.rem(z + d, NZ)
        part = pg.at[target] if item == 0 else pb.at[item - 1, target]
        return remote(
            part, land_o.at[item, z], r_send.at[item, d - 1], r_recv.at[item, d - 1], (dp, target)
        )

    def arrived(item):
        for d in range(1, NZ):
            source = lax.rem(z + NZ - d, NZ)
            ref = land_o.at[item, source]
            remote(ref, ref, r_send.at[item, d - 1], r_recv.at[item, d - 1], (dp, source)).wait_recv()

    def load(sources):
        copies = [pltpu.make_async_copy(ref, quad.at[i], l_sem.at[1 + i]) for i, ref in enumerate(sources)]
        for copy in copies:
            copy.start()
        for copy in copies:
            copy.wait()

    def load_item(item):
        arrived(item)
        own = pg.at[z] if item == 0 else pb.at[item - 1, z]
        load([own] + [land_o.at[item, lax.rem(z + d, NZ)] for d in range(1, NZ)])

    def quad_sum():
        return (quad[0].astype(F32) + quad[1].astype(F32)) + (quad[2].astype(F32) + quad[3].astype(F32))

    def middle(arr, flow, mb, dest):
        return jnp.logical_and(z > dest, z < NZ - 1) if flow == 0 else jnp.logical_and(z < dest, z > 0)

    cores, lands1, lands2 = (core_b, core_i), (st1_b, st1_i), (st2_b, st2_i)

    def core_copy(kind, e, src):
        return remote(src, cores[kind].at[e], c_send.at[kind, e], c_recv.at[kind, e], partner)

    def hop1(kind, e, slot):
        block = flips[kind] if slot == 0 else across
        return remote(
            cores[kind].at[e, block], lands1[kind].at[e, slot],
            s1_send.at[kind, e, slot], s1_recv.at[kind, e, slot], (flips[kind] * 2 + c, z),
        )

    def hop2(kind, e):
        return remote(
            cores[kind].at[e, flips[1 - kind]], lands2[kind].at[e],
            s2_send.at[kind, e], s2_recv.at[kind, e], (flips[1 - kind] * 2 + c, z),
        )

    def send1(kind, e):
        for slot in (1, 0):
            hop1(kind, e, slot).start()

    def turn(kind, e):
        ref = cores[kind]
        hop1(kind, e, 1).wait_recv()
        ref[e, flips[1 - kind]] = add_low(ref[e, flips[1 - kind]], lands1[kind][e, 1])
        hop2(kind, e).start()
        hop1(kind, e, 0).wait_recv()
        ref[e, yx] = add_low(ref[e, yx], lands1[kind][e, 0])

    outs = (wb_o, wi_o)

    def result(kind, e):
        return pltpu.make_async_copy(lands2[kind].at[e], outs[kind].at[e], f_sem.at[kind, e])

    def finish(kind, e):
        hop2(kind, e).wait_recv()
        lands2[kind][e] = add_low(lands2[kind][e], cores[kind][e, yx])
        result(kind, e).start()

    for item in range(3):
        for d in range(1, NZ):
            home(item, d).start()

    def weight_grads(wg_b, wg_i, act_s, gh_s, x_s, gp_s, xp):
        def fetch(e, which):
            pairs = ((act, act_s), (gp, gp_s), (xr, x_s), (gh, gh_s))
            return [
                pltpu.make_async_copy(pairs[i][0].at[e], pairs[i][1], o_sem.at[i]) for i in which
            ]

        def pull(e, which):
            for copy in fetch(e, which):
                copy.start()

        def ready(e, which):
            for copy in fetch(e, which):
                copy.wait()

        pull(0, (0, 1, 2, 3))

        def one(e, carry):
            def back_block(k, side):
                at = pl.ds(pl.multiple_of((2 * k + side) * PART, 128), PART)
                return dot(act_s[:, at], gp_s[...], TN)

            ready(e, (0, 1))

            @pl.when(e > 0)
            def _():
                core_copy(0, e - 1, wg_b).wait_send()

            def other_b(k, carry):
                wg_b[k] = back_block(k, 1 - c).astype(BF16)
                return carry

            lax.fori_loop(0, 4, other_b, 0)
            core_copy(0, e, wg_b).start()
            ready(e, (2, 3))
            for side in (0, 1):
                for k in range(4):
                    band = (2 * k + side) * BAND
                    xp[side, :, k * BAND : (k + 1) * BAND] = x_s[:, band : band + BAND]

            @pl.when(e > 0)
            def _():
                core_copy(1, e - 1, wg_i).wait_send()

            def other_i(f, carry):
                at = pl.ds(pl.multiple_of(f * CHUNK, 128), CHUNK)
                grad = dot(xp[1 - c], gh_s[:, at], TN).astype(BF16)
                for k in range(4):
                    wg_i[k, :, at] = grad[k * BAND : (k + 1) * BAND]
                return carry

            lax.fori_loop(0, 4, other_i, 0)
            core_copy(1, e, wg_i).start()
            core_copy(0, e, wg_b).wait_recv()

            def own_b(k, carry):
                core_b[e, k] = (core_b[e, k].astype(F32) + back_block(k, c)).astype(BF16)
                return carry

            lax.fori_loop(0, 4, own_b, 0)

            @pl.when(e < LOCAL - 1)
            def _():
                send1(0, e)
                pull(e + 1, (0, 1))

            core_copy(1, e, wg_i).wait_recv()

            def own_i(f, carry):
                at = pl.ds(pl.multiple_of(f * CHUNK, 128), CHUNK)
                grad = dot(xp[c], gh_s[:, at], TN)
                for k in range(4):
                    core_i[e, k, :, at] = (
                        core_i[e, k, :, at].astype(F32) + grad[k * BAND : (k + 1) * BAND]
                    ).astype(BF16)
                return carry

            lax.fori_loop(0, 4, own_i, 0)

            @pl.when(e < LOCAL - 1)
            def _():
                send1(1, e)
                pull(e + 1, (2, 3))

            return carry

        lax.fori_loop(0, LOCAL, one, 0)
        core_copy(0, LOCAL - 1, wg_b).wait_send()
        core_copy(1, LOCAL - 1, wg_i).wait_send()

    V = pltpu.VMEM
    rows = MB * ROWS
    pl.run_scoped(
        weight_grads,
        V((4, PART, D), BF16), V((4, BAND, HIDDEN), BF16), V((rows, HIDDEN), BF16), V((rows, HIDDEN), BF16),
        V((rows, D), BF16), V((rows, D), BF16), V((2, rows, D // 2), BF16),
    )

    def attention_grads(gqkv_s, nor_s, gat_s, mix_s, ext):
        def inside(wqkv_s, wout_s, qkv_s, tok_s, dout_s, res_s, gres, gm_s):
            loads = [
                pltpu.make_async_copy(src, dst, o_sem.at[4 + i])
                for i, (src, dst) in enumerate(
                    ((wqkv, wqkv_s), (wout, wout_s), (resid, res_s), (mixed, mix_s))
                )
            ]
            for copy in loads:
                copy.start()
            ext[...] = jnp.zeros_like(ext)
            qkv_s[T:KEYS, :] = jnp.zeros((KEYS - T, 3 * D), BF16)
            for d in range(1, NZ):
                gate_copy(d).wait_send()
                source = lax.rem(z + NZ - d, NZ)
                remote(ggr.at[source], ggr.at[source], g_send.at[d - 1], g_recv.at[d - 1], (dp, source)).wait_recv()
            own_gate.wait()
            for copy in loads:
                copy.wait()

            def image(mb, carry):
                @pl.when(mb == 0)
                def _():
                    load([pg0.at[p] for p in range(NZ)])

                @pl.when(mb == 1)
                def _():
                    load_item(0)

                fetches = [
                    pltpu.make_async_copy(src.at[mb], dst, o_sem.at[8 + i])
                    for i, (src, dst) in enumerate(((qkv, qkv_s.at[0:T]), (dout, dout_s), (tok, tok_s)))
                ]
                for fetch in fetches:
                    fetch.start()
                table, _ = route_table(rt, mb)
                gates = jnp.concatenate([ggr[p, mb] for p in range(NZ)], axis=0)
                g = jnp.where(table, gates, 0.0)
                probs = rp[mb]
                gl = (probs * (g - jnp.sum(probs * g, axis=0, keepdims=True))).astype(BF16)
                n2, r2 = normal(res_s[mb])
                inner = (n2 * vec[2:3] + vec[3:4]).astype(BF16)
                wr = dot(gl, inner)
                for p in range(NZ):
                    ext[8 + LOCAL * p : 8 + LOCAL * (p + 1), :] += wr[8 * p : 8 * p + LOCAL]
                gi = quad_sum() + dot(gl, wrt[...], TN)
                ext[5:6, :] += jnp.sum(gi * n2, axis=0, keepdims=True)
                ext[6:7, :] += jnp.sum(gi, axis=0, keepdims=True)
                u = gi * vec[2:3]
                fetches[1].wait()
                grad = dout_s[...].astype(F32) + r2 * (
                    u - jnp.mean(u, -1, keepdims=True) - n2 * jnp.mean(u * n2, -1, keepdims=True)
                )
                gres[mb] = grad
                low = grad.astype(BF16)
                gat_s[mb] = low
                ext[4:5, :] += jnp.sum(low.astype(F32), axis=0, keepdims=True)
                gm_s[...] = dot(low, wout_s[...], NT).astype(BF16)
                fetches[0].wait()

                def heads(p, carry):
                    at = [pl.ds(pl.multiple_of(i * D + p * 128, 128), 128) for i in range(3)]
                    q, k, v = qkv_s[0:T, at[0]], qkv_s[:, at[1]], qkv_s[:, at[2]]
                    gm = gm_s[:, at[0]]
                    gq = jnp.zeros((T, 128), F32)
                    gk = jnp.zeros((KEYS, 128), F32)
                    gv = jnp.zeros((KEYS, 128), F32)
                    for which in (0, 1):
                        mask = half_mask(which)
                        km = k * mask
                        prob = attention_probs(dot(q, km, NT) * HEAD_DIM ** (-0.5))
                        gpr = dot(gm, v * mask, NT)
                        gs = (prob * (gpr - jnp.sum(prob * gpr, axis=-1, keepdims=True))).astype(BF16)
                        gq = gq + dot(gs, km)
                        gk = gk + dot(gs, q * mask, TN)
                        gv = gv + dot(prob.astype(BF16), gm * mask, TN)
                    gqkv_s[mb, :, at[0]] = (gq * HEAD_DIM ** (-0.5)).astype(BF16)
                    gqkv_s[mb, :, at[1]] = (gk[0:T] * HEAD_DIM ** (-0.5)).astype(BF16)
                    gqkv_s[mb, :, at[2]] = gv[0:T].astype(BF16)
                    return carry

                lax.fori_loop(0, PAIRS, heads, 0)
                for row, i in ((2, 0), (3, 2)):
                    ext[row : row + 1, :] += jnp.sum(
                        gqkv_s[mb, :, i * D : (i + 1) * D].astype(F32), axis=0, keepdims=True
                    )
                gn = dot(gqkv_s[mb], wqkv_s[...], NT)
                fetches[2].wait()
                n1, r1 = normal(tok_s[...].astype(F32))
                nor_s[mb] = (n1 * vec[0:1] + vec[1:2]).astype(BF16)
                ext[0:1, :] += jnp.sum(gn * n1, axis=0, keepdims=True)
                ext[1:2, :] += jnp.sum(gn, axis=0, keepdims=True)
                w = gn * vec[0:1]
                gres[mb] += r1 * (
                    w - jnp.mean(w, -1, keepdims=True) - n1 * jnp.mean(w * n1, -1, keepdims=True)
                )
                pltpu.make_async_copy(gres.at[mb], ig_o.at[mb], o_sem.at[11 + mb]).start()
                return carry

            lax.fori_loop(0, MB, image, 0)
            for mb in range(MB):
                pltpu.make_async_copy(gres.at[mb], ig_o.at[mb], o_sem.at[11 + mb]).wait()

        pl.run_scoped(
            inside,
            V((D, 3 * D), BF16), V((D, D), BF16), V((KEYS, 3 * D), BF16), V((T, D), BF16), V((T, D), BF16),
            V((MB, T, D), F32), V((MB, T, D), F32), V((T, D), BF16),
        )

        def shared(a):
            for zz in range(NZ):
                @pl.when(z == zz)
                def _():
                    at = 24 + 5 * LOCAL * zz
                    ext[at : at + LOCAL, :] = bb[...]
                    for f in range(4):
                        ext[at + LOCAL * (f + 1) : at + LOCAL * (f + 2), :] = bi[:, f * CHUNK : (f + 1) * CHUNK]
            for i in range(3):
                total = jnp.zeros((D, D), F32)
                for mb in range(MB):
                    total = total + dot(nor_s[mb], gqkv_s[mb, :, i * D : (i + 1) * D], TN)
                a[i * D : (i + 1) * D, :] = total.astype(BF16)
            total = jnp.zeros((D, D), F32)
            for mb in range(MB):
                total = total + dot(mix_s[mb], gat_s[mb], TN)
            a[3 * D : 4 * D, :] = total.astype(BF16)
            a[4 * D : TOTAL, :] = ext[...].astype(BF16)

            def share(side, zz):
                return pl.ds(pl.multiple_of((side * NZ + zz) * SHARE, 16), SHARE)

            def to_core(zz):
                return remote(a.at[share(1 - c, zz)], ar_core.at[zz], ac_send.at[zz], ac_recv.at[zz], partner)

            for zz in range(NZ):
                to_core(zz).start()
            for kind in (0, 1):
                turn(kind, 0)

            def along(flow, zz, slot):
                return remote(
                    a.at[share(c, zz)], ar_z.at[flow, slot], az_send.at[flow, slot], az_recv.at[flow, slot],
                    (dp, z - 1 if flow == 0 else z + 1),
                )

            for j in range(NZ):
                zz = j
                to_core(zz).wait_recv()
                a[share(c, zz), :] = add_low(a[share(c, zz), :], ar_core[zz])
            for j in range(NZ - 1):
                @pl.when(z == NZ - 1)
                def _():
                    along(0, j, j).start()

                @pl.when(z == 0)
                def _():
                    along(1, NZ - 1 - j, NZ - 2 - j).start()

            def sum_step(j):
                for flow, dest in ((0, j), (1, NZ - 1 - j)):
                    slot = dest if flow == 0 else dest - 1
                    if 0 <= slot < NZ - 1:
                        passes = middle(0, flow, 0, dest)

                        @pl.when(jnp.logical_or(passes, z == dest))
                        def _():
                            along(flow, dest, slot).wait_recv()
                            a[share(c, dest), :] = add_low(a[share(c, dest), :], ar_z[flow, slot])

                        @pl.when(passes)
                        def _():
                            along(flow, dest, slot).start()

            for j in range(NZ):
                sum_step(j)
                if j == 1:
                    for kind in (0, 1):
                        turn(kind, 1)

            halves = (slice(0, 208), slice(208, SHARE))

            def cross(stage_no, half, src):
                dest = (ar_xy1, ar_xy2)[stage_no].at[halves[half]]
                way = half if stage_no == 0 else 1 - half
                return remote(
                    src, dest, ax_send.at[stage_no, half], ax_recv.at[stage_no, half], (flips[way] * 2 + c, z)
                )

            def mine(half):
                start_row = 0 if half == 0 else 208
                size = 208 if half == 0 else SHARE - 208
                return pl.ds(pl.multiple_of((c * NZ + z) * SHARE + start_row, 16), size)

            for half in (0, 1):
                cross(0, half, a.at[mine(half)]).start()
            for kind in (0, 1):
                turn(kind, 2)
            for half in (0, 1):
                cross(0, half, a.at[mine(half)]).wait_recv()
                ar_t[halves[half], :] = add_low(a[mine(half), :], ar_xy1[halves[half], :])
                cross(1, half, ar_t.at[halves[half]]).start()
            for kind in (0, 1):
                send1(kind, LOCAL - 1)
            for half in (0, 1):
                cross(1, half, ar_t.at[halves[half]]).wait()
                ar_t[halves[half], :] = add_low(ar_t[halves[half], :], ar_xy2[halves[half], :])
                cross(0, half, a.at[mine(half)]).wait_send()
            for zz in range(NZ):
                to_core(zz).wait_send()
                for flow in (0, 1):
                    slot = zz if flow == 0 else zz - 1
                    if 0 <= slot < NZ - 1:
                        goes = (z > zz) if flow == 0 else (z < zz)

                        @pl.when(goes)
                        def _():
                            along(flow, zz, slot).wait_send()

        pl.run_scoped(shared, V((TOTAL, D), BF16))

    pl.run_scoped(
        attention_grads,
        V((MB, T, 3 * D), BF16), V((MB, T, D), BF16), V((MB, T, D), BF16), V((MB, T, D), BF16), V((EXTRA, D), F32),
    )

    def place(zz):
        return ar_o.at[pl.ds(pl.multiple_of((c * NZ + zz) * SHARE, 16), SHARE)]

    own_share = pltpu.make_async_copy(ar_t, place(z), l_sem.at[6])
    own_share.start()

    def spread(up, h):
        source = z - h if up else z + h
        index = (0 if up else 1, h)
        return remote(
            ar_t if h == 0 else place(source), place(source), zz_send.at[index], zz_recv.at[index],
            (dp, z + 1 if up else z - 1),
        )

    def leaves(up, h):
        return jnp.logical_and(z - h >= 0, z + 1 < NZ) if up else jnp.logical_and(z + h < NZ, z >= 1)

    def to_partner(src, k, zz):
        return remote(src, place(zz), cc_send.at[k], cc_recv.at[k], partner)

    for up in (True, False):
        @pl.when(leaves(up, 0))
        def _():
            spread(up, 0).start()

    to_partner(ar_t, 0, z).start()
    for mb in range(MB):
        def image_out(base):
            fetch = pltpu.make_async_copy(resid.at[mb], base, l_sem.at[5])
            fetch.start()
            load_item(1 + mb)
            fetch.wait()
            block_o[mb] = (base[...] + quad_sum()).astype(BF16)

        pl.run_scoped(image_out, V((T, D), F32))
    for h in range(NZ - 1):
        for up in (True, False):
            source = z - h - 1 if up else z + h + 1

            @pl.when((z - h - 1 >= 0) if up else (z + h + 1 < NZ))
            def _():
                index = (0 if up else 1, h)
                remote(
                    place(source), place(source), zz_send.at[index], zz_recv.at[index],
                    (dp, z - 1 if up else z + 1),
                ).wait_recv()
                k = lax.rem(source - z + NZ, NZ)
                to_partner(place(source), k, source).start()

            if h + 1 < NZ - 1:
                @pl.when(leaves(up, h + 1))
                def _():
                    spread(up, h + 1).start()
    for kind in (0, 1):
        turn(kind, 3)
    for kind in (0, 1):
        for e in range(LOCAL):
            finish(kind, e)
    own_share.wait()
    for k in range(NZ):
        zz = lax.rem(z + k, NZ)
        src = ar_t if k == 0 else place(zz)
        to_partner(src, k, zz).wait_send()
        other = ar_o.at[pl.ds(pl.multiple_of(((1 - c) * NZ + zz) * SHARE, 16), SHARE)]
        remote(other, other, cc_send.at[k], cc_recv.at[k], partner).wait_recv()
    for h in range(NZ - 1):
        for up in (True, False):
            @pl.when(leaves(up, h))
            def _():
                spread(up, h).wait_send()
    for item in range(3):
        for d in range(1, NZ):
            home(item, d).wait_send()
    for kind in (0, 1):
        for e in range(LOCAL):
            for slot in (0, 1):
                hop1(kind, e, slot).wait_send()
            hop2(kind, e).wait_send()
            result(kind, e).wait()


def grads_call(*operands):
    vm = pl.BlockSpec(memory_space=pltpu.VMEM)
    hb = pl.BlockSpec(memory_space=pl.ANY)
    S = jax.ShapeDtypeStruct
    V = pltpu.VMEM
    DMA = pltpu.SemaphoreType.DMA
    outs = [
        (S((MB, T, D), BF16), vm),
        (S((MB, T, D), F32), hb),
        (S((TOTAL, D), BF16), hb),
        (S((LOCAL, BAND, HIDDEN), BF16), hb),
        (S((LOCAL, PART, D), BF16), hb),
        (S((3, NZ, T, D), BF16), hb),
    ]
    return pl.pallas_call(
        grads_kernel,
        out_shape=[o[0] for o in outs],
        in_specs=[vm] * 6 + [hb] * 15,
        out_specs=[o[1] for o in outs],
        scratch_shapes=[
            V((LOCAL, 4, PART, D), BF16), V((LOCAL, 4, BAND, HIDDEN), BF16),
            V((LOCAL, 2, PART, D), BF16), V((LOCAL, 2, BAND, HIDDEN), BF16),
            V((LOCAL, PART, D), BF16), V((LOCAL, BAND, HIDDEN), BF16),
            V((NZ, SHARE, D), BF16), V((2, NZ - 1, SHARE, D), BF16),
            V((SHARE, D), BF16), V((SHARE, D), BF16), V((SHARE, D), BF16),
            V((NZ, MB, 8, T), F32), V((NZ, T, D), BF16),
            DMA((2, LOCAL)), DMA((2, LOCAL)), DMA((2, LOCAL, 2)), DMA((2, LOCAL, 2)), DMA((2, LOCAL)), DMA((2, LOCAL)),
            DMA((3, NZ - 1)), DMA((3, NZ - 1)), DMA((NZ - 1,)), DMA((NZ - 1,)),
            DMA((NZ,)), DMA((NZ,)), DMA((2, NZ - 1)), DMA((2, NZ - 1)), DMA((2, 2)), DMA((2, 2)),
            DMA((2, NZ - 1)), DMA((2, NZ - 1)), DMA((NZ,)), DMA((NZ,)),
            DMA((8,)), DMA((13,)), DMA((2, LOCAL)),
        ],
        compiler_params=pltpu.CompilerParams(
            collective_id=2, has_side_effects=True, vmem_limit_bytes=60 << 20
        ),
        name="grads",
    )(*operands)

def fast_body(
    tokens, routes, gain_one, shift_one, w_qkv, qv_bias, w_out, out_bias, gain_two, shift_two,
    w_route, w_in, b_in, w_back, b_back, d_out,
):
    def windows(a):
        return jnp.pad(a.reshape(MB, SEQ, a.shape[1]), ((0, 0), (0, T - SEQ), (0, 0)))

    tok, dout = windows(tokens), windows(d_out)
    rt = jnp.pad(
        jnp.transpose(routes.reshape(MB, SEQ, TOP), (0, 2, 1)),
        ((0, 0), (0, 8 - TOP), (0, T - SEQ)), constant_values=-1,
    )
    vec = jnp.stack(
        [gain_one, shift_one, gain_two, shift_two, out_bias, qv_bias[0], qv_bias[1], jnp.zeros_like(out_bias)]
    )
    wrt = jnp.pad(w_route.T.reshape(NZ, LOCAL, D), ((0, 0), (0, 8 - LOCAL), (0, 0))).reshape(32, D)
    (qkv, mixed, resid, rp, gg, bb, bi, xr, gp, act, gh, pb, pg, pg0) = dispatch_call(
        tok, rt, vec, w_qkv, w_out, wrt, b_in, b_back, dout, w_in, w_back
    )
    block, ig, ar, wi, wb, _ = grads_call(
        vec, rt, wrt, bb, bi, rp, tok, dout, w_qkv, w_out, qkv, mixed, resid, gg, xr, gp, act, gh, pb, pg, pg0
    )
    dp, z = lax.axis_index("dp"), lax.axis_index("expert")
    rows = MB * SEQ
    ext = ar[4 * D :].astype(F32)
    qkv_grad = jnp.concatenate([ar[i * D : (i + 1) * D] for i in range(3)], axis=1).astype(F32)
    biases = lax.dynamic_slice(ext, (24 + 5 * LOCAL * z, 0), (5 * LOCAL, D))
    bb_grad = lax.dynamic_slice(biases[:LOCAL], (0, dp * BAND), (LOCAL, BAND))
    bi_grad = jnp.transpose(biases[LOCAL:].reshape(4, LOCAL, D), (1, 0, 2)).reshape(LOCAL, HIDDEN)
    bi_grad = lax.dynamic_slice(bi_grad, (0, dp * PART), (LOCAL, PART))
    return (
        block[:, :SEQ].reshape(rows, D),
        ig[:, :SEQ].reshape(rows, D),
        ext[0],
        ext[1],
        qkv_grad,
        ext[2:4],
        ar[3 * D : 4 * D].astype(F32),
        ext[4],
        ext[5],
        ext[6],
        ext[8 : 8 + NZ * LOCAL].T,
        wi.astype(F32),
        bi_grad,
        wb.astype(F32),
        bb_grad,
    )


def solution(mesh):
    fast = mesh.shape["dp"] == 8 and mesh.shape["expert"] == NZ
    return jax.shard_map(
        fast_body if fast else general_body,
        mesh=mesh,
        in_specs=(
            P(("dp", "expert"), None),
            P(("dp", "expert"), None),
            P(),
            P(),
            P(),
            P(),
            P(),
            P(),
            P(),
            P(),
            P(),
            P("expert", None, None),
            P("expert", None),
            P("expert", None, None),
            P("expert", None),
            P(("dp", "expert"), None),
        ),
        out_specs=(
            P(("dp", "expert"), None),
            P(("dp", "expert"), None),
            P(),
            P(),
            P(),
            P(),
            P(),
            P(),
            P(),
            P(),
            P(),
            P("expert", "dp", None),
            P("expert", "dp"),
            P("expert", "dp", None),
            P("expert", "dp"),
        ),
        check_vma=False,
    )
```

```python
import functools

import jax
import jax.numpy as jnp
from jax import lax
from jax.experimental import pallas as pl
from jax.experimental.pallas import tpu as pltpu
from jax.sharding import PartitionSpec as P

HEADS = 12
HEAD_DIM = 64
SEQ = 197
TOP = 2
MB = 2
ROWS_MB = 197
D = 768


HIGH = lax.Precision.HIGHEST
EPSILON = 1e-06


def layer_norm(value, gain, shift):
    center = value - jnp.mean(value, axis=-1, keepdims=True)
    spread = jnp.mean(center * center, axis=-1, keepdims=True)
    return center * lax.rsqrt(spread + EPSILON) * gain + shift


def route_soft(logits):
    return jax.nn.softmax(logits, axis=-1)


def general_body(
    tokens,
    routes,
    gain_one,
    shift_one,
    w_qkv,
    qv_bias,
    w_out,
    out_bias,
    gain_two,
    shift_two,
    w_route,
    w_in,
    b_in,
    w_back,
    b_back,
    d_out,
):
    groups = lax.axis_size("expert")
    local = w_in.shape[0]
    experts = groups * local
    width = tokens.shape[1]
    rows = ROWS_MB
    cap = 5 * rows * TOP // (3 * experts)
    images = rows // SEQ
    scale = HEAD_DIM ** (-0.5)
    expert_ids = jnp.arange(experts, dtype=jnp.int32)
    w_route_wide = w_route.astype(jnp.float32)
    acc_gain_one = jnp.zeros_like(gain_one)
    acc_shift_one = jnp.zeros_like(shift_one)
    acc_qkv = jnp.zeros(w_qkv.shape, jnp.float32)
    acc_qv = jnp.zeros_like(qv_bias)
    acc_out = jnp.zeros(w_out.shape, jnp.float32)
    acc_out_bias = jnp.zeros_like(out_bias)
    acc_gain_two = jnp.zeros_like(gain_two)
    acc_shift_two = jnp.zeros_like(shift_two)
    acc_route = jnp.zeros(w_route.shape, jnp.float32)
    acc_expert = None
    outputs = []
    input_grads = []
    for part in range(MB):
        x = tokens[part * rows : (part + 1) * rows].astype(jnp.float32)
        route = routes[part * rows : (part + 1) * rows]
        cotan = d_out[part * rows : (part + 1) * rows].astype(jnp.float32)
        normed, ln_one_pull = jax.vjp(layer_norm, x, gain_one, shift_one)
        normed_low = normed.astype(jnp.bfloat16)
        bias = jnp.concatenate([qv_bias[0], jnp.zeros_like(qv_bias[0]), qv_bias[1]])
        qkv = (jnp.dot(normed_low, w_qkv, preferred_element_type=jnp.float32) + bias).astype(
            jnp.bfloat16
        )
        query = qkv[:, :width].reshape(images, SEQ, HEADS, HEAD_DIM)
        keys = qkv[:, width : 2 * width].reshape(images, SEQ, HEADS, HEAD_DIM)
        values = qkv[:, 2 * width :].reshape(images, SEQ, HEADS, HEAD_DIM)
        scores = (
            jnp.einsum("ishd,ithd->ihst", query, keys, preferred_element_type=jnp.float32) * scale
        )
        log_total = jax.nn.logsumexp(scores, axis=-1, keepdims=True)
        probs_low = jnp.exp(scores - log_total).astype(jnp.bfloat16)
        mixed = jnp.einsum("ihst,ithd->ishd", probs_low, values, preferred_element_type=jnp.float32)
        mixed = mixed.reshape(rows, width).astype(jnp.bfloat16)
        resid = x + jnp.dot(mixed, w_out, preferred_element_type=jnp.float32) + out_bias
        inner, ln_two_pull = jax.vjp(layer_norm, resid, gain_two, shift_two)
        inner_low = inner.astype(jnp.bfloat16)
        logits = jnp.dot(inner_low, w_route, preferred_element_type=jnp.float32)
        route_probs, soft_pull = jax.vjp(route_soft, logits)
        choose = (route[:, :, None] == expert_ids[None, None, :]).astype(jnp.float32)
        gates = jnp.einsum("rke,re->rk", choose, route_probs, precision=HIGH)
        flat_ids = route.reshape(-1)
        table = (flat_ids[:, None] == expert_ids[None, :]).astype(jnp.int32)
        order = jnp.arange(rows * TOP, dtype=jnp.int32)
        earlier = (order[None, :] < order[:, None]).astype(jnp.bfloat16)
        before = jnp.dot(
            earlier, table.astype(jnp.bfloat16), preferred_element_type=jnp.float32
        ).astype(jnp.int32)
        slot = jnp.sum(before * table, axis=1)
        dest = flat_ids * cap + slot
        sending = (
            jnp.zeros((experts * cap, width), jnp.bfloat16)
            .at[dest]
            .set(jnp.repeat(inner_low, TOP, axis=0))
        )
        sending = sending.reshape(groups, local, cap, width)
        received = lax.all_to_all(sending, "expert", split_axis=0, concat_axis=0, tiled=True)
        hidden = jnp.einsum("secd,edf->secf", received, w_in, preferred_element_type=jnp.float32)
        hidden = hidden + b_in[None, :, None, :]
        active = jax.nn.gelu(hidden).astype(jnp.bfloat16)
        result = jnp.einsum("secf,efd->secd", active, w_back, preferred_element_type=jnp.float32)
        result = (result + b_back[None, :, None, :]).astype(jnp.bfloat16)
        returned = lax.all_to_all(result, "expert", split_axis=0, concat_axis=0, tiled=True)
        returned, kept_rows, kept_hidden = (returned, received, hidden)
        picked = (
            returned.reshape(experts * cap, width)[dest]
            .reshape(rows, TOP, width)
            .astype(jnp.float32)
        )
        block = resid + jnp.sum(gates[:, :, None] * picked, axis=1)
        outputs.append(block.astype(jnp.bfloat16))
        grad_gate = jnp.sum(picked * cotan[:, None, :], axis=2)
        grad_picked = (gates[:, :, None] * cotan[:, None, :]).astype(jnp.bfloat16)
        grad_send = (
            jnp.zeros((experts * cap, width), jnp.bfloat16)
            .at[dest]
            .set(grad_picked.reshape(rows * TOP, width))
        )
        grad_send = grad_send.reshape(groups, local, cap, width)
        grad_recv = lax.all_to_all(grad_send, "expert", split_axis=0, concat_axis=0, tiled=True)
        active, gelu_pull = jax.vjp(jax.nn.gelu, kept_hidden)
        active_low = active.astype(jnp.bfloat16)
        grad_active = jnp.einsum(
            "secd,efd->secf", grad_recv, w_back, preferred_element_type=jnp.float32
        )
        grad_hidden = gelu_pull(grad_active)[0].astype(jnp.bfloat16)
        step_w_back = jnp.einsum(
            "secf,secd->efd", active_low, grad_recv, preferred_element_type=jnp.float32
        )
        step_b_back = jnp.sum(grad_recv.astype(jnp.float32), axis=(0, 2))
        step_w_in = jnp.einsum(
            "secd,secf->edf", kept_rows, grad_hidden, preferred_element_type=jnp.float32
        )
        step_b_in = jnp.sum(grad_hidden.astype(jnp.float32), axis=(0, 2))
        grad_rows = jnp.einsum(
            "secf,edf->secd", grad_hidden, w_in, preferred_element_type=jnp.float32
        )
        grad_rows = grad_rows.astype(jnp.bfloat16)
        grad_back = lax.all_to_all(grad_rows, "expert", split_axis=0, concat_axis=0, tiled=True)
        shares = (step_w_in, step_b_in, step_w_back, step_b_back)
        if acc_expert is None:
            acc_expert = shares
        else:
            acc_expert = tuple((a + b for a, b in zip(acc_expert, shares)))
        grad_inner = jnp.sum(
            grad_back.reshape(experts * cap, width)[dest]
            .reshape(rows, TOP, width)
            .astype(jnp.float32),
            axis=1,
        )
        grad_probs = jnp.einsum("rk,rke->re", grad_gate, choose, precision=HIGH)
        grad_logits = soft_pull(grad_probs)[0]
        acc_route = acc_route + jnp.einsum(
            "rd,re->de", inner_low.astype(jnp.float32), grad_logits, precision=HIGH
        )
        grad_inner = grad_inner + jnp.einsum("re,de->rd", grad_logits, w_route_wide, precision=HIGH)
        grad_ln_two, grad_gain_two, grad_shift_two = ln_two_pull(grad_inner)
        acc_gain_two = acc_gain_two + grad_gain_two
        acc_shift_two = acc_shift_two + grad_shift_two
        grad_resid = cotan + grad_ln_two
        grad_att = grad_resid.astype(jnp.bfloat16)
        acc_out = acc_out + jnp.einsum(
            "rd,re->de", mixed, grad_att, preferred_element_type=jnp.float32
        )
        acc_out_bias = acc_out_bias + jnp.sum(grad_att.astype(jnp.float32), axis=0)
        grad_mixed = jnp.einsum("re,de->rd", grad_att, w_out, preferred_element_type=jnp.float32)
        grad_mixed = grad_mixed.astype(jnp.bfloat16).reshape(images, SEQ, HEADS, HEAD_DIM)
        again = (
            jnp.einsum("ishd,ithd->ihst", query, keys, preferred_element_type=jnp.float32) * scale
        )
        probs = jnp.exp(again - log_total)
        grad_probs_att = jnp.einsum(
            "ishd,ithd->ihst", grad_mixed, values, preferred_element_type=jnp.float32
        )
        row_total = jnp.sum(probs * grad_probs_att, axis=-1, keepdims=True)
        grad_scores = (probs * (grad_probs_att - row_total)).astype(jnp.bfloat16)
        grad_query = (
            jnp.einsum("ihst,ithd->ishd", grad_scores, keys, preferred_element_type=jnp.float32)
            * scale
        )
        grad_keys = (
            jnp.einsum("ihst,ishd->ithd", grad_scores, query, preferred_element_type=jnp.float32)
            * scale
        )
        grad_values = jnp.einsum(
            "ihst,ishd->ithd",
            probs.astype(jnp.bfloat16),
            grad_mixed,
            preferred_element_type=jnp.float32,
        )
        grad_qkv = jnp.concatenate(
            [
                grad_query.reshape(rows, width),
                grad_keys.reshape(rows, width),
                grad_values.reshape(rows, width),
            ],
            axis=1,
        ).astype(jnp.bfloat16)
        acc_qkv = acc_qkv + jnp.einsum(
            "rd,re->de", normed_low, grad_qkv, preferred_element_type=jnp.float32
        )
        column_sums = jnp.sum(grad_qkv.astype(jnp.float32), axis=0)
        acc_qv = acc_qv + jnp.stack([column_sums[:width], column_sums[2 * width :]])
        grad_normed = jnp.einsum("re,de->rd", grad_qkv, w_qkv, preferred_element_type=jnp.float32)
        grad_ln_one, grad_gain_one, grad_shift_one = ln_one_pull(grad_normed)
        acc_gain_one = acc_gain_one + grad_gain_one
        acc_shift_one = acc_shift_one + grad_shift_one
        input_grads.append(grad_resid + grad_ln_one)
    expert_grads = (
        lax.psum_scatter(
            acc_expert[0].astype(jnp.bfloat16), "dp", scatter_dimension=1, tiled=True
        ).astype(jnp.float32),
        lax.psum_scatter(
            acc_expert[1].astype(jnp.bfloat16), "dp", scatter_dimension=1, tiled=True
        ).astype(jnp.float32),
        lax.psum_scatter(
            acc_expert[2].astype(jnp.bfloat16), "dp", scatter_dimension=1, tiled=True
        ).astype(jnp.float32),
        lax.psum_scatter(
            acc_expert[3].astype(jnp.bfloat16), "dp", scatter_dimension=1, tiled=True
        ).astype(jnp.float32),
    )
    shared = (
        acc_gain_one,
        acc_shift_one,
        acc_qkv,
        acc_qv,
        acc_out,
        acc_out_bias,
        acc_gain_two,
        acc_shift_two,
        acc_route,
    )
    shared = lax.psum(
        (
            shared[0],
            shared[1],
            shared[2],
            shared[3],
            shared[4],
            shared[5],
            shared[6],
            shared[7],
            shared[8],
        ),
        ("dp", "expert"),
    )
    return (
        jnp.concatenate(outputs, axis=0),
        jnp.concatenate(input_grads, axis=0),
        shared[0],
        shared[1],
        shared[2],
        shared[3],
        shared[4],
        shared[5],
        shared[6],
        shared[7],
        shared[8],
        expert_grads[0],
        expert_grads[1],
        expert_grads[2],
        expert_grads[3],
    )


F32, BF16 = jnp.float32, jnp.bfloat16
NZ = 4
LOCAL = 4
PAIRS = HEADS // 2
T = 208
KEYS = 256
CAP_ROWS = 48
ROWS = NZ * CAP_ROWS
CHUNK = 768
MESH = pl.DeviceIdType.MESH
NT = (((1,), (1,)), ((), ()))
TN = (((0,), (0,)), ((), ()))


def dot(a, b, dims=(((1,), (0,)), ((), ()))):
    return lax.dot_general(a, b, dims, preferred_element_type=F32)


def normal(value):
    center = value - jnp.mean(value, axis=-1, keepdims=True)
    scale = lax.rsqrt(jnp.mean(center * center, axis=-1, keepdims=True) + EPSILON)
    return center * scale, scale


def half_mask(which):
    lane = lax.broadcasted_iota(jnp.int32, (1, 128), 1)
    return ((lane < 64) if which == 0 else (lane >= 64)).astype(F32).astype(BF16)


def attention_probs(scores):
    key = lax.broadcasted_iota(jnp.int32, scores.shape, 1)
    scores = jnp.where(key < SEQ, scores, -1e30)
    top = jnp.max(scores, axis=-1, keepdims=True)
    raised = jnp.exp(scores - top)
    return raised / jnp.sum(raised, axis=-1, keepdims=True)


def route_table(rt_ref, mb):
    row = lax.broadcasted_iota(jnp.int32, (32, T), 0)
    part = lax.rem(row, 8)
    expert = jnp.where(part < LOCAL, (row // 8) * LOCAL + part, -7)
    first = rt_ref[mb, 0:1, :]
    second = rt_ref[mb, 1:2, :]
    return jnp.logical_or(expert == first, expert == second), part < LOCAL


def route_softmax(logits, real):
    logits = jnp.where(real, logits, -1e30)
    raised = jnp.exp(logits - jnp.max(logits, axis=0, keepdims=True))
    raised = jnp.where(real, raised, 0.0)
    return raised / jnp.sum(raised, axis=0, keepdims=True)


def pick_matrix(slots):
    index = lax.broadcasted_iota(jnp.int32, (CAP_ROWS, T), 0).astype(F32)
    return jnp.concatenate(
        [(index == slots[e : e + 1, :]).astype(F32) for e in range(LOCAL)], axis=0
    )


def dispatch_kernel(
    tok, rt, vec, wqkv, wout, wrt, b_in, b_back, dout, w_in, w_back,
    qkv_o, mixed_o, resid_o, rp_o, gg_o, bb_o, bi_o, x_o, gp_o, act_o, gh_o, pb_o, pg_o, home_o,
    gi, gd, sg, qkv_s, mixed_s, inner_s, xs, gs, cs, rgs, ggs, wb1, wb2, act_st, gh_st, acc_o, acc_g,
    os_, grs, pb_s, pg_s,
    send_sem, recv_sem, d_sem, w_sem, st_sem, x_sem, p_sem, h_send, h_recv,
):
    dp = lax.axis_index("dp")
    z = lax.axis_index("expert")

    def item_ref(kind, source, mb):
        return (gd, sg, gi)[kind].at[source, mb]

    def hop(up, kind, mb, h):
        source = z - h if up else z + h
        target = z + 1 if up else z - 1
        index = (0 if up else 1, kind * MB + mb, h)
        return pltpu.make_async_remote_copy(
            src_ref=item_ref(kind, source, mb),
            dst_ref=item_ref(kind, source, mb),
            send_sem=send_sem.at[index],
            recv_sem=recv_sem.at[index],
            device_id=(dp, target),
            device_id_type=MESH,
        )

    def leaves(up, h):
        return jnp.logical_and(z - h >= 0, z + 1 < NZ) if up else jnp.logical_and(z + h < NZ, z >= 1)

    def arrives(up, h):
        return (z - h - 1 >= 0) if up else (z + h + 1 < NZ)

    def start(kind, mb, h):
        for up in (True, False):
            @pl.when(leaves(up, h))
            def _():
                hop(up, kind, mb, h).start()

    def pass_on(kind, mb, h):
        for up in (True, False):
            @pl.when(arrives(up, h))
            def _():
                source = z - h - 1 if up else z + h + 1
                index = (0 if up else 1, kind * MB + mb, h)
                ref = item_ref(kind, source, mb)
                pltpu.make_async_remote_copy(
                    src_ref=ref, dst_ref=ref, send_sem=send_sem.at[index], recv_sem=recv_sem.at[index],
                    device_id=(dp, z - 1 if up else z + 1), device_id_type=MESH,
                ).wait_recv()
            if h + 1 < NZ - 1:
                @pl.when(leaves(up, h + 1))
                def _():
                    hop(up, kind, mb, h + 1).start()

    def weights(n, slot):
        e = lax.rem(n, 16) // 4
        f = lax.rem(n, 4)
        cols = pl.ds(pl.multiple_of(f * CHUNK, CHUNK), CHUNK)
        return (
            pltpu.make_async_copy(w_in.at[e, :, cols], wb1.at[slot], w_sem.at[0, slot]),
            pltpu.make_async_copy(w_back.at[e, cols, :], wb2.at[slot], w_sem.at[1, slot]),
        )

    own = [pltpu.make_async_copy(dout.at[mb], gd.at[z, mb], d_sem.at[mb]) for mb in range(MB)]
    for copy in own:
        copy.start()
    barrier = pltpu.get_barrier_semaphore()
    for d in range(1, NZ):
        pl.semaphore_signal(barrier, inc=1, device_id=(dp, lax.rem(z + d, NZ)), device_id_type=MESH)
    pl.semaphore_wait(barrier, NZ - 1)
    for copy in own:
        copy.wait()
    start(0, 0, 0)
    for copy in weights(0, 0):
        copy.start()

    qkv_s[T:KEYS, :] = jnp.zeros((KEYS - T, 3 * D), BF16)
    bb_o[...] = jnp.zeros_like(bb_o)
    bi_o[...] = jnp.zeros_like(bi_o)

    def forward(mb, carry):
        x = tok[mb].astype(F32)
        normed = (normal(x)[0] * vec[0:1] + vec[1:2]).astype(BF16)
        for c in range(3):
            cols = slice(c * D, (c + 1) * D)
            part = dot(normed, wqkv[:, cols])
            if c != 1:
                row = 5 if c == 0 else 6
                part = part + vec[row : row + 1]
            qkv_s[0:T, cols] = part.astype(BF16)

        def heads(p, carry):
            at = [pl.ds(pl.multiple_of(c * D + p * 128, 128), 128) for c in range(3)]
            q, k, v = qkv_s[0:T, at[0]], qkv_s[:, at[1]], qkv_s[:, at[2]]
            mixed = jnp.zeros((T, 128), F32)
            for which in (0, 1):
                mask = half_mask(which)
                probs = attention_probs(dot(q, k * mask, NT) * HEAD_DIM ** (-0.5))
                mixed = mixed + dot(probs.astype(BF16), v * mask)
            mixed_s[:, at[0]] = mixed.astype(BF16)
            return carry

        lax.fori_loop(0, PAIRS, heads, 0)
        qkv_o[mb] = qkv_s[0:T, :]
        mixed_o[mb] = mixed_s[...]
        resid = x + dot(mixed_s[...], wout[...]) + vec[4:5]
        resid_o[mb] = resid
        inner = (normal(resid)[0] * vec[2:3] + vec[3:4]).astype(BF16)
        gi[z, mb] = inner
        table, real = route_table(rt, mb)
        probs = route_softmax(dot(wrt[...], inner, NT), real)
        rp_o[mb] = probs
        earlier = (
            lax.broadcasted_iota(jnp.int32, (T, T), 0) < lax.broadcasted_iota(jnp.int32, (T, T), 1)
        ).astype(F32).astype(BF16)
        before = dot(table.astype(F32).astype(BF16), earlier)
        slots = jnp.where(table, before, -1.0)
        gates = jnp.where(table, probs, 0.0)
        for p in range(NZ):
            sg[z, mb, 0, p] = slots[8 * p : 8 * p + 8, :]
            sg[z, mb, 1, p] = gates[8 * p : 8 * p + 8, :]

        @pl.when(mb == 0)
        def _():
            start(1, 0, 0)
            start(2, 0, 0)

        return carry

    lax.fori_loop(0, MB, forward, 0)
    for h in range(NZ - 1):
        for kind in range(3):
            pass_on(kind, 0, h)
    for kind in range(3):
        start(kind, 1, 0)

    def micro(mb, carry):
        @pl.when(mb == 1)
        def _():
            for kind in range(3):
                pass_on(kind, 1, 2)

        def spread(src, carry):
            pick = pick_matrix(sg[src, mb, 0, z])
            gate = sg[src, mb, 1, z]
            low = pick.astype(BF16)
            rows_x = dot(low, gi[src, mb]).astype(BF16)
            rows_c = dot(low, gd[src, mb])
            at = pl.ds(pl.multiple_of(mb * ROWS + src * CAP_ROWS, 16), CAP_ROWS)
            here = pl.ds(pl.multiple_of(src * CAP_ROWS, 16), CAP_ROWS)
            for e in range(LOCAL):
                part = slice(e * CAP_ROWS, (e + 1) * CAP_ROWS)
                gate_rows = jnp.sum(pick[part] * gate[e : e + 1, :], axis=1, keepdims=True)
                grad = (rows_c[part] * gate_rows).astype(BF16)
                xs[e, at, :] = rows_x[part]
                gs[e, at, :] = grad
                cs[e, here, :] = rows_c[part].astype(BF16)
                rgs[e, here, :] = jnp.broadcast_to(gate_rows, (CAP_ROWS, 128))
                bb_o[e : e + 1, :] += jnp.sum(grad.astype(F32), axis=0, keepdims=True)
            return carry

        lax.fori_loop(0, NZ, spread, 0)
        rows = pl.ds(pl.multiple_of(mb * ROWS, 16), ROWS)

        def expert(e, carry):
            acc_o[...] = jnp.zeros_like(acc_o)
            acc_g[...] = jnp.zeros_like(acc_g)

            def step(f, carry):
                n = mb * 16 + e * 4 + f
                slot = lax.rem(n, 2)
                cols = pl.ds(pl.multiple_of(f * CHUNK, CHUNK), CHUNK)

                @pl.when(n + 1 < 16 * MB)
                def _():
                    for copy in weights(n + 1, 1 - slot):
                        copy.start()

                @pl.when(n >= 2)
                def _():
                    for copy in stores(n - 2, slot):
                        copy.wait()

                for copy in weights(n, slot):
                    copy.wait()
                hid = dot(xs[e, rows, :], wb1[slot]) + b_in[pl.ds(e, 1), cols]
                square = hid * hid
                bend = jnp.tanh(hid * (0.7978845608 + (0.7978845608 * 0.044715) * square))
                half = 0.5 + 0.5 * bend
                act = (hid * half).astype(BF16)
                slope = half + (0.5 * hid) * (1.0 - bend * bend) * (
                    0.7978845608 + (3 * 0.7978845608 * 0.044715) * square
                )

                act_st[slot] = act
                acc_o[...] += dot(act, wb2[slot])
                grad = (dot(gs[e, rows, :], wb2[slot], NT) * slope).astype(BF16)
                gh_st[slot] = grad
                acc_g[...] += dot(grad, wb1[slot], NT)
                bi_o[pl.ds(e, 1), cols] += jnp.sum(grad.astype(F32), axis=0, keepdims=True)
                for copy in stores(n, slot):
                    copy.start()
                return carry

            lax.fori_loop(0, 4, step, 0)
            out = (acc_o[...] + b_back[pl.ds(e, 1), :]).astype(BF16).astype(F32)
            gg = jnp.sum(out * cs[e].astype(F32), axis=1, keepdims=True)
            scaled = (out * rgs[e][:, 0:1]).astype(BF16)
            back = acc_g[...].astype(BF16)
            at = pl.ds(pl.multiple_of(e * CAP_ROWS, 16), CAP_ROWS)
            for src in range(NZ):
                part = slice(src * CAP_ROWS, (src + 1) * CAP_ROWS)
                os_[src, at, :] = scaled[part]
                grs[src, at, :] = back[part]
                ggs[src, at, :] = jnp.broadcast_to(gg[part], (CAP_ROWS, 128))

            @pl.when(jnp.logical_and(mb == 1, e == 0))
            def _():
                for d in range(1, NZ):
                    sent_home(d).start()
                own_home().start()

            @pl.when(jnp.logical_and(mb == 0, e == 1))
            def _():
                for kind in range(3):
                    pass_on(kind, 1, 0)

            @pl.when(jnp.logical_and(mb == 0, e == 3))
            def _():
                for kind in range(3):
                    pass_on(kind, 1, 1)

            return carry

        def stores(n, slot):
            m = n // 16
            e = lax.rem(n, 16) // 4
            f = lax.rem(n, 4)
            at = (e, pl.ds(pl.multiple_of(m * ROWS, 16), ROWS), pl.ds(pl.multiple_of(f * CHUNK, CHUNK), CHUNK))
            return (
                pltpu.make_async_copy(act_st.at[slot], act_o.at[at], st_sem.at[0, slot]),
                pltpu.make_async_copy(gh_st.at[slot], gh_o.at[at], st_sem.at[1, slot]),
            )

        lax.fori_loop(0, LOCAL, expert, 0)

        @pl.when(mb == 1)
        def _():
            for slot in (0, 1):
                for copy in stores(16 * MB - 2 + slot, slot):
                    copy.wait()

        @pl.when(mb == 1)
        def _():
            for src in range(NZ):
                kept(0, src).wait()
            for d in range(1, NZ):
                sent_home(d).wait_send()
            own_home().wait()

        def gather(src, carry):
            pick = pick_matrix(sg[src, mb, 0, z])
            low = pick.astype(BF16)
            pb_s[src] = dot(low, os_[src], TN).astype(BF16)
            pg_s[src] = dot(low, grs[src], TN).astype(BF16)
            kept(mb, src).start()
            for e in range(LOCAL):
                part = slice(e * CAP_ROWS, (e + 1) * CAP_ROWS)
                gg_o[src, mb, e : e + 1, :] = jnp.sum(
                    pick[part] * ggs[src, part, 0:1], axis=0, keepdims=True
                )

            @pl.when(mb == 1)
            def _():
                kept_grad(src).start()

            return carry

        lax.fori_loop(0, NZ, gather, 0)

        @pl.when(mb == 1)
        def _():
            for src in range(NZ):
                kept(1, src).wait()
                kept_grad(src).wait()

        return carry

    def kept(mb, src):
        return pltpu.make_async_copy(pb_s.at[src], pb_o.at[mb, src], p_sem.at[0, src])

    def kept_grad(src):
        return pltpu.make_async_copy(pg_s.at[src], pg_o.at[src], p_sem.at[1, src])

    def sent_home(d):
        target = lax.rem(z + d, NZ)
        return pltpu.make_async_remote_copy(
            src_ref=pg_s.at[target], dst_ref=home_o.at[z], send_sem=h_send.at[d - 1], recv_sem=h_recv.at[d - 1],
            device_id=(dp, target), device_id_type=MESH,
        )

    def own_home():
        return pltpu.make_async_copy(pg_s.at[z], home_o.at[z], d_sem.at[0])

    gg_o[...] = jnp.zeros_like(gg_o)
    lax.fori_loop(0, MB, micro, 0)
    last = (
        pltpu.make_async_copy(xs, x_o, x_sem.at[0]),
        pltpu.make_async_copy(gs, gp_o, x_sem.at[1]),
    )
    for copy in last:
        copy.start()
    for copy in last:
        copy.wait()
    for d in range(1, NZ):
        source = lax.rem(z + NZ - d, NZ)
        pltpu.make_async_remote_copy(
            src_ref=home_o.at[source], dst_ref=home_o.at[source], send_sem=h_send.at[d - 1],
            recv_sem=h_recv.at[d - 1], device_id=(dp, source), device_id_type=MESH,
        ).wait_recv()
    for mb in range(MB):
        for kind in range(3):
            for h in range(NZ - 1):
                for up in (True, False):
                    @pl.when(leaves(up, h))
                    def _():
                        hop(up, kind, mb, h).wait_send()


def dispatch_call(*operands):
    vm = pl.BlockSpec(memory_space=pltpu.VMEM)
    hb = pl.BlockSpec(memory_space=pl.ANY)
    S = jax.ShapeDtypeStruct
    rows = MB * ROWS
    outs = [
        (S((MB, T, 3 * D), BF16), vm),
        (S((MB, T, D), BF16), vm),
        (S((MB, T, D), F32), vm),
        (S((MB, 32, T), F32), vm),
        (S((NZ, MB, 8, T), F32), vm),
        (S((LOCAL, D), F32), vm),
        (S((LOCAL, 4 * CHUNK), F32), vm),
        (S((LOCAL, rows, D), BF16), hb),
        (S((LOCAL, rows, D), BF16), hb),
        (S((LOCAL, rows, 4 * CHUNK), BF16), hb),
        (S((LOCAL, rows, 4 * CHUNK), BF16), hb),
        (S((MB, NZ, T, D), BF16), hb),
        (S((NZ, T, D), BF16), hb),
        (S((NZ, T, D), BF16), hb),
    ]
    V = pltpu.VMEM
    DMA = pltpu.SemaphoreType.DMA
    return pl.pallas_call(
        dispatch_kernel,
        out_shape=[o[0] for o in outs],
        in_specs=[vm] * 8 + [hb] * 3,
        out_specs=[o[1] for o in outs],
        scratch_shapes=[
            V((NZ, MB, T, D), BF16), V((NZ, MB, T, D), BF16), V((NZ, MB, 2, NZ, 8, T), F32),
            V((KEYS, 3 * D), BF16), V((T, D), BF16), V((8, 128), F32),
            V((LOCAL, rows, D), BF16), V((LOCAL, rows, D), BF16), V((LOCAL, ROWS, D), BF16),
            V((LOCAL, ROWS, 128), F32), V((NZ, ROWS, 128), F32),
            V((2, D, CHUNK), BF16), V((2, CHUNK, D), BF16),
            V((2, ROWS, CHUNK), BF16), V((2, ROWS, CHUNK), BF16),
            V((ROWS, D), F32), V((ROWS, D), F32),
            V((NZ, ROWS, D), BF16), V((NZ, ROWS, D), BF16),
            V((NZ, T, D), BF16), V((NZ, T, D), BF16),
            DMA((2, 3 * MB, NZ - 1)), DMA((2, 3 * MB, NZ - 1)), DMA((MB,)), DMA((2, 2)), DMA((2, 2)),
            DMA((2,)), DMA((2, NZ)), DMA((NZ - 1,)), DMA((NZ - 1,)),
        ],
        compiler_params=pltpu.CompilerParams(
            collective_id=1, has_side_effects=True, vmem_limit_bytes=58 << 20
        ),
        name="dispatch",
    )(*operands)


HIDDEN = 4 * CHUNK
PART = HIDDEN // 8
BAND = D // 8
SHARE = 400
EXTRA = 128
TOTAL = 8 * SHARE


def add_low(a, b):
    return (a.astype(F32) + b.astype(F32)).astype(BF16)


def grads_kernel(
    vec, rt, wrt, bb, bi, rp,
    tok, dout, wqkv, wout, qkv, mixed, resid, gg, xr, gp, act, gh, pb, pg, pg0,
    block_o, ig_o, ar_o, kb_o, ki_o, lb_o, li_o, land_o,
    core_b, core_i, st1_b, st1_i, ar_core, ar_z, ar_xy1, ar_xy2, ar_t,
    ggr,
    c_send, c_recv, s1_send, s1_recv, s2_send, s2_recv, r_send, r_recv, g_send, g_recv,
    ac_send, ac_recv, az_send, az_recv, ax_send, ax_recv, zz_send, zz_recv, cc_send, cc_recv,
    l_sem, o_sem, f_sem,
):
    dp = lax.axis_index("dp")
    z = lax.axis_index("expert")
    y, x, c = dp // 4, lax.rem(dp // 2, 2), lax.rem(dp, 2)
    yx = y * 2 + x
    partner = (yx * 2 + (1 - c), z)
    flips = ((y * 2 + (1 - x)), ((1 - y) * 2 + x))
    across = (1 - y) * 2 + (1 - x)

    def remote(src, dst, ssem, rsem, target):
        return pltpu.make_async_remote_copy(
            src_ref=src, dst_ref=dst, send_sem=ssem, recv_sem=rsem, device_id=target, device_id_type=MESH
        )

    barrier = pltpu.get_barrier_semaphore()
    for target in [partner, (flips[0] * 2 + c, z), (flips[1] * 2 + c, z)]:
        pl.semaphore_signal(barrier, inc=1, device_id=target, device_id_type=MESH)
    for d in range(1, NZ):
        pl.semaphore_signal(barrier, inc=1, device_id=(dp, lax.rem(z + d, NZ)), device_id_type=MESH)
    pl.semaphore_wait(barrier, 6)

    def gate_copy(d):
        return remote(gg.at[lax.rem(z + d, NZ)], ggr.at[z], g_send.at[d - 1], g_recv.at[d - 1], (dp, lax.rem(z + d, NZ)))

    for d in range(1, NZ):
        gate_copy(d).start()
    own_gate = pltpu.make_async_copy(gg.at[z], ggr.at[z], l_sem.at[0])
    own_gate.start()

    def home(item, d):
        target = lax.rem(z + d, NZ)
        part = pg.at[target] if item == 0 else pb.at[item - 1, target]
        return remote(
            part, land_o.at[item, z], r_send.at[item, d - 1], r_recv.at[item, d - 1], (dp, target)
        )

    def arrived(item):
        for d in range(1, NZ):
            source = lax.rem(z + NZ - d, NZ)
            ref = land_o.at[item, source]
            remote(ref, ref, r_send.at[item, d - 1], r_recv.at[item, d - 1], (dp, source)).wait_recv()

    def load(quad, sources):
        copies = [pltpu.make_async_copy(ref, quad[i], l_sem.at[1 + i]) for i, ref in enumerate(sources)]
        for copy in copies:
            copy.start()
        for copy in copies:
            copy.wait()

    def load_item(quad, item):
        arrived(item)
        own = pg.at[z] if item == 0 else pb.at[item - 1, z]
        load(quad, [own] + [land_o.at[item, lax.rem(z + d, NZ)] for d in range(1, NZ)])

    def quad_sum(quad):
        parts = [ref[...].astype(F32) for ref in quad]
        return (parts[0] + parts[1]) + (parts[2] + parts[3])

    def middle(arr, flow, mb, dest):
        return jnp.logical_and(z > dest, z < NZ - 1) if flow == 0 else jnp.logical_and(z < dest, z > 0)

    cores, lands1, lands2, keeps = (core_b, core_i), (st1_b, st1_i), (lb_o, li_o), (kb_o, ki_o)

    def core_copy(kind, e, src):
        return remote(src, cores[kind].at[e], c_send.at[kind, e], c_recv.at[kind, e], partner)

    def hop1(kind, e, slot):
        block = flips[kind] if slot == 0 else across
        return remote(
            cores[kind].at[e, block], lands1[kind].at[e, slot],
            s1_send.at[kind, e, slot], s1_recv.at[kind, e, slot], (flips[kind] * 2 + c, z),
        )

    def hop2(kind, e):
        return remote(
            cores[kind].at[e, flips[1 - kind]], lands2[kind].at[e],
            s2_send.at[kind, e], s2_recv.at[kind, e], (flips[1 - kind] * 2 + c, z),
        )

    def send1(kind, e):
        for slot in (1, 0):
            hop1(kind, e, slot).start()

    def turn(kind, e):
        ref = cores[kind]
        hop1(kind, e, 1).wait_recv()
        ref[e, flips[1 - kind]] = add_low(ref[e, flips[1 - kind]], lands1[kind][e, 1])
        hop2(kind, e).start()
        hop1(kind, e, 0).wait_recv()
        ref[e, yx] = add_low(ref[e, yx], lands1[kind][e, 0])
        keep(kind, e).start()

    def keep(kind, e):
        return pltpu.make_async_copy(cores[kind].at[e, yx], keeps[kind].at[e], f_sem.at[kind, e])

    for item in range(3):
        for d in range(1, NZ):
            home(item, d).start()

    V = pltpu.VMEM
    rows = MB * ROWS

    def attention_grads(one, gqkv_s, nor_s, gat_s, ext):
        def inside(wqkv_s, wout_s, qkv_s, tok_s, dout_s, res_s, gres, gm_s):
            loads = [
                pltpu.make_async_copy(src, dst, o_sem.at[4 + i])
                for i, (src, dst) in enumerate(
                    ((wqkv, wqkv_s), (wout, wout_s))
                )
            ]
            for copy in loads:
                copy.start()
            ext[...] = jnp.zeros_like(ext)
            qkv_s[T:KEYS, :] = jnp.zeros((KEYS - T, 3 * D), BF16)
            for d in range(1, NZ):
                gate_copy(d).wait_send()
                source = lax.rem(z + NZ - d, NZ)
                remote(ggr.at[source], ggr.at[source], g_send.at[d - 1], g_recv.at[d - 1], (dp, source)).wait_recv()
            own_gate.wait()
            for copy in loads:
                copy.wait()

            def image(mb, carry):
                quad = [gqkv_s.at[mb, :, i * D : (i + 1) * D] for i in range(3)] + [gm_s]

                @pl.when(mb == 0)
                def _():
                    load(quad, [pg0.at[p] for p in range(NZ)])

                @pl.when(mb == 1)
                def _():
                    load_item(quad, 0)

                fetches = [
                    pltpu.make_async_copy(src.at[mb], dst, o_sem.at[8 + i])
                    for i, (src, dst) in enumerate(((qkv, qkv_s.at[0:T]), (dout, dout_s), (tok, tok_s), (resid, res_s)))
                ]
                for fetch in fetches:
                    fetch.start()
                table, _ = route_table(rt, mb)
                gates = jnp.concatenate([ggr[p, mb] for p in range(NZ)], axis=0)
                g = jnp.where(table, gates, 0.0)
                probs = rp[mb]
                gl = (probs * (g - jnp.sum(probs * g, axis=0, keepdims=True))).astype(BF16)
                fetches[3].wait()
                n2, r2 = normal(res_s[...])
                inner = (n2 * vec[2:3] + vec[3:4]).astype(BF16)
                wr = dot(gl, inner)
                for p in range(NZ):
                    ext[8 + LOCAL * p : 8 + LOCAL * (p + 1), :] += wr[8 * p : 8 * p + LOCAL]
                gi = quad_sum(quad) + dot(gl, wrt[...], TN)
                ext[5:6, :] += jnp.sum(gi * n2, axis=0, keepdims=True)
                ext[6:7, :] += jnp.sum(gi, axis=0, keepdims=True)
                u = gi * vec[2:3]
                fetches[1].wait()
                grad = dout_s[...].astype(F32) + r2 * (
                    u - jnp.mean(u, -1, keepdims=True) - n2 * jnp.mean(u * n2, -1, keepdims=True)
                )

                @pl.when(mb == 1)
                def _():
                    pltpu.make_async_copy(gres, ig_o.at[0], o_sem.at[12]).wait()

                gres[...] = grad
                low = grad.astype(BF16)
                gat_s[mb] = low
                ext[4:5, :] += jnp.sum(low.astype(F32), axis=0, keepdims=True)
                gm_s[...] = dot(low, wout_s[...], NT).astype(BF16)
                fetches[0].wait()

                def heads(p, carry):
                    at = [pl.ds(pl.multiple_of(i * D + p * 128, 128), 128) for i in range(3)]
                    q, k, v = qkv_s[0:T, at[0]], qkv_s[:, at[1]], qkv_s[:, at[2]]
                    gm = gm_s[:, at[0]]
                    gq = jnp.zeros((T, 128), F32)
                    gk = jnp.zeros((KEYS, 128), F32)
                    gv = jnp.zeros((KEYS, 128), F32)
                    for which in (0, 1):
                        mask = half_mask(which)
                        km = k * mask
                        prob = attention_probs(dot(q, km, NT) * HEAD_DIM ** (-0.5))
                        gpr = dot(gm, v * mask, NT)
                        gs = (prob * (gpr - jnp.sum(prob * gpr, axis=-1, keepdims=True))).astype(BF16)
                        gq = gq + dot(gs, km)
                        gk = gk + dot(gs, q * mask, TN)
                        gv = gv + dot(prob.astype(BF16), gm * mask, TN)
                    gqkv_s[mb, :, at[0]] = (gq * HEAD_DIM ** (-0.5)).astype(BF16)
                    gqkv_s[mb, :, at[1]] = (gk[0:T] * HEAD_DIM ** (-0.5)).astype(BF16)
                    gqkv_s[mb, :, at[2]] = gv[0:T].astype(BF16)
                    return carry

                lax.fori_loop(0, PAIRS, heads, 0)
                for row, i in ((2, 0), (3, 2)):
                    ext[row : row + 1, :] += jnp.sum(
                        gqkv_s[mb, :, i * D : (i + 1) * D].astype(F32), axis=0, keepdims=True
                    )
                gn = dot(gqkv_s[mb], wqkv_s[...], NT)
                fetches[2].wait()
                n1, r1 = normal(tok_s[...].astype(F32))
                nor_s[mb] = (n1 * vec[0:1] + vec[1:2]).astype(BF16)
                ext[0:1, :] += jnp.sum(gn * n1, axis=0, keepdims=True)
                ext[1:2, :] += jnp.sum(gn, axis=0, keepdims=True)
                w = gn * vec[0:1]
                gres[...] += r1 * (
                    w - jnp.mean(w, -1, keepdims=True) - n1 * jnp.mean(w * n1, -1, keepdims=True)
                )
                pltpu.make_async_copy(gres, ig_o.at[mb], o_sem.at[12 + mb]).start()

                @pl.when(mb == 0)
                def _():
                    one(1)

                return carry

            lax.fori_loop(0, MB, image, 0)
            pltpu.make_async_copy(gres, ig_o.at[1], o_sem.at[13]).wait()

        pl.run_scoped(
            inside,
            V((D, 3 * D), BF16), V((D, D), BF16), V((KEYS, 3 * D), BF16), V((T, D), BF16), V((T, D), BF16),
            V((T, D), F32), V((T, D), F32), V((T, D), BF16),
        )

        def shared(a, mix_s):
            mix = pltpu.make_async_copy(mixed, mix_s, o_sem.at[4])
            mix.start()
            for zz in range(NZ):
                @pl.when(z == zz)
                def _():
                    at = 24 + 5 * LOCAL * zz
                    ext[at : at + LOCAL, :] = bb[...]
                    for f in range(4):
                        ext[at + LOCAL * (f + 1) : at + LOCAL * (f + 2), :] = bi[:, f * CHUNK : (f + 1) * CHUNK]
            for i in range(3):
                total = jnp.zeros((D, D), F32)
                for mb in range(MB):
                    total = total + dot(nor_s[mb], gqkv_s[mb, :, i * D : (i + 1) * D], TN)
                a[i * D : (i + 1) * D, :] = total.astype(BF16)
            mix.wait()
            total = jnp.zeros((D, D), F32)
            for mb in range(MB):
                total = total + dot(mix_s[mb], gat_s[mb], TN)
            a[3 * D : 4 * D, :] = total.astype(BF16)
            a[4 * D : TOTAL, :] = ext[...].astype(BF16)

            def share(side, zz):
                return pl.ds(pl.multiple_of((side * NZ + zz) * SHARE, 16), SHARE)

            def to_core(zz):
                return remote(a.at[share(1 - c, zz)], ar_core.at[zz], ac_send.at[zz], ac_recv.at[zz], partner)

            for zz in range(NZ):
                to_core(zz).start()
            for kind in (0, 1):
                turn(kind, 0)

            def along(flow, zz, slot):
                return remote(
                    a.at[share(c, zz)], ar_z.at[flow, slot], az_send.at[flow, slot], az_recv.at[flow, slot],
                    (dp, z - 1 if flow == 0 else z + 1),
                )

            for j in range(NZ):
                zz = j
                to_core(zz).wait_recv()
                a[share(c, zz), :] = add_low(a[share(c, zz), :], ar_core[zz])
            for j in range(NZ - 1):
                @pl.when(z == NZ - 1)
                def _():
                    along(0, j, j).start()

                @pl.when(z == 0)
                def _():
                    along(1, NZ - 1 - j, NZ - 2 - j).start()

            def sum_step(j):
                for flow, dest in ((0, j), (1, NZ - 1 - j)):
                    slot = dest if flow == 0 else dest - 1
                    if 0 <= slot < NZ - 1:
                        passes = middle(0, flow, 0, dest)

                        @pl.when(jnp.logical_or(passes, z == dest))
                        def _():
                            along(flow, dest, slot).wait_recv()
                            a[share(c, dest), :] = add_low(a[share(c, dest), :], ar_z[flow, slot])

                        @pl.when(passes)
                        def _():
                            along(flow, dest, slot).start()

            one(2)
            for j in range(NZ):
                sum_step(j)
                if j == 1:
                    for kind in (0, 1):
                        turn(kind, 1)

            halves = (slice(0, 208), slice(208, SHARE))

            def cross(stage_no, half, src):
                dest = (ar_xy1, ar_xy2)[stage_no].at[halves[half]]
                way = half if stage_no == 0 else 1 - half
                return remote(
                    src, dest, ax_send.at[stage_no, half], ax_recv.at[stage_no, half], (flips[way] * 2 + c, z)
                )

            def mine(half):
                start_row = 0 if half == 0 else 208
                size = 208 if half == 0 else SHARE - 208
                return pl.ds(pl.multiple_of((c * NZ + z) * SHARE + start_row, 16), size)

            for half in (0, 1):
                cross(0, half, a.at[mine(half)]).start()
            for half in (0, 1):
                cross(0, half, a.at[mine(half)]).wait_recv()
                ar_t[halves[half], :] = add_low(a[mine(half), :], ar_xy1[halves[half], :])
                cross(1, half, ar_t.at[halves[half]]).start()
            one(3)
            for half in (0, 1):
                cross(1, half, ar_t.at[halves[half]]).wait()
                ar_t[halves[half], :] = add_low(ar_t[halves[half], :], ar_xy2[halves[half], :])
                cross(0, half, a.at[mine(half)]).wait_send()
            for zz in range(NZ):
                to_core(zz).wait_send()
                for flow in (0, 1):
                    slot = zz if flow == 0 else zz - 1
                    if 0 <= slot < NZ - 1:
                        goes = (z > zz) if flow == 0 else (z < zz)

                        @pl.when(goes)
                        def _():
                            along(flow, zz, slot).wait_send()

        pl.run_scoped(shared, V((TOTAL, D), BF16), V((MB, T, D), BF16))

    def body(wg_b, wg_i, act_s, gh_s, x_s, gp_s, xp):
        def fetch(e, which):
            pairs = ((act, act_s), (gp, gp_s), (xr, x_s), (gh, gh_s))
            return [
                pltpu.make_async_copy(pairs[i][0].at[e], pairs[i][1], o_sem.at[i]) for i in which
            ]

        def pull(e, which):
            for copy in fetch(e, which):
                copy.start()

        def ready(e, which):
            for copy in fetch(e, which):
                copy.wait()

        pull(0, (0, 1, 2, 3))

        def one(e):
            def back_block(k, side):
                at = pl.ds(pl.multiple_of((2 * k + side) * PART, 128), PART)
                return dot(act_s[:, at], gp_s[...], TN)

            ready(e, (0, 1))

            if e > 0:
                core_copy(0, e - 1, wg_b).wait_send()

            def other_b(k, carry):
                wg_b[k] = back_block(k, 1 - c).astype(BF16)
                return carry

            lax.fori_loop(0, 4, other_b, 0)
            core_copy(0, e, wg_b).start()
            ready(e, (2, 3))
            for side in (0, 1):
                for k in range(4):
                    band = (2 * k + side) * BAND
                    xp[side, :, k * BAND : (k + 1) * BAND] = x_s[:, band : band + BAND]

            if e > 0:
                core_copy(1, e - 1, wg_i).wait_send()

            def other_i(f, carry):
                at = pl.ds(pl.multiple_of(f * CHUNK, 128), CHUNK)
                grad = dot(xp[1 - c], gh_s[:, at], TN).astype(BF16)
                for k in range(4):
                    wg_i[k, :, at] = grad[k * BAND : (k + 1) * BAND]
                return carry

            lax.fori_loop(0, 4, other_i, 0)
            core_copy(1, e, wg_i).start()
            core_copy(0, e, wg_b).wait_recv()

            def own_b(k, carry):
                core_b[e, k] = (core_b[e, k].astype(F32) + back_block(k, c)).astype(BF16)
                return carry

            lax.fori_loop(0, 4, own_b, 0)

            send1(0, e)
            if e < LOCAL - 1:
                pull(e + 1, (0, 1))

            core_copy(1, e, wg_i).wait_recv()

            def own_i(f, carry):
                at = pl.ds(pl.multiple_of(f * CHUNK, 128), CHUNK)
                grad = dot(xp[c], gh_s[:, at], TN)
                for k in range(4):
                    core_i[e, k, :, at] = (
                        core_i[e, k, :, at].astype(F32) + grad[k * BAND : (k + 1) * BAND]
                    ).astype(BF16)
                return carry

            lax.fori_loop(0, 4, own_i, 0)

            send1(1, e)
            if e < LOCAL - 1:
                pull(e + 1, (2, 3))

        one(0)
        pl.run_scoped(
            functools.partial(attention_grads, one),
            V((MB, T, 3 * D), BF16), V((MB, T, D), BF16), V((MB, T, D), BF16), V((EXTRA, D), F32),
        )
        core_copy(0, LOCAL - 1, wg_b).wait_send()
        core_copy(1, LOCAL - 1, wg_i).wait_send()

    pl.run_scoped(
        body,
        V((4, PART, D), BF16), V((4, BAND, HIDDEN), BF16), V((rows, HIDDEN), BF16), V((rows, HIDDEN), BF16),
        V((rows, D), BF16), V((rows, D), BF16), V((2, rows, D // 2), BF16),
    )

    def place(zz):
        return ar_o.at[pl.ds(pl.multiple_of((c * NZ + zz) * SHARE, 16), SHARE)]

    own_share = pltpu.make_async_copy(ar_t, place(z), l_sem.at[6])
    own_share.start()

    def spread(up, h):
        source = z - h if up else z + h
        index = (0 if up else 1, h)
        return remote(
            ar_t if h == 0 else place(source), place(source), zz_send.at[index], zz_recv.at[index],
            (dp, z + 1 if up else z - 1),
        )

    def leaves(up, h):
        return jnp.logical_and(z - h >= 0, z + 1 < NZ) if up else jnp.logical_and(z + h < NZ, z >= 1)

    def to_partner(src, k, zz):
        return remote(src, place(zz), cc_send.at[k], cc_recv.at[k], partner)

    for up in (True, False):
        @pl.when(leaves(up, 0))
        def _():
            spread(up, 0).start()

    to_partner(ar_t, 0, z).start()
    for mb in range(MB):
        def image_out(base, quad_s, low):
            quad = [quad_s.at[i] for i in range(NZ)]
            fetch = pltpu.make_async_copy(resid.at[mb], base, l_sem.at[5])
            fetch.start()
            load_item(quad, 1 + mb)
            fetch.wait()
            low[...] = (base[...] + quad_sum(quad)).astype(BF16)
            store = pltpu.make_async_copy(low, block_o.at[mb], l_sem.at[7])
            store.start()
            store.wait()

        pl.run_scoped(image_out, V((T, D), F32), V((NZ, T, D), BF16), V((T, D), BF16))
    for h in range(NZ - 1):
        for up in (True, False):
            source = z - h - 1 if up else z + h + 1

            @pl.when((z - h - 1 >= 0) if up else (z + h + 1 < NZ))
            def _():
                index = (0 if up else 1, h)
                remote(
                    place(source), place(source), zz_send.at[index], zz_recv.at[index],
                    (dp, z - 1 if up else z + 1),
                ).wait_recv()
                k = lax.rem(source - z + NZ, NZ)
                to_partner(place(source), k, source).start()

            if h + 1 < NZ - 1:
                @pl.when(leaves(up, h + 1))
                def _():
                    spread(up, h + 1).start()
        if h < 2:
            for kind in (0, 1):
                turn(kind, 2 + h)
    own_share.wait()
    for k in range(NZ):
        zz = lax.rem(z + k, NZ)
        src = ar_t if k == 0 else place(zz)
        to_partner(src, k, zz).wait_send()
        other = ar_o.at[pl.ds(pl.multiple_of(((1 - c) * NZ + zz) * SHARE, 16), SHARE)]
        remote(other, other, cc_send.at[k], cc_recv.at[k], partner).wait_recv()
    for h in range(NZ - 1):
        for up in (True, False):
            @pl.when(leaves(up, h))
            def _():
                spread(up, h).wait_send()
    for item in range(3):
        for d in range(1, NZ):
            home(item, d).wait_send()
    for kind in (0, 1):
        for e in range(LOCAL):
            for slot in (0, 1):
                hop1(kind, e, slot).wait_send()
            hop2(kind, e).wait()
            keep(kind, e).wait()


def grads_call(*operands):
    vm = pl.BlockSpec(memory_space=pltpu.VMEM)
    hb = pl.BlockSpec(memory_space=pl.ANY)
    S = jax.ShapeDtypeStruct
    V = pltpu.VMEM
    DMA = pltpu.SemaphoreType.DMA
    outs = [
        (S((MB, T, D), BF16), hb),
        (S((MB, T, D), F32), hb),
        (S((TOTAL, D), BF16), hb),
        (S((LOCAL, PART, D), BF16), hb),
        (S((LOCAL, BAND, HIDDEN), BF16), hb),
        (S((LOCAL, PART, D), BF16), hb),
        (S((LOCAL, BAND, HIDDEN), BF16), hb),
        (S((3, NZ, T, D), BF16), hb),
    ]
    return pl.pallas_call(
        grads_kernel,
        out_shape=[o[0] for o in outs],
        in_specs=[vm] * 6 + [hb] * 15,
        out_specs=[o[1] for o in outs],
        scratch_shapes=[
            V((LOCAL, 4, PART, D), BF16), V((LOCAL, 4, BAND, HIDDEN), BF16),
            V((LOCAL, 2, PART, D), BF16), V((LOCAL, 2, BAND, HIDDEN), BF16),
            V((NZ, SHARE, D), BF16), V((2, NZ - 1, SHARE, D), BF16),
            V((SHARE, D), BF16), V((SHARE, D), BF16), V((SHARE, D), BF16),
            V((NZ, MB, 8, T), F32),
            DMA((2, LOCAL)), DMA((2, LOCAL)), DMA((2, LOCAL, 2)), DMA((2, LOCAL, 2)), DMA((2, LOCAL)), DMA((2, LOCAL)),
            DMA((3, NZ - 1)), DMA((3, NZ - 1)), DMA((NZ - 1,)), DMA((NZ - 1,)),
            DMA((NZ,)), DMA((NZ,)), DMA((2, NZ - 1)), DMA((2, NZ - 1)), DMA((2, 2)), DMA((2, 2)),
            DMA((2, NZ - 1)), DMA((2, NZ - 1)), DMA((NZ,)), DMA((NZ,)),
            DMA((8,)), DMA((14,)), DMA((2, LOCAL)),
        ],
        compiler_params=pltpu.CompilerParams(
            collective_id=2, has_side_effects=True, vmem_limit_bytes=63 << 20
        ),
        name="grads",
    )(*operands)

def fast_body(
    tokens, routes, gain_one, shift_one, w_qkv, qv_bias, w_out, out_bias, gain_two, shift_two,
    w_route, w_in, b_in, w_back, b_back, d_out,
):
    def windows(a):
        return jnp.pad(a.reshape(MB, SEQ, a.shape[1]), ((0, 0), (0, T - SEQ), (0, 0)))

    tok, dout = windows(tokens), windows(d_out)
    rt = jnp.pad(
        jnp.transpose(routes.reshape(MB, SEQ, TOP), (0, 2, 1)),
        ((0, 0), (0, 8 - TOP), (0, T - SEQ)), constant_values=-1,
    )
    vec = jnp.stack(
        [gain_one, shift_one, gain_two, shift_two, out_bias, qv_bias[0], qv_bias[1], jnp.zeros_like(out_bias)]
    )
    wrt = jnp.pad(w_route.T.reshape(NZ, LOCAL, D), ((0, 0), (0, 8 - LOCAL), (0, 0))).reshape(32, D)
    (qkv, mixed, resid, rp, gg, bb, bi, xr, gp, act, gh, pb, pg, pg0) = dispatch_call(
        tok, rt, vec, w_qkv, w_out, wrt, b_in, b_back, dout, w_in, w_back
    )
    block, ig, ar, kb, ki, lb, li, _ = grads_call(
        vec, rt, wrt, bb, bi, rp, tok, dout, w_qkv, w_out, qkv, mixed, resid, gg, xr, gp, act, gh, pb, pg, pg0
    )
    dp, z = lax.axis_index("dp"), lax.axis_index("expert")
    rows = MB * SEQ
    ext = ar[4 * D :].astype(F32)
    qkv_grad = jnp.concatenate([ar[i * D : (i + 1) * D] for i in range(3)], axis=1).astype(F32)
    biases = lax.dynamic_slice(ext, (24 + 5 * LOCAL * z, 0), (5 * LOCAL, D))
    bb_grad = lax.dynamic_slice(biases[:LOCAL], (0, dp * BAND), (LOCAL, BAND))
    bi_grad = jnp.transpose(biases[LOCAL:].reshape(4, LOCAL, D), (1, 0, 2)).reshape(LOCAL, HIDDEN)
    bi_grad = lax.dynamic_slice(bi_grad, (0, dp * PART), (LOCAL, PART))
    return (
        block[:, :SEQ].reshape(rows, D),
        ig[:, :SEQ].reshape(rows, D),
        ext[0],
        ext[1],
        qkv_grad,
        ext[2:4],
        ar[3 * D : 4 * D].astype(F32),
        ext[4],
        ext[5],
        ext[6],
        ext[8 : 8 + NZ * LOCAL].T,
        ki.astype(F32) + li.astype(F32),
        bi_grad,
        kb.astype(F32) + lb.astype(F32),
        bb_grad,
    )


def solution(mesh):
    fast = mesh.shape["dp"] == 8 and mesh.shape["expert"] == NZ
    return jax.shard_map(
        fast_body if fast else general_body,
        mesh=mesh,
        in_specs=(
            P(("dp", "expert"), None),
            P(("dp", "expert"), None),
            P(),
            P(),
            P(),
            P(),
            P(),
            P(),
            P(),
            P(),
            P(),
            P("expert", None, None),
            P("expert", None),
            P("expert", None, None),
            P("expert", None),
            P(("dp", "expert"), None),
        ),
        out_specs=(
            P(("dp", "expert"), None),
            P(("dp", "expert"), None),
            P(),
            P(),
            P(),
            P(),
            P(),
            P(),
            P(),
            P(),
            P(),
            P("expert", "dp", None),
            P("expert", "dp"),
            P("expert", "dp", None),
            P("expert", "dp"),
        ),
        check_vma=False,
    )
```

```python
import functools

import jax
import jax.numpy as jnp
from jax import lax
from jax.experimental import pallas as pl
from jax.experimental.pallas import tpu as pltpu
from jax.sharding import PartitionSpec as P

HEADS = 12
HEAD_DIM = 64
SEQ = 197
TOP = 2
MB = 2
ROWS_MB = 197
D = 768


HIGH = lax.Precision.HIGHEST
EPSILON = 1e-06


def layer_norm(value, gain, shift):
    center = value - jnp.mean(value, axis=-1, keepdims=True)
    spread = jnp.mean(center * center, axis=-1, keepdims=True)
    return center * lax.rsqrt(spread + EPSILON) * gain + shift


def route_soft(logits):
    return jax.nn.softmax(logits, axis=-1)


def general_body(
    tokens,
    routes,
    gain_one,
    shift_one,
    w_qkv,
    qv_bias,
    w_out,
    out_bias,
    gain_two,
    shift_two,
    w_route,
    w_in,
    b_in,
    w_back,
    b_back,
    d_out,
):
    groups = lax.axis_size("expert")
    local = w_in.shape[0]
    experts = groups * local
    width = tokens.shape[1]
    rows = ROWS_MB
    cap = 5 * rows * TOP // (3 * experts)
    images = rows // SEQ
    scale = HEAD_DIM ** (-0.5)
    expert_ids = jnp.arange(experts, dtype=jnp.int32)
    w_route_wide = w_route.astype(jnp.float32)
    acc_gain_one = jnp.zeros_like(gain_one)
    acc_shift_one = jnp.zeros_like(shift_one)
    acc_qkv = jnp.zeros(w_qkv.shape, jnp.float32)
    acc_qv = jnp.zeros_like(qv_bias)
    acc_out = jnp.zeros(w_out.shape, jnp.float32)
    acc_out_bias = jnp.zeros_like(out_bias)
    acc_gain_two = jnp.zeros_like(gain_two)
    acc_shift_two = jnp.zeros_like(shift_two)
    acc_route = jnp.zeros(w_route.shape, jnp.float32)
    acc_expert = None
    outputs = []
    input_grads = []
    for part in range(MB):
        x = tokens[part * rows : (part + 1) * rows].astype(jnp.float32)
        route = routes[part * rows : (part + 1) * rows]
        cotan = d_out[part * rows : (part + 1) * rows].astype(jnp.float32)
        normed, ln_one_pull = jax.vjp(layer_norm, x, gain_one, shift_one)
        normed_low = normed.astype(jnp.bfloat16)
        bias = jnp.concatenate([qv_bias[0], jnp.zeros_like(qv_bias[0]), qv_bias[1]])
        qkv = (jnp.dot(normed_low, w_qkv, preferred_element_type=jnp.float32) + bias).astype(
            jnp.bfloat16
        )
        query = qkv[:, :width].reshape(images, SEQ, HEADS, HEAD_DIM)
        keys = qkv[:, width : 2 * width].reshape(images, SEQ, HEADS, HEAD_DIM)
        values = qkv[:, 2 * width :].reshape(images, SEQ, HEADS, HEAD_DIM)
        scores = (
            jnp.einsum("ishd,ithd->ihst", query, keys, preferred_element_type=jnp.float32) * scale
        )
        log_total = jax.nn.logsumexp(scores, axis=-1, keepdims=True)
        probs_low = jnp.exp(scores - log_total).astype(jnp.bfloat16)
        mixed = jnp.einsum("ihst,ithd->ishd", probs_low, values, preferred_element_type=jnp.float32)
        mixed = mixed.reshape(rows, width).astype(jnp.bfloat16)
        resid = x + jnp.dot(mixed, w_out, preferred_element_type=jnp.float32) + out_bias
        inner, ln_two_pull = jax.vjp(layer_norm, resid, gain_two, shift_two)
        inner_low = inner.astype(jnp.bfloat16)
        logits = jnp.dot(inner_low, w_route, preferred_element_type=jnp.float32)
        route_probs, soft_pull = jax.vjp(route_soft, logits)
        choose = (route[:, :, None] == expert_ids[None, None, :]).astype(jnp.float32)
        gates = jnp.einsum("rke,re->rk", choose, route_probs, precision=HIGH)
        flat_ids = route.reshape(-1)
        table = (flat_ids[:, None] == expert_ids[None, :]).astype(jnp.int32)
        order = jnp.arange(rows * TOP, dtype=jnp.int32)
        earlier = (order[None, :] < order[:, None]).astype(jnp.bfloat16)
        before = jnp.dot(
            earlier, table.astype(jnp.bfloat16), preferred_element_type=jnp.float32
        ).astype(jnp.int32)
        slot = jnp.sum(before * table, axis=1)
        dest = flat_ids * cap + slot
        sending = (
            jnp.zeros((experts * cap, width), jnp.bfloat16)
            .at[dest]
            .set(jnp.repeat(inner_low, TOP, axis=0))
        )
        sending = sending.reshape(groups, local, cap, width)
        received = lax.all_to_all(sending, "expert", split_axis=0, concat_axis=0, tiled=True)
        hidden = jnp.einsum("secd,edf->secf", received, w_in, preferred_element_type=jnp.float32)
        hidden = hidden + b_in[None, :, None, :]
        active = jax.nn.gelu(hidden).astype(jnp.bfloat16)
        result = jnp.einsum("secf,efd->secd", active, w_back, preferred_element_type=jnp.float32)
        result = (result + b_back[None, :, None, :]).astype(jnp.bfloat16)
        returned = lax.all_to_all(result, "expert", split_axis=0, concat_axis=0, tiled=True)
        returned, kept_rows, kept_hidden = (returned, received, hidden)
        picked = (
            returned.reshape(experts * cap, width)[dest]
            .reshape(rows, TOP, width)
            .astype(jnp.float32)
        )
        block = resid + jnp.sum(gates[:, :, None] * picked, axis=1)
        outputs.append(block.astype(jnp.bfloat16))
        grad_gate = jnp.sum(picked * cotan[:, None, :], axis=2)
        grad_picked = (gates[:, :, None] * cotan[:, None, :]).astype(jnp.bfloat16)
        grad_send = (
            jnp.zeros((experts * cap, width), jnp.bfloat16)
            .at[dest]
            .set(grad_picked.reshape(rows * TOP, width))
        )
        grad_send = grad_send.reshape(groups, local, cap, width)
        grad_recv = lax.all_to_all(grad_send, "expert", split_axis=0, concat_axis=0, tiled=True)
        active, gelu_pull = jax.vjp(jax.nn.gelu, kept_hidden)
        active_low = active.astype(jnp.bfloat16)
        grad_active = jnp.einsum(
            "secd,efd->secf", grad_recv, w_back, preferred_element_type=jnp.float32
        )
        grad_hidden = gelu_pull(grad_active)[0].astype(jnp.bfloat16)
        step_w_back = jnp.einsum(
            "secf,secd->efd", active_low, grad_recv, preferred_element_type=jnp.float32
        )
        step_b_back = jnp.sum(grad_recv.astype(jnp.float32), axis=(0, 2))
        step_w_in = jnp.einsum(
            "secd,secf->edf", kept_rows, grad_hidden, preferred_element_type=jnp.float32
        )
        step_b_in = jnp.sum(grad_hidden.astype(jnp.float32), axis=(0, 2))
        grad_rows = jnp.einsum(
            "secf,edf->secd", grad_hidden, w_in, preferred_element_type=jnp.float32
        )
        grad_rows = grad_rows.astype(jnp.bfloat16)
        grad_back = lax.all_to_all(grad_rows, "expert", split_axis=0, concat_axis=0, tiled=True)
        shares = (step_w_in, step_b_in, step_w_back, step_b_back)
        if acc_expert is None:
            acc_expert = shares
        else:
            acc_expert = tuple((a + b for a, b in zip(acc_expert, shares)))
        grad_inner = jnp.sum(
            grad_back.reshape(experts * cap, width)[dest]
            .reshape(rows, TOP, width)
            .astype(jnp.float32),
            axis=1,
        )
        grad_probs = jnp.einsum("rk,rke->re", grad_gate, choose, precision=HIGH)
        grad_logits = soft_pull(grad_probs)[0]
        acc_route = acc_route + jnp.einsum(
            "rd,re->de", inner_low.astype(jnp.float32), grad_logits, precision=HIGH
        )
        grad_inner = grad_inner + jnp.einsum("re,de->rd", grad_logits, w_route_wide, precision=HIGH)
        grad_ln_two, grad_gain_two, grad_shift_two = ln_two_pull(grad_inner)
        acc_gain_two = acc_gain_two + grad_gain_two
        acc_shift_two = acc_shift_two + grad_shift_two
        grad_resid = cotan + grad_ln_two
        grad_att = grad_resid.astype(jnp.bfloat16)
        acc_out = acc_out + jnp.einsum(
            "rd,re->de", mixed, grad_att, preferred_element_type=jnp.float32
        )
        acc_out_bias = acc_out_bias + jnp.sum(grad_att.astype(jnp.float32), axis=0)
        grad_mixed = jnp.einsum("re,de->rd", grad_att, w_out, preferred_element_type=jnp.float32)
        grad_mixed = grad_mixed.astype(jnp.bfloat16).reshape(images, SEQ, HEADS, HEAD_DIM)
        again = (
            jnp.einsum("ishd,ithd->ihst", query, keys, preferred_element_type=jnp.float32) * scale
        )
        probs = jnp.exp(again - log_total)
        grad_probs_att = jnp.einsum(
            "ishd,ithd->ihst", grad_mixed, values, preferred_element_type=jnp.float32
        )
        row_total = jnp.sum(probs * grad_probs_att, axis=-1, keepdims=True)
        grad_scores = (probs * (grad_probs_att - row_total)).astype(jnp.bfloat16)
        grad_query = (
            jnp.einsum("ihst,ithd->ishd", grad_scores, keys, preferred_element_type=jnp.float32)
            * scale
        )
        grad_keys = (
            jnp.einsum("ihst,ishd->ithd", grad_scores, query, preferred_element_type=jnp.float32)
            * scale
        )
        grad_values = jnp.einsum(
            "ihst,ishd->ithd",
            probs.astype(jnp.bfloat16),
            grad_mixed,
            preferred_element_type=jnp.float32,
        )
        grad_qkv = jnp.concatenate(
            [
                grad_query.reshape(rows, width),
                grad_keys.reshape(rows, width),
                grad_values.reshape(rows, width),
            ],
            axis=1,
        ).astype(jnp.bfloat16)
        acc_qkv = acc_qkv + jnp.einsum(
            "rd,re->de", normed_low, grad_qkv, preferred_element_type=jnp.float32
        )
        column_sums = jnp.sum(grad_qkv.astype(jnp.float32), axis=0)
        acc_qv = acc_qv + jnp.stack([column_sums[:width], column_sums[2 * width :]])
        grad_normed = jnp.einsum("re,de->rd", grad_qkv, w_qkv, preferred_element_type=jnp.float32)
        grad_ln_one, grad_gain_one, grad_shift_one = ln_one_pull(grad_normed)
        acc_gain_one = acc_gain_one + grad_gain_one
        acc_shift_one = acc_shift_one + grad_shift_one
        input_grads.append(grad_resid + grad_ln_one)
    expert_grads = (
        lax.psum_scatter(
            acc_expert[0].astype(jnp.bfloat16), "dp", scatter_dimension=1, tiled=True
        ).astype(jnp.float32),
        lax.psum_scatter(
            acc_expert[1].astype(jnp.bfloat16), "dp", scatter_dimension=1, tiled=True
        ).astype(jnp.float32),
        lax.psum_scatter(
            acc_expert[2].astype(jnp.bfloat16), "dp", scatter_dimension=1, tiled=True
        ).astype(jnp.float32),
        lax.psum_scatter(
            acc_expert[3].astype(jnp.bfloat16), "dp", scatter_dimension=1, tiled=True
        ).astype(jnp.float32),
    )
    shared = (
        acc_gain_one,
        acc_shift_one,
        acc_qkv,
        acc_qv,
        acc_out,
        acc_out_bias,
        acc_gain_two,
        acc_shift_two,
        acc_route,
    )
    shared = lax.psum(
        (
            shared[0],
            shared[1],
            shared[2],
            shared[3],
            shared[4],
            shared[5],
            shared[6],
            shared[7],
            shared[8],
        ),
        ("dp", "expert"),
    )
    return (
        jnp.concatenate(outputs, axis=0),
        jnp.concatenate(input_grads, axis=0),
        shared[0],
        shared[1],
        shared[2],
        shared[3],
        shared[4],
        shared[5],
        shared[6],
        shared[7],
        shared[8],
        expert_grads[0],
        expert_grads[1],
        expert_grads[2],
        expert_grads[3],
    )


F32, BF16 = jnp.float32, jnp.bfloat16
NZ = 4
LOCAL = 4
PAIRS = HEADS // 2
T = 208
KEYS = 256
CAP = 41
CAP_ROWS = 48
PACKED = 176
ROWS = NZ * CAP_ROWS
CHUNK = 768
MESH = pl.DeviceIdType.MESH
NT = (((1,), (1,)), ((), ()))
TN = (((0,), (0,)), ((), ()))


def dot(a, b, dims=(((1,), (0,)), ((), ()))):
    return lax.dot_general(a, b, dims, preferred_element_type=F32)


def normal(value):
    center = value - jnp.mean(value, axis=-1, keepdims=True)
    scale = lax.rsqrt(jnp.mean(center * center, axis=-1, keepdims=True) + EPSILON)
    return center * scale, scale


def half_mask(which):
    lane = lax.broadcasted_iota(jnp.int32, (1, 128), 1)
    return ((lane < 64) if which == 0 else (lane >= 64)).astype(F32).astype(BF16)


def attention_probs(scores):
    key = lax.broadcasted_iota(jnp.int32, scores.shape, 1)
    scores = jnp.where(key < SEQ, scores, -1e30)
    top = jnp.max(scores, axis=-1, keepdims=True)
    raised = jnp.exp(scores - top)
    return raised / jnp.sum(raised, axis=-1, keepdims=True)


def route_softmax(logits, real):
    logits = jnp.where(real, logits, -1e30)
    raised = jnp.exp(logits - jnp.max(logits, axis=0, keepdims=True))
    raised = jnp.where(real, raised, 0.0)
    return raised / jnp.sum(raised, axis=0, keepdims=True)


def pick_matrix(slots):
    index = lax.broadcasted_iota(jnp.int32, (CAP_ROWS, T), 0).astype(F32)
    return jnp.concatenate(
        [(index == slots[e : e + 1, :]).astype(F32) for e in range(LOCAL)], axis=0
    )


def dispatch_kernel(
    tok, dout, routes, v0, v1, v2, v3, v4, qv, wqkv, wout, wrt, b_in, b_back, w_in, w_back,
    vec, tab_o, tw_o, qkv_o, mixed_o, resid_o, rp_o, gg_o, bb_o, bi_o, dw_o, x_o, gp_o, act_o, gh_o, pb_o, pg_o, home_o,
    gi, gd, sl, sg, dense, qkv_s, mixed_s, inner_s, xs, gs, cs, rgs, ggs, wb1, wb2, act_st, gh_st, acc_o, acc_g,
    os_, grs, pb_s, pg_s,
    send_sem, recv_sem, d_sem, w_sem, st_sem, x_sem, p_sem, h_send, h_recv,
):
    dp = lax.axis_index("dp")
    z = lax.axis_index("expert")

    def item_ref(kind, source, mb):
        return (gd, sg, gi, sl)[kind].at[source, mb]

    def copy_of(up, kind, mb, h, source, target, packed):
        index = (0 if up else 1, kind * MB + mb, h)
        dst = item_ref(kind, source, mb)
        src = dst
        if packed:
            src, dst = dense.at[kind // 2, mb, h], dst.at[0:PACKED]
        return pltpu.make_async_remote_copy(
            src_ref=src, dst_ref=dst, send_sem=send_sem.at[index], recv_sem=recv_sem.at[index],
            device_id=(dp, target), device_id_type=MESH,
        )

    def hop(up, kind, mb, h, packed):
        return copy_of(up, kind, mb, h, z - h if up else z + h, z + 1 if up else z - 1, packed)

    def leaves(up, h):
        return jnp.logical_and(z - h >= 0, z + 1 < NZ) if up else jnp.logical_and(z + h < NZ, z >= 1)

    def arrives(up, h):
        return (z - h - 1 >= 0) if up else (z + h + 1 < NZ)

    def to_end(up):
        return (z + 1 == NZ - 1) if up else (z == 1)

    def at_end(up):
        return (z == NZ - 1) if up else (z == 0)

    def each(kind, condition, where, action):
        if kind in (0, 2):
            @pl.when(jnp.logical_and(condition, where))
            def _():
                action(True)

            @pl.when(jnp.logical_and(condition, jnp.logical_not(where)))
            def _():
                action(False)
        else:
            @pl.when(condition)
            def _():
                action(False)

    def start(kind, mb, h):
        for up in (True, False):
            def go(packed):
                if packed:
                    source = z - h if up else z + h
                    slots = sl[source, mb, NZ - 1 if up else 0]
                    row = lax.broadcasted_iota(jnp.int32, (PACKED, T), 0)
                    owner = row // CAP
                    wanted = jnp.full((PACKED, T), -5.0, F32)
                    for e in range(LOCAL):
                        wanted = jnp.where(owner == e, slots[e : e + 1, :], wanted)
                    chosen = (wanted == (row - owner * CAP).astype(F32)).astype(F32).astype(BF16)
                    dense[kind // 2, mb, h] = dot(chosen, item_ref(kind, source, mb)[...]).astype(BF16)
                hop(up, kind, mb, h, packed).start()

            each(kind, leaves(up, h), to_end(up), go)

    def pass_on(kind, mb, h):
        for up in (True, False):
            def take(packed):
                source = z - h - 1 if up else z + h + 1
                copy_of(up, kind, mb, h, source, z - 1 if up else z + 1, packed).wait_recv()

            each(kind, arrives(up, h), at_end(up), take)
        if h + 1 < NZ - 1:
            start(kind, mb, h + 1)

    def weights(n, slot):
        e = lax.rem(n, 16) // 4
        f = lax.rem(n, 4)
        cols = pl.ds(pl.multiple_of(f * CHUNK, CHUNK), CHUNK)
        return (
            pltpu.make_async_copy(w_in.at[e, :, cols], wb1.at[slot], w_sem.at[0, slot]),
            pltpu.make_async_copy(w_back.at[e, cols, :], wb2.at[slot], w_sem.at[1, slot]),
        )

    for copy in weights(0, 0):
        copy.start()
    for ref in (gi, gd):
        for source in range(NZ):
            for mb in range(MB):
                ref[source, mb, PACKED:T, :] = jnp.zeros((T - PACKED, D), BF16)
    for row, ref in enumerate((v0, v1, v2, v3, v4)):
        vec[row : row + 1, :] = ref[...].reshape(1, D)
    vec[5:7, :] = qv[...]
    vec[7:8, :] = jnp.zeros((1, D), F32)
    lane = lax.broadcasted_iota(jnp.int32, (1, 32), 1)
    part = lax.rem(lane, 8)
    expert_of = jnp.where(part < LOCAL, (lane // 8) * LOCAL + part, -7)
    chosen_all = jnp.logical_or(routes[:, 0:1] == expert_of, routes[:, 1:2] == expert_of)
    chosen_all = chosen_all.astype(F32).astype(BF16)
    token = lax.broadcasted_iota(jnp.int32, (MB * SEQ, T), 0)
    column = lax.broadcasted_iota(jnp.int32, (MB * SEQ, T), 1)
    for mb in range(MB):
        here = jnp.logical_and(token == column + mb * SEQ, column < SEQ).astype(F32).astype(BF16)
        ahead = jnp.logical_and(token >= mb * SEQ, token < column + mb * SEQ).astype(F32).astype(BF16)
        table = dot(chosen_all, here, TN)
        tab_o[mb] = table
        slots = jnp.where(table > 0.5, dot(chosen_all, ahead, TN), -1.0)
        for p in range(NZ):
            sl[z, mb, p] = slots[8 * p : 8 * p + 8, :]
        tw_o[mb] = dot(here, tok[...], TN).astype(BF16)
        gd[z, mb] = dot(here, dout[...], TN).astype(BF16)
    barrier = pltpu.get_barrier_semaphore()
    for d in range(1, NZ):
        pl.semaphore_signal(barrier, inc=1, device_id=(dp, lax.rem(z + d, NZ)), device_id_type=MESH)
    pl.semaphore_wait(barrier, NZ - 1)
    start(3, 0, 0)
    start(0, 0, 0)
    start(3, 1, 0)
    own = [pltpu.make_async_copy(gd.at[z, mb], dw_o.at[mb], d_sem.at[mb]) for mb in range(MB)]
    for copy in own:
        copy.start()

    qkv_s[T:KEYS, :] = jnp.zeros((KEYS - T, 3 * D), BF16)
    bb_o[...] = jnp.zeros_like(bb_o)
    bi_o[...] = jnp.zeros_like(bi_o)

    def forward(mb, carry):
        x = tw_o[mb].astype(F32)
        normed = (normal(x)[0] * vec[0:1] + vec[1:2]).astype(BF16)
        for c in range(3):
            cols = slice(c * D, (c + 1) * D)
            part = dot(normed, wqkv[:, cols])
            if c != 1:
                row = 5 if c == 0 else 6
                part = part + vec[row : row + 1]
            qkv_s[0:T, cols] = part.astype(BF16)

        def heads(p, carry):
            at = [pl.ds(pl.multiple_of(c * D + p * 128, 128), 128) for c in range(3)]
            q, k, v = qkv_s[0:T, at[0]], qkv_s[:, at[1]], qkv_s[:, at[2]]
            mixed = jnp.zeros((T, 128), F32)
            for which in (0, 1):
                mask = half_mask(which)
                probs = attention_probs(dot(q, k * mask, NT) * HEAD_DIM ** (-0.5))
                mixed = mixed + dot(probs.astype(BF16), v * mask)
            mixed_s[:, at[0]] = mixed.astype(BF16)
            return carry

        lax.fori_loop(0, PAIRS, heads, 0)
        qkv_o[mb] = qkv_s[0:T, :]
        mixed_o[mb] = mixed_s[...]
        resid = x + dot(mixed_s[...], wout[...]) + vec[4:5]
        resid_o[mb] = resid
        inner = (normal(resid)[0] * vec[2:3] + vec[3:4]).astype(BF16)
        gi[z, mb] = inner
        real = lax.rem(lax.broadcasted_iota(jnp.int32, (32, T), 0), 8) < LOCAL
        probs = route_softmax(dot(wrt[...], inner, NT), real)
        rp_o[mb] = probs
        gates = tab_o[mb] * probs
        for p in range(NZ):
            sg[z, mb, p] = gates[8 * p : 8 * p + 8, :]

        @pl.when(mb == 0)
        def _():
            start(1, 0, 0)
            start(2, 0, 0)

        return carry

    lax.fori_loop(0, MB, forward, 0)
    for h in range(NZ - 1):
        for kind in (3, 0, 1, 2):
            pass_on(kind, 0, h)
        pass_on(3, 1, h)
    for kind in range(3):
        start(kind, 1, 0)

    def micro(mb, carry):
        @pl.when(mb == 1)
        def _():
            for kind in range(3):
                pass_on(kind, 1, 2)

        def spread(src, carry):
            pick = pick_matrix(sl[src, mb, z])
            gate = sg[src, mb, z]
            row = lax.broadcasted_iota(jnp.int32, (ROWS, T), 0)
            owner = row // CAP_ROWS
            place = row - owner * CAP_ROWS
            unpack = jnp.logical_and(
                place < CAP, lax.broadcasted_iota(jnp.int32, (ROWS, T), 1) == owner * CAP + place
            ).astype(F32)
            packed = jnp.logical_and(jnp.logical_or(z == 0, z == NZ - 1), src != z)
            low = jnp.where(packed, unpack, pick).astype(BF16)
            rows_x = dot(low, gi[src, mb]).astype(BF16)
            rows_c = dot(low, gd[src, mb])
            at = pl.ds(pl.multiple_of(mb * ROWS + src * CAP_ROWS, 16), CAP_ROWS)
            here = pl.ds(pl.multiple_of(src * CAP_ROWS, 16), CAP_ROWS)
            for e in range(LOCAL):
                part = slice(e * CAP_ROWS, (e + 1) * CAP_ROWS)
                gate_rows = jnp.sum(pick[part] * gate[e : e + 1, :], axis=1, keepdims=True)
                grad = (rows_c[part] * gate_rows).astype(BF16)
                xs[e, at, :] = rows_x[part]
                gs[e, at, :] = grad
                cs[e, here, :] = rows_c[part].astype(BF16)
                rgs[e, here, :] = jnp.broadcast_to(gate_rows, (CAP_ROWS, 128))
                bb_o[e : e + 1, :] += jnp.sum(grad.astype(F32), axis=0, keepdims=True)
            return carry

        lax.fori_loop(0, NZ, spread, 0)
        rows = pl.ds(pl.multiple_of(mb * ROWS, 16), ROWS)

        def expert(e, carry):
            acc_o[...] = jnp.zeros_like(acc_o)
            acc_g[...] = jnp.zeros_like(acc_g)

            def step(f, carry):
                n = mb * 16 + e * 4 + f
                slot = lax.rem(n, 2)
                cols = pl.ds(pl.multiple_of(f * CHUNK, CHUNK), CHUNK)

                @pl.when(n + 1 < 16 * MB)
                def _():
                    for copy in weights(n + 1, 1 - slot):
                        copy.start()

                @pl.when(n >= 2)
                def _():
                    for copy in stores(n - 2, slot):
                        copy.wait()

                for copy in weights(n, slot):
                    copy.wait()
                hid = dot(xs[e, rows, :], wb1[slot]) + b_in[pl.ds(e, 1), cols]
                square = hid * hid
                bend = jnp.tanh(hid * (0.7978845608 + (0.7978845608 * 0.044715) * square))
                half = 0.5 + 0.5 * bend
                act = (hid * half).astype(BF16)
                slope = half + (0.5 * hid) * (1.0 - bend * bend) * (
                    0.7978845608 + (3 * 0.7978845608 * 0.044715) * square
                )

                act_st[slot] = act
                acc_o[...] += dot(act, wb2[slot])
                grad = (dot(gs[e, rows, :], wb2[slot], NT) * slope).astype(BF16)
                gh_st[slot] = grad
                acc_g[...] += dot(grad, wb1[slot], NT)
                bi_o[pl.ds(e, 1), cols] += jnp.sum(grad.astype(F32), axis=0, keepdims=True)
                for copy in stores(n, slot):
                    copy.start()
                return carry

            lax.fori_loop(0, 4, step, 0)
            out = (acc_o[...] + b_back[pl.ds(e, 1), :]).astype(BF16).astype(F32)
            gg = jnp.sum(out * cs[e].astype(F32), axis=1, keepdims=True)
            scaled = (out * rgs[e][:, 0:1]).astype(BF16)
            back = acc_g[...].astype(BF16)
            at = pl.ds(pl.multiple_of(e * CAP_ROWS, 16), CAP_ROWS)
            for src in range(NZ):
                part = slice(src * CAP_ROWS, (src + 1) * CAP_ROWS)
                os_[src, at, :] = scaled[part]
                grs[src, at, :] = back[part]
                ggs[src, at, :] = jnp.broadcast_to(gg[part], (CAP_ROWS, 128))

            @pl.when(jnp.logical_and(mb == 1, e == 0))
            def _():
                for d in range(1, NZ):
                    sent_home(d).start()
                own_home().start()

            @pl.when(jnp.logical_and(mb == 0, e == 1))
            def _():
                for kind in range(3):
                    pass_on(kind, 1, 0)

            @pl.when(jnp.logical_and(mb == 0, e == 3))
            def _():
                for kind in range(3):
                    pass_on(kind, 1, 1)

            return carry

        def stores(n, slot):
            m = n // 16
            e = lax.rem(n, 16) // 4
            f = lax.rem(n, 4)
            at = (e, pl.ds(pl.multiple_of(m * ROWS, 16), ROWS), pl.ds(pl.multiple_of(f * CHUNK, CHUNK), CHUNK))
            return (
                pltpu.make_async_copy(act_st.at[slot], act_o.at[at], st_sem.at[0, slot]),
                pltpu.make_async_copy(gh_st.at[slot], gh_o.at[at], st_sem.at[1, slot]),
            )

        lax.fori_loop(0, LOCAL, expert, 0)

        @pl.when(mb == 1)
        def _():
            for slot in (0, 1):
                for copy in stores(16 * MB - 2 + slot, slot):
                    copy.wait()

        @pl.when(mb == 1)
        def _():
            for src in range(NZ):
                kept(0, src).wait()
            for d in range(1, NZ):
                sent_home(d).wait_send()
            own_home().wait()

        def gather(src, carry):
            pick = pick_matrix(sl[src, mb, z])
            low = pick.astype(BF16)
            pb_s[src] = dot(low, os_[src], TN).astype(BF16)
            pg_s[src] = dot(low, grs[src], TN).astype(BF16)
            kept(mb, src).start()
            for e in range(LOCAL):
                part = slice(e * CAP_ROWS, (e + 1) * CAP_ROWS)
                gg_o[src, mb, e : e + 1, :] = jnp.sum(
                    pick[part] * ggs[src, part, 0:1], axis=0, keepdims=True
                )

            @pl.when(mb == 1)
            def _():
                kept_grad(src).start()

            return carry

        lax.fori_loop(0, NZ, gather, 0)

        @pl.when(mb == 1)
        def _():
            for src in range(NZ):
                kept(1, src).wait()
                kept_grad(src).wait()

        return carry

    def kept(mb, src):
        return pltpu.make_async_copy(pb_s.at[src], pb_o.at[mb, src], p_sem.at[0, src])

    def kept_grad(src):
        return pltpu.make_async_copy(pg_s.at[src], pg_o.at[src], p_sem.at[1, src])

    def sent_home(d):
        target = lax.rem(z + d, NZ)
        return pltpu.make_async_remote_copy(
            src_ref=pg_s.at[target], dst_ref=home_o.at[z], send_sem=h_send.at[d - 1], recv_sem=h_recv.at[d - 1],
            device_id=(dp, target), device_id_type=MESH,
        )

    def own_home():
        return pltpu.make_async_copy(pg_s.at[z], home_o.at[z], d_sem.at[MB])

    gg_o[...] = jnp.zeros_like(gg_o)
    lax.fori_loop(0, MB, micro, 0)
    last = (
        pltpu.make_async_copy(xs, x_o, x_sem.at[0]),
        pltpu.make_async_copy(gs, gp_o, x_sem.at[1]),
    )
    for copy in last:
        copy.start()
    for copy in last:
        copy.wait()
    for d in range(1, NZ):
        source = lax.rem(z + NZ - d, NZ)
        pltpu.make_async_remote_copy(
            src_ref=home_o.at[source], dst_ref=home_o.at[source], send_sem=h_send.at[d - 1],
            recv_sem=h_recv.at[d - 1], device_id=(dp, source), device_id_type=MESH,
        ).wait_recv()
    for copy in own:
        copy.wait()
    for mb in range(MB):
        for kind in range(4):
            for h in range(NZ - 1):
                for up in (True, False):
                    each(
                        kind, leaves(up, h), to_end(up),
                        lambda packed: hop(up, kind, mb, h, packed).wait_send(),
                    )


def dispatch_call(*operands):
    vm = pl.BlockSpec(memory_space=pltpu.VMEM)
    hb = pl.BlockSpec(memory_space=pl.ANY)
    S = jax.ShapeDtypeStruct
    rows = MB * ROWS
    outs = [
        (S((8, D), F32), vm),
        (S((MB, 32, T), F32), vm),
        (S((MB, T, D), BF16), vm),
        (S((MB, T, 3 * D), BF16), vm),
        (S((MB, T, D), BF16), vm),
        (S((MB, T, D), F32), vm),
        (S((MB, 32, T), F32), vm),
        (S((NZ, MB, 8, T), F32), vm),
        (S((LOCAL, D), F32), vm),
        (S((LOCAL, 4 * CHUNK), F32), vm),
        (S((MB, T, D), BF16), hb),
        (S((LOCAL, rows, D), BF16), hb),
        (S((LOCAL, rows, D), BF16), hb),
        (S((LOCAL, rows, 4 * CHUNK), BF16), hb),
        (S((LOCAL, rows, 4 * CHUNK), BF16), hb),
        (S((MB, NZ, T, D), BF16), hb),
        (S((NZ, T, D), BF16), hb),
        (S((NZ, T, D), BF16), hb),
    ]
    V = pltpu.VMEM
    DMA = pltpu.SemaphoreType.DMA
    return pl.pallas_call(
        dispatch_kernel,
        out_shape=[o[0] for o in outs],
        in_specs=[vm] * 14 + [hb] * 2,
        out_specs=[o[1] for o in outs],
        scratch_shapes=[
            V((NZ, MB, T, D), BF16), V((NZ, MB, T, D), BF16), V((NZ, MB, NZ, 8, T), F32), V((NZ, MB, NZ, 8, T), F32), V((2, MB, NZ - 1, PACKED, D), BF16),
            V((KEYS, 3 * D), BF16), V((T, D), BF16), V((8, 128), F32),
            V((LOCAL, rows, D), BF16), V((LOCAL, rows, D), BF16), V((LOCAL, ROWS, D), BF16),
            V((LOCAL, ROWS, 128), F32), V((NZ, ROWS, 128), F32),
            V((2, D, CHUNK), BF16), V((2, CHUNK, D), BF16),
            V((2, ROWS, CHUNK), BF16), V((2, ROWS, CHUNK), BF16),
            V((ROWS, D), F32), V((ROWS, D), F32),
            V((NZ, ROWS, D), BF16), V((NZ, ROWS, D), BF16),
            V((NZ, T, D), BF16), V((NZ, T, D), BF16),
            DMA((2, 4 * MB, NZ - 1)), DMA((2, 4 * MB, NZ - 1)), DMA((MB + 1,)), DMA((2, 2)), DMA((2, 2)),
            DMA((2,)), DMA((2, NZ)), DMA((NZ - 1,)), DMA((NZ - 1,)),
        ],
        compiler_params=pltpu.CompilerParams(
            collective_id=1, has_side_effects=True, vmem_limit_bytes=58 << 20
        ),
        name="dispatch",
    )(*operands)


HIDDEN = 4 * CHUNK
PART = HIDDEN // 8
BAND = D // 8
SHARE = 400
EXTRA = 128
TOTAL = 8 * SHARE


def add_low(a, b):
    return (a.astype(F32) + b.astype(F32)).astype(BF16)


def grads_kernel(
    vec, tab, wrt, bb, bi, rp,
    tok, dout, wqkv, wout, qkv, mixed, resid, gg, xr, gp, act, gh, pb, pg, pg0,
    block_o, ig_o, ar_o, kb_o, ki_o, lb_o, li_o, land_o,
    core_b, core_i, st1_b, st1_i, ar_core, ar_z, ar_xy1, ar_xy2, ar_t,
    ggr,
    c_send, c_recv, s1_send, s1_recv, s2_send, s2_recv, r_send, r_recv, g_send, g_recv,
    ac_send, ac_recv, az_send, az_recv, ax_send, ax_recv, zz_send, zz_recv, cc_send, cc_recv,
    l_sem, o_sem, f_sem,
):
    dp = lax.axis_index("dp")
    z = lax.axis_index("expert")
    y, x, c = dp // 4, lax.rem(dp // 2, 2), lax.rem(dp, 2)
    yx = y * 2 + x
    partner = (yx * 2 + (1 - c), z)
    flips = ((y * 2 + (1 - x)), ((1 - y) * 2 + x))
    across = (1 - y) * 2 + (1 - x)

    def remote(src, dst, ssem, rsem, target):
        return pltpu.make_async_remote_copy(
            src_ref=src, dst_ref=dst, send_sem=ssem, recv_sem=rsem, device_id=target, device_id_type=MESH
        )

    barrier = pltpu.get_barrier_semaphore()
    for target in [partner, (flips[0] * 2 + c, z), (flips[1] * 2 + c, z)]:
        pl.semaphore_signal(barrier, inc=1, device_id=target, device_id_type=MESH)
    for d in range(1, NZ):
        pl.semaphore_signal(barrier, inc=1, device_id=(dp, lax.rem(z + d, NZ)), device_id_type=MESH)
    pl.semaphore_wait(barrier, 6)

    def gate_copy(d):
        return remote(gg.at[lax.rem(z + d, NZ)], ggr.at[z], g_send.at[d - 1], g_recv.at[d - 1], (dp, lax.rem(z + d, NZ)))

    for d in range(1, NZ):
        gate_copy(d).start()
    own_gate = pltpu.make_async_copy(gg.at[z], ggr.at[z], l_sem.at[0])
    own_gate.start()

    def home(item, d):
        target = lax.rem(z + d, NZ)
        part = pg.at[target] if item == 0 else pb.at[item - 1, target]
        return remote(
            part, land_o.at[item, z], r_send.at[item, d - 1], r_recv.at[item, d - 1], (dp, target)
        )

    def arrived(item):
        for d in range(1, NZ):
            source = lax.rem(z + NZ - d, NZ)
            ref = land_o.at[item, source]
            remote(ref, ref, r_send.at[item, d - 1], r_recv.at[item, d - 1], (dp, source)).wait_recv()

    def load(quad, sources):
        copies = [pltpu.make_async_copy(ref, quad[i], l_sem.at[1 + i]) for i, ref in enumerate(sources)]
        for copy in copies:
            copy.start()
        for copy in copies:
            copy.wait()

    def load_item(quad, item):
        arrived(item)
        own = pg.at[z] if item == 0 else pb.at[item - 1, z]
        load(quad, [own] + [land_o.at[item, lax.rem(z + d, NZ)] for d in range(1, NZ)])

    def quad_sum(quad):
        parts = [ref[...].astype(F32) for ref in quad]
        return (parts[0] + parts[1]) + (parts[2] + parts[3])

    cores, lands1, lands2, keeps = (core_b, core_i), (st1_b, st1_i), (lb_o, li_o), (kb_o, ki_o)

    def core_copy(kind, e, src):
        return remote(src, cores[kind].at[e], c_send.at[kind, e], c_recv.at[kind, e], partner)

    def hop1(kind, e, slot):
        block = flips[kind] if slot == 0 else across
        return remote(
            cores[kind].at[e, block], lands1[kind].at[e, slot],
            s1_send.at[kind, e, slot], s1_recv.at[kind, e, slot], (flips[kind] * 2 + c, z),
        )

    def hop2(kind, e):
        return remote(
            cores[kind].at[e, flips[1 - kind]], lands2[kind].at[e],
            s2_send.at[kind, e], s2_recv.at[kind, e], (flips[1 - kind] * 2 + c, z),
        )

    def send1(kind, e):
        for slot in (1, 0):
            hop1(kind, e, slot).start()

    def turn(kind, e):
        ref = cores[kind]
        hop1(kind, e, 1).wait_recv()
        ref[e, flips[1 - kind]] = add_low(ref[e, flips[1 - kind]], lands1[kind][e, 1])
        hop2(kind, e).start()
        hop1(kind, e, 0).wait_recv()
        ref[e, yx] = add_low(ref[e, yx], lands1[kind][e, 0])
        keep(kind, e).start()

    def keep(kind, e):
        return pltpu.make_async_copy(cores[kind].at[e, yx], keeps[kind].at[e], f_sem.at[kind, e])

    for item in range(3):
        for d in range(1, NZ):
            home(item, d).start()

    V = pltpu.VMEM
    rows = MB * ROWS

    def attention_grads(one, gqkv_s, nor_s, gat_s, ext):
        def inside(wqkv_s, wout_s, qkv_s, tok_s, dout_s, res_s, gres, gm_s):
            loads = [
                pltpu.make_async_copy(src, dst, o_sem.at[4 + i])
                for i, (src, dst) in enumerate(
                    ((wqkv, wqkv_s), (wout, wout_s))
                )
            ]
            for copy in loads:
                copy.start()
            ext[...] = jnp.zeros_like(ext)
            qkv_s[T:KEYS, :] = jnp.zeros((KEYS - T, 3 * D), BF16)
            for d in range(1, NZ):
                gate_copy(d).wait_send()
                source = lax.rem(z + NZ - d, NZ)
                remote(ggr.at[source], ggr.at[source], g_send.at[d - 1], g_recv.at[d - 1], (dp, source)).wait_recv()
            own_gate.wait()
            for copy in loads:
                copy.wait()

            def image(mb, carry):
                quad = [gqkv_s.at[mb, :, i * D : (i + 1) * D] for i in range(3)] + [gm_s]

                @pl.when(mb == 0)
                def _():
                    load(quad, [pg0.at[p] for p in range(NZ)])

                @pl.when(mb == 1)
                def _():
                    load_item(quad, 0)

                fetches = [
                    pltpu.make_async_copy(src.at[mb], dst, o_sem.at[8 + i])
                    for i, (src, dst) in enumerate(((qkv, qkv_s.at[0:T]), (dout, dout_s), (tok, tok_s), (resid, res_s)))
                ]
                for fetch in fetches:
                    fetch.start()
                gates = jnp.concatenate([ggr[p, mb] for p in range(NZ)], axis=0)
                g = tab[mb] * gates
                probs = rp[mb]
                gl = (probs * (g - jnp.sum(probs * g, axis=0, keepdims=True))).astype(BF16)
                fetches[3].wait()
                n2, r2 = normal(res_s[...])
                inner = (n2 * vec[2:3] + vec[3:4]).astype(BF16)
                wr = dot(gl, inner)
                for p in range(NZ):
                    ext[8 + LOCAL * p : 8 + LOCAL * (p + 1), :] += wr[8 * p : 8 * p + LOCAL]
                gi = quad_sum(quad) + dot(gl, wrt[...], TN)
                ext[5:6, :] += jnp.sum(gi * n2, axis=0, keepdims=True)
                ext[6:7, :] += jnp.sum(gi, axis=0, keepdims=True)
                u = gi * vec[2:3]
                fetches[1].wait()
                grad = dout_s[...].astype(F32) + r2 * (
                    u - jnp.mean(u, -1, keepdims=True) - n2 * jnp.mean(u * n2, -1, keepdims=True)
                )

                @pl.when(mb == 1)
                def _():
                    pltpu.make_async_copy(gres, ig_o.at[0], o_sem.at[12]).wait()

                gres[...] = grad
                low = grad.astype(BF16)
                gat_s[mb] = low
                ext[4:5, :] += jnp.sum(low.astype(F32), axis=0, keepdims=True)
                gm_s[...] = dot(low, wout_s[...], NT).astype(BF16)
                fetches[0].wait()

                def heads(p, carry):
                    at = [pl.ds(pl.multiple_of(i * D + p * 128, 128), 128) for i in range(3)]
                    q, k, v = qkv_s[0:T, at[0]], qkv_s[:, at[1]], qkv_s[:, at[2]]
                    gm = gm_s[:, at[0]]
                    gq = jnp.zeros((T, 128), F32)
                    gk = jnp.zeros((KEYS, 128), F32)
                    gv = jnp.zeros((KEYS, 128), F32)
                    for which in (0, 1):
                        mask = half_mask(which)
                        km = k * mask
                        prob = attention_probs(dot(q, km, NT) * HEAD_DIM ** (-0.5))
                        gpr = dot(gm, v * mask, NT)
                        gs = (prob * (gpr - jnp.sum(prob * gpr, axis=-1, keepdims=True))).astype(BF16)
                        gq = gq + dot(gs, km)
                        gk = gk + dot(gs, q * mask, TN)
                        gv = gv + dot(prob.astype(BF16), gm * mask, TN)
                    gqkv_s[mb, :, at[0]] = (gq * HEAD_DIM ** (-0.5)).astype(BF16)
                    gqkv_s[mb, :, at[1]] = (gk[0:T] * HEAD_DIM ** (-0.5)).astype(BF16)
                    gqkv_s[mb, :, at[2]] = gv[0:T].astype(BF16)
                    return carry

                lax.fori_loop(0, PAIRS, heads, 0)
                for row, i in ((2, 0), (3, 2)):
                    ext[row : row + 1, :] += jnp.sum(
                        gqkv_s[mb, :, i * D : (i + 1) * D].astype(F32), axis=0, keepdims=True
                    )
                gn = dot(gqkv_s[mb], wqkv_s[...], NT)
                fetches[2].wait()
                n1, r1 = normal(tok_s[...].astype(F32))
                nor_s[mb] = (n1 * vec[0:1] + vec[1:2]).astype(BF16)
                ext[0:1, :] += jnp.sum(gn * n1, axis=0, keepdims=True)
                ext[1:2, :] += jnp.sum(gn, axis=0, keepdims=True)
                w = gn * vec[0:1]
                gres[...] += r1 * (
                    w - jnp.mean(w, -1, keepdims=True) - n1 * jnp.mean(w * n1, -1, keepdims=True)
                )
                pltpu.make_async_copy(gres, ig_o.at[mb], o_sem.at[12 + mb]).start()

                @pl.when(mb == 0)
                def _():
                    one(1)

                return carry

            lax.fori_loop(0, MB, image, 0)
            pltpu.make_async_copy(gres, ig_o.at[1], o_sem.at[13]).wait()

        pl.run_scoped(
            inside,
            V((D, 3 * D), BF16), V((D, D), BF16), V((KEYS, 3 * D), BF16), V((T, D), BF16), V((T, D), BF16),
            V((T, D), F32), V((T, D), F32), V((T, D), BF16),
        )

        def shared(a, mix_s):
            mix = pltpu.make_async_copy(mixed, mix_s, o_sem.at[4])
            mix.start()
            for zz in range(NZ):
                @pl.when(z == zz)
                def _():
                    at = 24 + 5 * LOCAL * zz
                    ext[at : at + LOCAL, :] = bb[...]
                    for f in range(4):
                        ext[at + LOCAL * (f + 1) : at + LOCAL * (f + 2), :] = bi[:, f * CHUNK : (f + 1) * CHUNK]
            for i in range(3):
                total = jnp.zeros((D, D), F32)
                for mb in range(MB):
                    total = total + dot(nor_s[mb], gqkv_s[mb, :, i * D : (i + 1) * D], TN)
                a[i * D : (i + 1) * D, :] = total.astype(BF16)
            mix.wait()
            total = jnp.zeros((D, D), F32)
            for mb in range(MB):
                total = total + dot(mix_s[mb], gat_s[mb], TN)
            a[3 * D : 4 * D, :] = total.astype(BF16)
            a[4 * D : TOTAL, :] = ext[...].astype(BF16)

            def share(side, zz):
                return pl.ds(pl.multiple_of((side * NZ + zz) * SHARE, 16), SHARE)

            def to_core(zz):
                return remote(a.at[share(1 - c, zz)], ar_core.at[zz], ac_send.at[zz], ac_recv.at[zz], partner)

            for zz in range(NZ):
                to_core(zz).start()
            for kind in (0, 1):
                turn(kind, 0)

            def along(flow, zz, slot):
                return remote(
                    a.at[share(c, zz)], ar_z.at[flow, slot], az_send.at[flow, slot], az_recv.at[flow, slot],
                    (dp, z - 1 if flow == 0 else z + 1),
                )

            for j in range(NZ):
                zz = j
                to_core(zz).wait_recv()
                a[share(c, zz), :] = add_low(a[share(c, zz), :], ar_core[zz])
            for j in range(NZ - 1):
                @pl.when(z == NZ - 1)
                def _():
                    along(0, j, j).start()

                @pl.when(z == 0)
                def _():
                    along(1, NZ - 1 - j, NZ - 2 - j).start()

            def sum_one(flow, dest, at):
                slot = dest if flow == 0 else dest - 1

                @pl.when(z == at)
                def _():
                    along(flow, dest, slot).wait_recv()
                    a[share(c, dest), :] = add_low(a[share(c, dest), :], ar_z[flow, slot])
                    if at != dest:
                        along(flow, dest, slot).start()

            one(2)
            for step, order in enumerate((
                ((0, 0, 2), (1, 3, 1)),
                ((0, 1, 2), (1, 3, 2), (1, 2, 1), (0, 0, 1)),
                ((0, 2, 2), (1, 2, 2), (1, 1, 1), (0, 1, 1), (0, 0, 0), (1, 3, 3)),
            )):
                for flow, dest, at in order:
                    sum_one(flow, dest, at)
                if step == 1:
                    for kind in (0, 1):
                        turn(kind, 1)

            halves = (slice(0, 208), slice(208, SHARE))

            def cross(stage_no, half, src):
                dest = (ar_xy1, ar_xy2)[stage_no].at[halves[half]]
                way = half if stage_no == 0 else 1 - half
                return remote(
                    src, dest, ax_send.at[stage_no, half], ax_recv.at[stage_no, half], (flips[way] * 2 + c, z)
                )

            def mine(half):
                start_row = 0 if half == 0 else 208
                size = 208 if half == 0 else SHARE - 208
                return pl.ds(pl.multiple_of((c * NZ + z) * SHARE + start_row, 16), size)

            for half in (0, 1):
                cross(0, half, a.at[mine(half)]).start()
            for half in (0, 1):
                cross(0, half, a.at[mine(half)]).wait_recv()
                ar_t[halves[half], :] = add_low(a[mine(half), :], ar_xy1[halves[half], :])
                cross(1, half, ar_t.at[halves[half]]).start()
            one(3)
            for half in (0, 1):
                cross(1, half, ar_t.at[halves[half]]).wait()
                ar_t[halves[half], :] = add_low(ar_t[halves[half], :], ar_xy2[halves[half], :])
                cross(0, half, a.at[mine(half)]).wait_send()
            for zz in range(NZ):
                to_core(zz).wait_send()
                for flow in (0, 1):
                    slot = zz if flow == 0 else zz - 1
                    if 0 <= slot < NZ - 1:
                        goes = (z > zz) if flow == 0 else (z < zz)

                        @pl.when(goes)
                        def _():
                            along(flow, zz, slot).wait_send()

        pl.run_scoped(shared, V((TOTAL, D), BF16), V((MB, T, D), BF16))

    def body(wg_b, wg_i, act_s, gh_s, x_s, gp_s, xp):
        def fetch(e, which):
            pairs = ((act, act_s), (gp, gp_s), (xr, x_s), (gh, gh_s))
            return [
                pltpu.make_async_copy(pairs[i][0].at[e], pairs[i][1], o_sem.at[i]) for i in which
            ]

        def pull(e, which):
            for copy in fetch(e, which):
                copy.start()

        def ready(e, which):
            for copy in fetch(e, which):
                copy.wait()

        pull(0, (0, 1, 2, 3))

        def one(e):
            def back_block(k, side):
                at = pl.ds(pl.multiple_of((2 * k + side) * PART, 128), PART)
                return dot(act_s[:, at], gp_s[...], TN)

            ready(e, (0, 1))

            if e > 0:
                core_copy(0, e - 1, wg_b).wait_send()

            def other_b(k, carry):
                wg_b[k] = back_block(k, 1 - c).astype(BF16)
                return carry

            lax.fori_loop(0, 4, other_b, 0)
            core_copy(0, e, wg_b).start()
            ready(e, (2, 3))
            for side in (0, 1):
                for k in range(4):
                    band = (2 * k + side) * BAND
                    xp[side, :, k * BAND : (k + 1) * BAND] = x_s[:, band : band + BAND]

            if e > 0:
                core_copy(1, e - 1, wg_i).wait_send()

            def other_i(f, carry):
                at = pl.ds(pl.multiple_of(f * CHUNK, 128), CHUNK)
                grad = dot(xp[1 - c], gh_s[:, at], TN).astype(BF16)
                for k in range(4):
                    wg_i[k, :, at] = grad[k * BAND : (k + 1) * BAND]
                return carry

            lax.fori_loop(0, 4, other_i, 0)
            core_copy(1, e, wg_i).start()
            core_copy(0, e, wg_b).wait_recv()

            def own_b(k, carry):
                core_b[e, k] = (core_b[e, k].astype(F32) + back_block(k, c)).astype(BF16)
                return carry

            lax.fori_loop(0, 4, own_b, 0)

            send1(0, e)
            if e < LOCAL - 1:
                pull(e + 1, (0, 1))

            core_copy(1, e, wg_i).wait_recv()

            def own_i(f, carry):
                at = pl.ds(pl.multiple_of(f * CHUNK, 128), CHUNK)
                grad = dot(xp[c], gh_s[:, at], TN)
                for k in range(4):
                    core_i[e, k, :, at] = (
                        core_i[e, k, :, at].astype(F32) + grad[k * BAND : (k + 1) * BAND]
                    ).astype(BF16)
                return carry

            lax.fori_loop(0, 4, own_i, 0)

            send1(1, e)
            if e < LOCAL - 1:
                pull(e + 1, (2, 3))

        one(0)
        pl.run_scoped(
            functools.partial(attention_grads, one),
            V((MB, T, 3 * D), BF16), V((MB, T, D), BF16), V((MB, T, D), BF16), V((EXTRA, D), F32),
        )
        core_copy(0, LOCAL - 1, wg_b).wait_send()
        core_copy(1, LOCAL - 1, wg_i).wait_send()

    pl.run_scoped(
        body,
        V((4, PART, D), BF16), V((4, BAND, HIDDEN), BF16), V((rows, HIDDEN), BF16), V((rows, HIDDEN), BF16),
        V((rows, D), BF16), V((rows, D), BF16), V((2, rows, D // 2), BF16),
    )

    def place(zz):
        return ar_o.at[pl.ds(pl.multiple_of((c * NZ + zz) * SHARE, 16), SHARE)]

    own_share = pltpu.make_async_copy(ar_t, place(z), l_sem.at[6])
    own_share.start()

    def spread(up, h):
        source = z - h if up else z + h
        index = (0 if up else 1, h)
        return remote(
            ar_t if h == 0 else place(source), place(source), zz_send.at[index], zz_recv.at[index],
            (dp, z + 1 if up else z - 1),
        )

    def leaves(up, h):
        return jnp.logical_and(z - h >= 0, z + 1 < NZ) if up else jnp.logical_and(z + h < NZ, z >= 1)

    def to_partner(src, k, zz):
        return remote(src, place(zz), cc_send.at[k], cc_recv.at[k], partner)

    for up in (True, False):
        @pl.when(leaves(up, 0))
        def _():
            spread(up, 0).start()

    to_partner(ar_t, 0, z).start()
    for mb in range(MB):
        def image_out(base, quad_s, low):
            quad = [quad_s.at[i] for i in range(NZ)]
            fetch = pltpu.make_async_copy(resid.at[mb], base, l_sem.at[5])
            fetch.start()
            load_item(quad, 1 + mb)
            fetch.wait()
            low[...] = (base[...] + quad_sum(quad)).astype(BF16)
            store = pltpu.make_async_copy(low, block_o.at[mb], l_sem.at[7])
            store.start()
            store.wait()

        pl.run_scoped(image_out, V((T, D), F32), V((NZ, T, D), BF16), V((T, D), BF16))
    for h in range(NZ - 1):
        for up in (True, False):
            source = z - h - 1 if up else z + h + 1

            @pl.when((z - h - 1 >= 0) if up else (z + h + 1 < NZ))
            def _():
                index = (0 if up else 1, h)
                remote(
                    place(source), place(source), zz_send.at[index], zz_recv.at[index],
                    (dp, z - 1 if up else z + 1),
                ).wait_recv()
                k = lax.rem(source - z + NZ, NZ)
                to_partner(place(source), k, source).start()

            if h + 1 < NZ - 1:
                @pl.when(leaves(up, h + 1))
                def _():
                    spread(up, h + 1).start()
        if h < 2:
            for kind in (0, 1):
                turn(kind, 2 + h)
    own_share.wait()
    for k in range(NZ):
        zz = lax.rem(z + k, NZ)
        src = ar_t if k == 0 else place(zz)
        to_partner(src, k, zz).wait_send()
        other = ar_o.at[pl.ds(pl.multiple_of(((1 - c) * NZ + zz) * SHARE, 16), SHARE)]
        remote(other, other, cc_send.at[k], cc_recv.at[k], partner).wait_recv()
    for h in range(NZ - 1):
        for up in (True, False):
            @pl.when(leaves(up, h))
            def _():
                spread(up, h).wait_send()
    for item in range(3):
        for d in range(1, NZ):
            home(item, d).wait_send()
    for kind in (0, 1):
        for e in range(LOCAL):
            for slot in (0, 1):
                hop1(kind, e, slot).wait_send()
            hop2(kind, e).wait()
            keep(kind, e).wait()


def grads_call(*operands):
    vm = pl.BlockSpec(memory_space=pltpu.VMEM)
    hb = pl.BlockSpec(memory_space=pl.ANY)
    S = jax.ShapeDtypeStruct
    V = pltpu.VMEM
    DMA = pltpu.SemaphoreType.DMA
    outs = [
        (S((MB, T, D), BF16), hb),
        (S((MB, T, D), F32), hb),
        (S((TOTAL, D), BF16), hb),
        (S((LOCAL, PART, D), BF16), hb),
        (S((LOCAL, BAND, HIDDEN), BF16), hb),
        (S((LOCAL, PART, D), BF16), hb),
        (S((LOCAL, BAND, HIDDEN), BF16), hb),
        (S((3, NZ, T, D), BF16), hb),
    ]
    return pl.pallas_call(
        grads_kernel,
        out_shape=[o[0] for o in outs],
        in_specs=[vm] * 6 + [hb] * 15,
        out_specs=[o[1] for o in outs],
        scratch_shapes=[
            V((LOCAL, 4, PART, D), BF16), V((LOCAL, 4, BAND, HIDDEN), BF16),
            V((LOCAL, 2, PART, D), BF16), V((LOCAL, 2, BAND, HIDDEN), BF16),
            V((NZ, SHARE, D), BF16), V((2, NZ - 1, SHARE, D), BF16),
            V((SHARE, D), BF16), V((SHARE, D), BF16), V((SHARE, D), BF16),
            V((NZ, MB, 8, T), F32),
            DMA((2, LOCAL)), DMA((2, LOCAL)), DMA((2, LOCAL, 2)), DMA((2, LOCAL, 2)), DMA((2, LOCAL)), DMA((2, LOCAL)),
            DMA((3, NZ - 1)), DMA((3, NZ - 1)), DMA((NZ - 1,)), DMA((NZ - 1,)),
            DMA((NZ,)), DMA((NZ,)), DMA((2, NZ - 1)), DMA((2, NZ - 1)), DMA((2, 2)), DMA((2, 2)),
            DMA((2, NZ - 1)), DMA((2, NZ - 1)), DMA((NZ,)), DMA((NZ,)),
            DMA((8,)), DMA((14,)), DMA((2, LOCAL)),
        ],
        compiler_params=pltpu.CompilerParams(
            collective_id=2, has_side_effects=True, vmem_limit_bytes=63 << 20
        ),
        name="grads",
    )(*operands)


def finish_kernel(
    ar, kb, ki, lb, li, block, ig,
    block_o, ig_o, g1_o, s1_o, qkv_o, qv_o, wout_o, bout_o, g2_o, s2_o, route_o, wi_o, bi_o, wb_o, bb_o,
    ar_s, kb_s, ki_s, lb_s, li_s, block_s, ig_s, wide, narrow, out_i, out_b, tall,
    in_sem, out_sem,
):
    dp = lax.axis_index("dp")
    z = lax.axis_index("expert")

    def fetch(src, dst, i):
        copy = pltpu.make_async_copy(src, dst, in_sem.at[i])
        copy.start()
        return copy

    back = [(fetch(kb.at[e], kb_s.at[e], e), fetch(lb.at[e], lb_s.at[e], 4 + e)) for e in range(LOCAL)]
    ahead = [(fetch(ki.at[e], ki_s.at[e], 8 + e), fetch(li.at[e], li_s.at[e], 12 + e)) for e in range(LOCAL)]
    dense = [
        fetch(ar.at[i * D : (i + 1) * D], ar_s.at[i * D : (i + 1) * D], 16 + i) for i in range(4)
    ]
    few = fetch(ar.at[4 * D : TOTAL], ar_s.at[4 * D : TOTAL], 20)
    rows_in = (fetch(block, block_s, 21), fetch(ig, ig_s, 22))
    sent = []

    def send(src, dst):
        copy = pltpu.make_async_copy(src, dst, out_sem.at[len(sent)])
        copy.start()
        sent.append(copy)

    for pairs, kept, landed, out, dst in ((back, kb_s, lb_s, out_b, wb_o), (ahead, ki_s, li_s, out_i, wi_o)):
        for e in range(LOCAL):
            for copy in pairs[e]:
                copy.wait()
            out[e] = kept[e].astype(F32) + landed[e].astype(F32)
            send(out.at[e], dst.at[e])
    for i in range(4):
        dense[i].wait()
        part = ar_s[i * D : (i + 1) * D, :].astype(F32)
        if i < 3:
            wide[i] = part
            send(wide.at[i], qkv_o.at[:, i * D : (i + 1) * D])
        else:
            narrow[...] = part
            send(narrow, wout_o)
    few.wait()
    low = ar_s[4 * D : TOTAL, :]
    ext = low.astype(F32)
    for row, ref in ((0, g1_o), (1, s1_o), (4, bout_o), (5, g2_o), (6, s2_o)):
        ref[...] = ext[row]
    qv_o[...] = ext[2:4]
    route_o[...] = ext[8 : 8 + NZ * LOCAL]

    def pick(first):
        at = lax.broadcasted_iota(jnp.int32, (8, EXTRA), 0) + first
        return dot((at == lax.broadcasted_iota(jnp.int32, (8, EXTRA), 1)).astype(F32).astype(BF16), low)

    base = 24 + 5 * LOCAL * z
    column = lax.broadcasted_iota(jnp.int32, (D, BAND), 1) + dp * BAND
    chosen = (column == lax.broadcasted_iota(jnp.int32, (D, BAND), 0)).astype(F32).astype(BF16)
    bb_o[...] = dot(pick(base).astype(BF16), chosen)[:LOCAL]
    rows = pick(base + LOCAL * (dp // 2 + 1))
    bi_o[...] = jnp.where(lax.rem(dp, 2) == 0, rows[:, :PART], rows[:, PART:])[:LOCAL]
    for copy in rows_in:
        copy.wait()
    for mb in range(MB):
        at = slice(mb * SEQ, (mb + 1) * SEQ)
        tall[at, :] = block_s[mb].astype(F32)[:SEQ]
        ig_o[at, :] = ig_s[mb, :SEQ, :]
    block_o[...] = tall[0 : MB * SEQ, :].astype(BF16)
    for copy in sent:
        copy.wait()


def finish_call(*operands):
    vm = pl.BlockSpec(memory_space=pltpu.VMEM)
    hb = pl.BlockSpec(memory_space=pl.ANY)
    S = jax.ShapeDtypeStruct
    V = pltpu.VMEM
    rows = MB * SEQ
    vector = (S((D,), F32), vm)
    outs = [
        (S((rows, D), BF16), vm),
        (S((rows, D), F32), vm),
        vector,
        vector,
        (S((D, 3 * D), F32), hb),
        (S((2, D), F32), vm),
        (S((D, D), F32), hb),
        vector,
        vector,
        vector,
        (S((NZ * LOCAL, D), F32), vm),
        (S((LOCAL, BAND, HIDDEN), F32), hb),
        (S((LOCAL, PART), F32), vm),
        (S((LOCAL, PART, D), F32), hb),
        (S((LOCAL, BAND), F32), vm),
    ]
    return pl.pallas_call(
        finish_kernel,
        out_shape=[o[0] for o in outs],
        in_specs=[hb] * 7,
        out_specs=[o[1] for o in outs],
        scratch_shapes=[
            V((TOTAL, D), BF16),
            V((LOCAL, PART, D), BF16), V((LOCAL, BAND, HIDDEN), BF16), V((LOCAL, PART, D), BF16), V((LOCAL, BAND, HIDDEN), BF16),
            V((MB, T, D), BF16), V((MB, T, D), F32), V((3, D, D), F32), V((D, D), F32),
            V((LOCAL, BAND, HIDDEN), F32), V((LOCAL, PART, D), F32), V((400, D), F32),
            pltpu.SemaphoreType.DMA((23,)), pltpu.SemaphoreType.DMA((12,)),
        ],
        compiler_params=pltpu.CompilerParams(vmem_limit_bytes=58 << 20),
        name="finish",
    )(*operands)

def fast_body(
    tokens, routes, gain_one, shift_one, w_qkv, qv_bias, w_out, out_bias, gain_two, shift_two,
    w_route, w_in, b_in, w_back, b_back, d_out,
):
    wrt = jnp.pad(w_route.T.reshape(NZ, LOCAL, D), ((0, 0), (0, 8 - LOCAL), (0, 0))).reshape(32, D)
    (vec, tab, tw, qkv, mixed, resid, rp, gg, bb, bi, dw, xr, gp, act, gh, pb, pg, pg0) = dispatch_call(
        tokens, d_out, routes, gain_one, shift_one, gain_two, shift_two, out_bias, qv_bias,
        w_qkv, w_out, wrt, b_in, b_back, w_in, w_back,
    )
    block, ig, ar, kb, ki, lb, li, _ = grads_call(
        vec, tab, wrt, bb, bi, rp, tw, dw, w_qkv, w_out, qkv, mixed, resid, gg, xr, gp, act, gh, pb, pg, pg0
    )
    out = list(finish_call(ar, kb, ki, lb, li, block, ig))
    out[10] = out[10].T
    return tuple(out)


def solution(mesh):
    fast = mesh.shape["dp"] == 8 and mesh.shape["expert"] == NZ
    return jax.shard_map(
        fast_body if fast else general_body,
        mesh=mesh,
        in_specs=(
            P(("dp", "expert"), None),
            P(("dp", "expert"), None),
            P(),
            P(),
            P(),
            P(),
            P(),
            P(),
            P(),
            P(),
            P(),
            P("expert", None, None),
            P("expert", None),
            P("expert", None, None),
            P("expert", None),
            P(("dp", "expert"), None),
        ),
        out_specs=(
            P(("dp", "expert"), None),
            P(("dp", "expert"), None),
            P(),
            P(),
            P(),
            P(),
            P(),
            P(),
            P(),
            P(),
            P(),
            P("expert", "dp", None),
            P("expert", "dp"),
            P("expert", "dp", None),
            P("expert", "dp"),
        ),
        check_vma=False,
    )
```

```python
import functools

import jax
import jax.numpy as jnp
from jax import lax
from jax.experimental import pallas as pl
from jax.experimental.pallas import tpu as pltpu
from jax.sharding import PartitionSpec as P

HEADS = 12
HEAD_DIM = 64
SEQ = 197
TOP = 2
MB = 2
ROWS_MB = 197
D = 768


HIGH = lax.Precision.HIGHEST
EPSILON = 1e-06


def layer_norm(value, gain, shift):
    center = value - jnp.mean(value, axis=-1, keepdims=True)
    spread = jnp.mean(center * center, axis=-1, keepdims=True)
    return center * lax.rsqrt(spread + EPSILON) * gain + shift


def route_soft(logits):
    return jax.nn.softmax(logits, axis=-1)


def general_body(
    tokens,
    routes,
    gain_one,
    shift_one,
    w_qkv,
    qv_bias,
    w_out,
    out_bias,
    gain_two,
    shift_two,
    w_route,
    w_in,
    b_in,
    w_back,
    b_back,
    d_out,
):
    groups = lax.axis_size("expert")
    local = w_in.shape[0]
    experts = groups * local
    width = tokens.shape[1]
    rows = ROWS_MB
    cap = 5 * rows * TOP // (3 * experts)
    images = rows // SEQ
    scale = HEAD_DIM ** (-0.5)
    expert_ids = jnp.arange(experts, dtype=jnp.int32)
    w_route_wide = w_route.astype(jnp.float32)
    acc_gain_one = jnp.zeros_like(gain_one)
    acc_shift_one = jnp.zeros_like(shift_one)
    acc_qkv = jnp.zeros(w_qkv.shape, jnp.float32)
    acc_qv = jnp.zeros_like(qv_bias)
    acc_out = jnp.zeros(w_out.shape, jnp.float32)
    acc_out_bias = jnp.zeros_like(out_bias)
    acc_gain_two = jnp.zeros_like(gain_two)
    acc_shift_two = jnp.zeros_like(shift_two)
    acc_route = jnp.zeros(w_route.shape, jnp.float32)
    acc_expert = None
    outputs = []
    input_grads = []
    for part in range(MB):
        x = tokens[part * rows : (part + 1) * rows].astype(jnp.float32)
        route = routes[part * rows : (part + 1) * rows]
        cotan = d_out[part * rows : (part + 1) * rows].astype(jnp.float32)
        normed, ln_one_pull = jax.vjp(layer_norm, x, gain_one, shift_one)
        normed_low = normed.astype(jnp.bfloat16)
        bias = jnp.concatenate([qv_bias[0], jnp.zeros_like(qv_bias[0]), qv_bias[1]])
        qkv = (jnp.dot(normed_low, w_qkv, preferred_element_type=jnp.float32) + bias).astype(
            jnp.bfloat16
        )
        query = qkv[:, :width].reshape(images, SEQ, HEADS, HEAD_DIM)
        keys = qkv[:, width : 2 * width].reshape(images, SEQ, HEADS, HEAD_DIM)
        values = qkv[:, 2 * width :].reshape(images, SEQ, HEADS, HEAD_DIM)
        scores = (
            jnp.einsum("ishd,ithd->ihst", query, keys, preferred_element_type=jnp.float32) * scale
        )
        log_total = jax.nn.logsumexp(scores, axis=-1, keepdims=True)
        probs_low = jnp.exp(scores - log_total).astype(jnp.bfloat16)
        mixed = jnp.einsum("ihst,ithd->ishd", probs_low, values, preferred_element_type=jnp.float32)
        mixed = mixed.reshape(rows, width).astype(jnp.bfloat16)
        resid = x + jnp.dot(mixed, w_out, preferred_element_type=jnp.float32) + out_bias
        inner, ln_two_pull = jax.vjp(layer_norm, resid, gain_two, shift_two)
        inner_low = inner.astype(jnp.bfloat16)
        logits = jnp.dot(inner_low, w_route, preferred_element_type=jnp.float32)
        route_probs, soft_pull = jax.vjp(route_soft, logits)
        choose = (route[:, :, None] == expert_ids[None, None, :]).astype(jnp.float32)
        gates = jnp.einsum("rke,re->rk", choose, route_probs, precision=HIGH)
        flat_ids = route.reshape(-1)
        table = (flat_ids[:, None] == expert_ids[None, :]).astype(jnp.int32)
        order = jnp.arange(rows * TOP, dtype=jnp.int32)
        earlier = (order[None, :] < order[:, None]).astype(jnp.bfloat16)
        before = jnp.dot(
            earlier, table.astype(jnp.bfloat16), preferred_element_type=jnp.float32
        ).astype(jnp.int32)
        slot = jnp.sum(before * table, axis=1)
        dest = flat_ids * cap + slot
        sending = (
            jnp.zeros((experts * cap, width), jnp.bfloat16)
            .at[dest]
            .set(jnp.repeat(inner_low, TOP, axis=0))
        )
        sending = sending.reshape(groups, local, cap, width)
        received = lax.all_to_all(sending, "expert", split_axis=0, concat_axis=0, tiled=True)
        hidden = jnp.einsum("secd,edf->secf", received, w_in, preferred_element_type=jnp.float32)
        hidden = hidden + b_in[None, :, None, :]
        active = jax.nn.gelu(hidden).astype(jnp.bfloat16)
        result = jnp.einsum("secf,efd->secd", active, w_back, preferred_element_type=jnp.float32)
        result = (result + b_back[None, :, None, :]).astype(jnp.bfloat16)
        returned = lax.all_to_all(result, "expert", split_axis=0, concat_axis=0, tiled=True)
        returned, kept_rows, kept_hidden = (returned, received, hidden)
        picked = (
            returned.reshape(experts * cap, width)[dest]
            .reshape(rows, TOP, width)
            .astype(jnp.float32)
        )
        block = resid + jnp.sum(gates[:, :, None] * picked, axis=1)
        outputs.append(block.astype(jnp.bfloat16))
        grad_gate = jnp.sum(picked * cotan[:, None, :], axis=2)
        grad_picked = (gates[:, :, None] * cotan[:, None, :]).astype(jnp.bfloat16)
        grad_send = (
            jnp.zeros((experts * cap, width), jnp.bfloat16)
            .at[dest]
            .set(grad_picked.reshape(rows * TOP, width))
        )
        grad_send = grad_send.reshape(groups, local, cap, width)
        grad_recv = lax.all_to_all(grad_send, "expert", split_axis=0, concat_axis=0, tiled=True)
        active, gelu_pull = jax.vjp(jax.nn.gelu, kept_hidden)
        active_low = active.astype(jnp.bfloat16)
        grad_active = jnp.einsum(
            "secd,efd->secf", grad_recv, w_back, preferred_element_type=jnp.float32
        )
        grad_hidden = gelu_pull(grad_active)[0].astype(jnp.bfloat16)
        step_w_back = jnp.einsum(
            "secf,secd->efd", active_low, grad_recv, preferred_element_type=jnp.float32
        )
        step_b_back = jnp.sum(grad_recv.astype(jnp.float32), axis=(0, 2))
        step_w_in = jnp.einsum(
            "secd,secf->edf", kept_rows, grad_hidden, preferred_element_type=jnp.float32
        )
        step_b_in = jnp.sum(grad_hidden.astype(jnp.float32), axis=(0, 2))
        grad_rows = jnp.einsum(
            "secf,edf->secd", grad_hidden, w_in, preferred_element_type=jnp.float32
        )
        grad_rows = grad_rows.astype(jnp.bfloat16)
        grad_back = lax.all_to_all(grad_rows, "expert", split_axis=0, concat_axis=0, tiled=True)
        shares = (step_w_in, step_b_in, step_w_back, step_b_back)
        if acc_expert is None:
            acc_expert = shares
        else:
            acc_expert = tuple((a + b for a, b in zip(acc_expert, shares)))
        grad_inner = jnp.sum(
            grad_back.reshape(experts * cap, width)[dest]
            .reshape(rows, TOP, width)
            .astype(jnp.float32),
            axis=1,
        )
        grad_probs = jnp.einsum("rk,rke->re", grad_gate, choose, precision=HIGH)
        grad_logits = soft_pull(grad_probs)[0]
        acc_route = acc_route + jnp.einsum(
            "rd,re->de", inner_low.astype(jnp.float32), grad_logits, precision=HIGH
        )
        grad_inner = grad_inner + jnp.einsum("re,de->rd", grad_logits, w_route_wide, precision=HIGH)
        grad_ln_two, grad_gain_two, grad_shift_two = ln_two_pull(grad_inner)
        acc_gain_two = acc_gain_two + grad_gain_two
        acc_shift_two = acc_shift_two + grad_shift_two
        grad_resid = cotan + grad_ln_two
        grad_att = grad_resid.astype(jnp.bfloat16)
        acc_out = acc_out + jnp.einsum(
            "rd,re->de", mixed, grad_att, preferred_element_type=jnp.float32
        )
        acc_out_bias = acc_out_bias + jnp.sum(grad_att.astype(jnp.float32), axis=0)
        grad_mixed = jnp.einsum("re,de->rd", grad_att, w_out, preferred_element_type=jnp.float32)
        grad_mixed = grad_mixed.astype(jnp.bfloat16).reshape(images, SEQ, HEADS, HEAD_DIM)
        again = (
            jnp.einsum("ishd,ithd->ihst", query, keys, preferred_element_type=jnp.float32) * scale
        )
        probs = jnp.exp(again - log_total)
        grad_probs_att = jnp.einsum(
            "ishd,ithd->ihst", grad_mixed, values, preferred_element_type=jnp.float32
        )
        row_total = jnp.sum(probs * grad_probs_att, axis=-1, keepdims=True)
        grad_scores = (probs * (grad_probs_att - row_total)).astype(jnp.bfloat16)
        grad_query = (
            jnp.einsum("ihst,ithd->ishd", grad_scores, keys, preferred_element_type=jnp.float32)
            * scale
        )
        grad_keys = (
            jnp.einsum("ihst,ishd->ithd", grad_scores, query, preferred_element_type=jnp.float32)
            * scale
        )
        grad_values = jnp.einsum(
            "ihst,ishd->ithd",
            probs.astype(jnp.bfloat16),
            grad_mixed,
            preferred_element_type=jnp.float32,
        )
        grad_qkv = jnp.concatenate(
            [
                grad_query.reshape(rows, width),
                grad_keys.reshape(rows, width),
                grad_values.reshape(rows, width),
            ],
            axis=1,
        ).astype(jnp.bfloat16)
        acc_qkv = acc_qkv + jnp.einsum(
            "rd,re->de", normed_low, grad_qkv, preferred_element_type=jnp.float32
        )
        column_sums = jnp.sum(grad_qkv.astype(jnp.float32), axis=0)
        acc_qv = acc_qv + jnp.stack([column_sums[:width], column_sums[2 * width :]])
        grad_normed = jnp.einsum("re,de->rd", grad_qkv, w_qkv, preferred_element_type=jnp.float32)
        grad_ln_one, grad_gain_one, grad_shift_one = ln_one_pull(grad_normed)
        acc_gain_one = acc_gain_one + grad_gain_one
        acc_shift_one = acc_shift_one + grad_shift_one
        input_grads.append(grad_resid + grad_ln_one)
    expert_grads = (
        lax.psum_scatter(
            acc_expert[0].astype(jnp.bfloat16), "dp", scatter_dimension=1, tiled=True
        ).astype(jnp.float32),
        lax.psum_scatter(
            acc_expert[1].astype(jnp.bfloat16), "dp", scatter_dimension=1, tiled=True
        ).astype(jnp.float32),
        lax.psum_scatter(
            acc_expert[2].astype(jnp.bfloat16), "dp", scatter_dimension=1, tiled=True
        ).astype(jnp.float32),
        lax.psum_scatter(
            acc_expert[3].astype(jnp.bfloat16), "dp", scatter_dimension=1, tiled=True
        ).astype(jnp.float32),
    )
    shared = (
        acc_gain_one,
        acc_shift_one,
        acc_qkv,
        acc_qv,
        acc_out,
        acc_out_bias,
        acc_gain_two,
        acc_shift_two,
        acc_route,
    )
    shared = lax.psum(
        (
            shared[0],
            shared[1],
            shared[2],
            shared[3],
            shared[4],
            shared[5],
            shared[6],
            shared[7],
            shared[8],
        ),
        ("dp", "expert"),
    )
    return (
        jnp.concatenate(outputs, axis=0),
        jnp.concatenate(input_grads, axis=0),
        shared[0],
        shared[1],
        shared[2],
        shared[3],
        shared[4],
        shared[5],
        shared[6],
        shared[7],
        shared[8],
        expert_grads[0],
        expert_grads[1],
        expert_grads[2],
        expert_grads[3],
    )


F32, BF16 = jnp.float32, jnp.bfloat16
NZ = 4
LOCAL = 4
PAIRS = HEADS // 2
T = 208
KEYS = 256
CAP = 41
CAP_ROWS = 48
PACKED = 176
ROWS = NZ * CAP_ROWS
CHUNK = 768
PIECE = 1536
PIECES = 4 * CHUNK // PIECE
MESH = pl.DeviceIdType.MESH
NT = (((1,), (1,)), ((), ()))
TN = (((0,), (0,)), ((), ()))


def dot(a, b, dims=(((1,), (0,)), ((), ()))):
    return lax.dot_general(a, b, dims, preferred_element_type=F32)


def normal(value):
    center = value - jnp.mean(value, axis=-1, keepdims=True)
    scale = lax.rsqrt(jnp.mean(center * center, axis=-1, keepdims=True) + EPSILON)
    return center * scale, scale


def half_mask(which):
    lane = lax.broadcasted_iota(jnp.int32, (1, 128), 1)
    return ((lane < 64) if which == 0 else (lane >= 64)).astype(F32).astype(BF16)


def attention_probs(scores):
    key = lax.broadcasted_iota(jnp.int32, scores.shape, 1)
    scores = jnp.where(key < SEQ, scores, -1e30)
    top = jnp.max(scores, axis=-1, keepdims=True)
    raised = jnp.exp(scores - top)
    return raised / jnp.sum(raised, axis=-1, keepdims=True)


def route_softmax(logits, real):
    logits = jnp.where(real, logits, -1e30)
    raised = jnp.exp(logits - jnp.max(logits, axis=0, keepdims=True))
    raised = jnp.where(real, raised, 0.0)
    return raised / jnp.sum(raised, axis=0, keepdims=True)


def pick_matrix(slots):
    index = lax.broadcasted_iota(jnp.int32, (CAP_ROWS, T), 0).astype(F32)
    return jnp.concatenate(
        [(index == slots[e : e + 1, :]).astype(F32) for e in range(LOCAL)], axis=0
    )


def dispatch_kernel(
    tok, dout, routes, v0, v1, v2, v3, v4, qv, wqkv, wout, wrt, b_in, b_back, w_in, w_back,
    vec, tab_o, tw_o, qkv_o, mixed_o, resid_o, rp_o, gg_o, bb_o, bi_o, dw_o, x_o, gp_o, act_o, gh_o, pb_o, pg_o, home_o,
    gi, gd, sl, sg, dense, qkv_s, mixed_s, inner_s, xs, gs, cs, rgs, ggs, wb1, wb2, act_st, gh_st, acc_o, acc_g,
    os_, grs, pb_s, pg_s,
    send_sem, recv_sem, d_sem, w_sem, st_sem, x_sem, p_sem, h_send, h_recv,
):
    dp = lax.axis_index("dp")
    z = lax.axis_index("expert")

    def item_ref(kind, source, mb):
        return (gd, sg, gi, sl)[kind].at[source, mb]

    def copy_of(up, kind, mb, h, source, target, packed):
        index = (0 if up else 1, kind * MB + mb, h)
        dst = item_ref(kind, source, mb)
        src = dst
        if packed:
            src, dst = dense.at[kind // 2, mb, h], dst.at[0:PACKED]
        return pltpu.make_async_remote_copy(
            src_ref=src, dst_ref=dst, send_sem=send_sem.at[index], recv_sem=recv_sem.at[index],
            device_id=(dp, target), device_id_type=MESH,
        )

    def hop(up, kind, mb, h, packed):
        return copy_of(up, kind, mb, h, z - h if up else z + h, z + 1 if up else z - 1, packed)

    def leaves(up, h):
        return jnp.logical_and(z - h >= 0, z + 1 < NZ) if up else jnp.logical_and(z + h < NZ, z >= 1)

    def arrives(up, h):
        return (z - h - 1 >= 0) if up else (z + h + 1 < NZ)

    def to_end(up):
        return (z + 1 == NZ - 1) if up else (z == 1)

    def at_end(up):
        return (z == NZ - 1) if up else (z == 0)

    def each(kind, condition, where, action):
        if kind in (0, 2):
            @pl.when(jnp.logical_and(condition, where))
            def _():
                action(True)

            @pl.when(jnp.logical_and(condition, jnp.logical_not(where)))
            def _():
                action(False)
        else:
            @pl.when(condition)
            def _():
                action(False)

    def start(kind, mb, h):
        for up in (True, False):
            def go(packed):
                if packed:
                    source = z - h if up else z + h
                    slots = sl[source, mb, NZ - 1 if up else 0]
                    row = lax.broadcasted_iota(jnp.int32, (PACKED, T), 0)
                    owner = row // CAP
                    wanted = jnp.full((PACKED, T), -5.0, F32)
                    for e in range(LOCAL):
                        wanted = jnp.where(owner == e, slots[e : e + 1, :], wanted)
                    chosen = (wanted == (row - owner * CAP).astype(F32)).astype(F32).astype(BF16)
                    dense[kind // 2, mb, h] = dot(chosen, item_ref(kind, source, mb)[...]).astype(BF16)
                hop(up, kind, mb, h, packed).start()

            each(kind, leaves(up, h), to_end(up), go)

    def pass_on(kind, mb, h):
        for up in (True, False):
            def take(packed):
                source = z - h - 1 if up else z + h + 1
                copy_of(up, kind, mb, h, source, z - 1 if up else z + 1, packed).wait_recv()

            each(kind, arrives(up, h), at_end(up), take)
        if h + 1 < NZ - 1:
            start(kind, mb, h + 1)

    def weights(n, slot):
        e = lax.rem(n, LOCAL * PIECES) // PIECES
        f = lax.rem(n, PIECES)
        cols = pl.ds(pl.multiple_of(f * PIECE, PIECE), PIECE)
        return (
            pltpu.make_async_copy(w_in.at[e, :, cols], wb1.at[slot], w_sem.at[0, slot]),
            pltpu.make_async_copy(w_back.at[e, cols, :], wb2.at[slot], w_sem.at[1, slot]),
        )

    for copy in weights(0, 0):
        copy.start()
    for ref in (gi, gd):
        for source in range(NZ):
            for mb in range(MB):
                ref[source, mb, PACKED:T, :] = jnp.zeros((T - PACKED, D), BF16)
    for row, ref in enumerate((v0, v1, v2, v3, v4)):
        vec[row : row + 1, :] = ref[...].reshape(1, D)
    vec[5:7, :] = qv[...]
    vec[7:8, :] = jnp.zeros((1, D), F32)
    lane = lax.broadcasted_iota(jnp.int32, (1, 32), 1)
    part = lax.rem(lane, 8)
    expert_of = jnp.where(part < LOCAL, (lane // 8) * LOCAL + part, -7)
    chosen_all = jnp.logical_or(routes[:, 0:1] == expert_of, routes[:, 1:2] == expert_of)
    chosen_all = chosen_all.astype(F32).astype(BF16)
    token = lax.broadcasted_iota(jnp.int32, (MB * SEQ, T), 0)
    column = lax.broadcasted_iota(jnp.int32, (MB * SEQ, T), 1)
    for mb in range(MB):
        here = jnp.logical_and(token == column + mb * SEQ, column < SEQ).astype(F32).astype(BF16)
        ahead = jnp.logical_and(token >= mb * SEQ, token < column + mb * SEQ).astype(F32).astype(BF16)
        table = dot(chosen_all, here, TN)
        tab_o[mb] = table
        slots = jnp.where(table > 0.5, dot(chosen_all, ahead, TN), -1.0)
        for p in range(NZ):
            sl[z, mb, p] = slots[8 * p : 8 * p + 8, :]
        tw_o[mb] = dot(here, tok[...], TN).astype(BF16)
        gd[z, mb] = dot(here, dout[...], TN).astype(BF16)
    barrier = pltpu.get_barrier_semaphore()
    for d in range(1, NZ):
        pl.semaphore_signal(barrier, inc=1, device_id=(dp, lax.rem(z + d, NZ)), device_id_type=MESH)
    pl.semaphore_wait(barrier, NZ - 1)
    start(3, 0, 0)
    start(0, 0, 0)
    start(3, 1, 0)
    own = [pltpu.make_async_copy(gd.at[z, mb], dw_o.at[mb], d_sem.at[mb]) for mb in range(MB)]
    for copy in own:
        copy.start()

    qkv_s[T:KEYS, :] = jnp.zeros((KEYS - T, 3 * D), BF16)
    bb_o[...] = jnp.zeros_like(bb_o)
    bi_o[...] = jnp.zeros_like(bi_o)

    def forward(mb, carry):
        x = tw_o[mb].astype(F32)
        normed = (normal(x)[0] * vec[0:1] + vec[1:2]).astype(BF16)
        for c in range(3):
            cols = slice(c * D, (c + 1) * D)
            part = dot(normed, wqkv[:, cols])
            if c != 1:
                row = 5 if c == 0 else 6
                part = part + vec[row : row + 1]
            qkv_s[0:T, cols] = part.astype(BF16)

        def heads(p, carry):
            at = [pl.ds(pl.multiple_of(c * D + p * 128, 128), 128) for c in range(3)]
            q, k, v = qkv_s[0:T, at[0]], qkv_s[:, at[1]], qkv_s[:, at[2]]
            mixed = jnp.zeros((T, 128), F32)
            for which in (0, 1):
                mask = half_mask(which)
                probs = attention_probs(dot(q, k * mask, NT) * HEAD_DIM ** (-0.5))
                mixed = mixed + dot(probs.astype(BF16), v * mask)
            mixed_s[:, at[0]] = mixed.astype(BF16)
            return carry

        lax.fori_loop(0, PAIRS, heads, 0, unroll=3)
        qkv_o[mb] = qkv_s[0:T, :]
        mixed_o[mb] = mixed_s[...]
        resid = x + dot(mixed_s[...], wout[...]) + vec[4:5]
        resid_o[mb] = resid
        inner = (normal(resid)[0] * vec[2:3] + vec[3:4]).astype(BF16)
        gi[z, mb] = inner
        real = lax.rem(lax.broadcasted_iota(jnp.int32, (32, T), 0), 8) < LOCAL
        probs = route_softmax(dot(wrt[...], inner, NT), real)
        rp_o[mb] = probs
        gates = tab_o[mb] * probs
        for p in range(NZ):
            sg[z, mb, p] = gates[8 * p : 8 * p + 8, :]

        @pl.when(mb == 0)
        def _():
            start(1, 0, 0)
            start(2, 0, 0)

        return carry

    lax.fori_loop(0, MB, forward, 0)
    middle = jnp.logical_and(z > 0, z < NZ - 1)

    @pl.when(jnp.logical_not(middle))
    def _():
        for kind in range(3):
            start(kind, 1, 0)

    for h in range(NZ - 1):
        for kind in (3, 0, 1, 2):
            pass_on(kind, 0, h)
        pass_on(3, 1, h)

    @pl.when(middle)
    def _():
        for kind in range(3):
            start(kind, 1, 0)

    def micro(mb, carry):
        @pl.when(mb == 1)
        def _():
            for kind in range(3):
                pass_on(kind, 1, 2)

        def spread(src, carry):
            pick = pick_matrix(sl[src, mb, z])
            gate = sg[src, mb, z]
            row = lax.broadcasted_iota(jnp.int32, (ROWS, T), 0)
            owner = row // CAP_ROWS
            place = row - owner * CAP_ROWS
            unpack = jnp.logical_and(
                place < CAP, lax.broadcasted_iota(jnp.int32, (ROWS, T), 1) == owner * CAP + place
            ).astype(F32)
            packed = jnp.logical_and(jnp.logical_or(z == 0, z == NZ - 1), src != z)
            low = jnp.where(packed, unpack, pick).astype(BF16)
            rows_x = dot(low, gi[src, mb]).astype(BF16)
            rows_c = dot(low, gd[src, mb])
            at = pl.ds(pl.multiple_of(mb * ROWS + src * CAP_ROWS, 16), CAP_ROWS)
            here = pl.ds(pl.multiple_of(src * CAP_ROWS, 16), CAP_ROWS)
            for e in range(LOCAL):
                part = slice(e * CAP_ROWS, (e + 1) * CAP_ROWS)
                gate_rows = jnp.sum(pick[part] * gate[e : e + 1, :], axis=1, keepdims=True)
                grad = (rows_c[part] * gate_rows).astype(BF16)
                xs[e, at, :] = rows_x[part]
                gs[e, at, :] = grad
                cs[e, here, :] = rows_c[part].astype(BF16)
                rgs[e, here, :] = jnp.broadcast_to(gate_rows, (CAP_ROWS, 128))
                bb_o[e : e + 1, :] += jnp.sum(grad.astype(F32), axis=0, keepdims=True)
            return carry

        lax.fori_loop(0, NZ, spread, 0)
        rows = pl.ds(pl.multiple_of(mb * ROWS, 16), ROWS)

        def expert(e, carry):
            acc_o[...] = jnp.zeros_like(acc_o)
            acc_g[...] = jnp.zeros_like(acc_g)

            def step(f, carry):
                n = (mb * LOCAL + e) * PIECES + f
                slot = lax.rem(n, 2)
                cols = pl.ds(pl.multiple_of(f * PIECE, PIECE), PIECE)

                @pl.when(n + 1 < LOCAL * PIECES * MB)
                def _():
                    for copy in weights(n + 1, 1 - slot):
                        copy.start()

                @pl.when(n >= 2)
                def _():
                    for copy in stores(n - 2, slot):
                        copy.wait()

                for copy in weights(n, slot):
                    copy.wait()
                hid = dot(xs[e, rows, :], wb1[slot]) + b_in[pl.ds(e, 1), cols]
                square = hid * hid
                bend = jnp.tanh(hid * (0.7978845608 + (0.7978845608 * 0.044715) * square))
                half = 0.5 + 0.5 * bend
                act = (hid * half).astype(BF16)
                slope = half + (0.5 * hid) * (1.0 - bend * bend) * (
                    0.7978845608 + (3 * 0.7978845608 * 0.044715) * square
                )

                act_st[slot] = act
                acc_o[...] += dot(act, wb2[slot])
                grad = (dot(gs[e, rows, :], wb2[slot], NT) * slope).astype(BF16)
                gh_st[slot] = grad
                acc_g[...] += dot(grad, wb1[slot], NT)
                bi_o[pl.ds(e, 1), cols] += jnp.sum(grad.astype(F32), axis=0, keepdims=True)
                for copy in stores(n, slot):
                    copy.start()
                return carry

            lax.fori_loop(0, PIECES, step, 0)
            out = (acc_o[...] + b_back[pl.ds(e, 1), :]).astype(BF16).astype(F32)
            gg = jnp.sum(out * cs[e].astype(F32), axis=1, keepdims=True)
            scaled = (out * rgs[e][:, 0:1]).astype(BF16)
            back = acc_g[...].astype(BF16)
            at = pl.ds(pl.multiple_of(e * CAP_ROWS, 16), CAP_ROWS)
            for src in range(NZ):
                part = slice(src * CAP_ROWS, (src + 1) * CAP_ROWS)
                os_[src, at, :] = scaled[part]
                grs[src, at, :] = back[part]
                ggs[src, at, :] = jnp.broadcast_to(gg[part], (CAP_ROWS, 128))

            @pl.when(jnp.logical_and(mb == 1, e == jnp.where(middle, 1, 0)))
            def _():
                for d in range(1, NZ):
                    sent_home(d).start()
                own_home().start()

            @pl.when(jnp.logical_and(mb == 0, e == 0))
            def _():
                for kind in range(3):
                    pass_on(kind, 1, 0)

            @pl.when(jnp.logical_and(mb == 0, e == 2))
            def _():
                for kind in range(3):
                    pass_on(kind, 1, 1)

            return carry

        def stores(n, slot):
            m = n // (LOCAL * PIECES)
            e = lax.rem(n, LOCAL * PIECES) // PIECES
            f = lax.rem(n, PIECES)
            at = (e, pl.ds(pl.multiple_of(m * ROWS, 16), ROWS), pl.ds(pl.multiple_of(f * PIECE, PIECE), PIECE))
            return (
                pltpu.make_async_copy(act_st.at[slot], act_o.at[at], st_sem.at[0, slot]),
                pltpu.make_async_copy(gh_st.at[slot], gh_o.at[at], st_sem.at[1, slot]),
            )

        lax.fori_loop(0, LOCAL, expert, 0)

        @pl.when(mb == 1)
        def _():
            for slot in (0, 1):
                for copy in stores(LOCAL * PIECES * MB - 2 + slot, slot):
                    copy.wait()

        @pl.when(mb == 1)
        def _():
            for src in range(NZ):
                kept(0, src).wait()
            for d in range(1, NZ):
                sent_home(d).wait_send()
            own_home().wait()

        def gather(src, carry):
            pick = pick_matrix(sl[src, mb, z])
            low = pick.astype(BF16)
            pb_s[src] = dot(low, os_[src], TN).astype(BF16)
            pg_s[src] = dot(low, grs[src], TN).astype(BF16)
            kept(mb, src).start()
            for e in range(LOCAL):
                part = slice(e * CAP_ROWS, (e + 1) * CAP_ROWS)
                gg_o[src, mb, e : e + 1, :] = jnp.sum(
                    pick[part] * ggs[src, part, 0:1], axis=0, keepdims=True
                )

            @pl.when(mb == 1)
            def _():
                kept_grad(src).start()

            return carry

        lax.fori_loop(0, NZ, gather, 0)

        @pl.when(mb == 1)
        def _():
            for src in range(NZ):
                kept(1, src).wait()
                kept_grad(src).wait()

        return carry

    def kept(mb, src):
        return pltpu.make_async_copy(pb_s.at[src], pb_o.at[mb, src], p_sem.at[0, src])

    def kept_grad(src):
        return pltpu.make_async_copy(pg_s.at[src], pg_o.at[src], p_sem.at[1, src])

    def sent_home(d):
        target = lax.rem(z + d, NZ)
        return pltpu.make_async_remote_copy(
            src_ref=pg_s.at[target], dst_ref=home_o.at[z], send_sem=h_send.at[d - 1], recv_sem=h_recv.at[d - 1],
            device_id=(dp, target), device_id_type=MESH,
        )

    def own_home():
        return pltpu.make_async_copy(pg_s.at[z], home_o.at[z], d_sem.at[MB])

    gg_o[...] = jnp.zeros_like(gg_o)
    lax.fori_loop(0, MB, micro, 0)
    last = (
        pltpu.make_async_copy(xs, x_o, x_sem.at[0]),
        pltpu.make_async_copy(gs, gp_o, x_sem.at[1]),
    )
    for copy in last:
        copy.start()
    for copy in last:
        copy.wait()
    for d in range(1, NZ):
        source = lax.rem(z + NZ - d, NZ)
        pltpu.make_async_remote_copy(
            src_ref=home_o.at[source], dst_ref=home_o.at[source], send_sem=h_send.at[d - 1],
            recv_sem=h_recv.at[d - 1], device_id=(dp, source), device_id_type=MESH,
        ).wait_recv()
    for copy in own:
        copy.wait()
    for mb in range(MB):
        for kind in range(4):
            for h in range(NZ - 1):
                for up in (True, False):
                    each(
                        kind, leaves(up, h), to_end(up),
                        lambda packed: hop(up, kind, mb, h, packed).wait_send(),
                    )


def dispatch_call(*operands):
    vm = pl.BlockSpec(memory_space=pltpu.VMEM)
    hb = pl.BlockSpec(memory_space=pl.ANY)
    S = jax.ShapeDtypeStruct
    rows = MB * ROWS
    outs = [
        (S((8, D), F32), vm),
        (S((MB, 32, T), F32), vm),
        (S((MB, T, D), BF16), vm),
        (S((MB, T, 3 * D), BF16), vm),
        (S((MB, T, D), BF16), vm),
        (S((MB, T, D), F32), vm),
        (S((MB, 32, T), F32), vm),
        (S((NZ, MB, 8, T), F32), vm),
        (S((LOCAL, D), F32), vm),
        (S((LOCAL, 4 * CHUNK), F32), vm),
        (S((MB, T, D), BF16), hb),
        (S((LOCAL, rows, D), BF16), hb),
        (S((LOCAL, rows, D), BF16), hb),
        (S((LOCAL, rows, 4 * CHUNK), BF16), hb),
        (S((LOCAL, rows, 4 * CHUNK), BF16), hb),
        (S((MB, NZ, T, D), BF16), hb),
        (S((NZ, T, D), BF16), hb),
        (S((NZ, T, D), BF16), hb),
    ]
    V = pltpu.VMEM
    DMA = pltpu.SemaphoreType.DMA
    return pl.pallas_call(
        dispatch_kernel,
        out_shape=[o[0] for o in outs],
        in_specs=[vm] * 14 + [hb] * 2,
        out_specs=[o[1] for o in outs],
        scratch_shapes=[
            V((NZ, MB, T, D), BF16), V((NZ, MB, T, D), BF16), V((NZ, MB, NZ, 8, T), F32), V((NZ, MB, NZ, 8, T), F32), V((2, MB, NZ - 1, PACKED, D), BF16),
            V((KEYS, 3 * D), BF16), V((T, D), BF16), V((8, 128), F32),
            V((LOCAL, rows, D), BF16), V((LOCAL, rows, D), BF16), V((LOCAL, ROWS, D), BF16),
            V((LOCAL, ROWS, 128), F32), V((NZ, ROWS, 128), F32),
            V((2, D, PIECE), BF16), V((2, PIECE, D), BF16),
            V((2, ROWS, PIECE), BF16), V((2, ROWS, PIECE), BF16),
            V((ROWS, D), F32), V((ROWS, D), F32),
            V((NZ, ROWS, D), BF16), V((NZ, ROWS, D), BF16),
            V((NZ, T, D), BF16), V((NZ, T, D), BF16),
            DMA((2, 4 * MB, NZ - 1)), DMA((2, 4 * MB, NZ - 1)), DMA((MB + 1,)), DMA((2, 2)), DMA((2, 2)),
            DMA((2,)), DMA((2, NZ)), DMA((NZ - 1,)), DMA((NZ - 1,)),
        ],
        compiler_params=pltpu.CompilerParams(
            collective_id=1, has_side_effects=True, vmem_limit_bytes=58 << 20
        ),
        name="dispatch",
    )(*operands)


HIDDEN = 4 * CHUNK
PART = HIDDEN // 8
BAND = D // 8
SHARE = 400
EXTRA = 128
TOTAL = 8 * SHARE


def add_low(a, b):
    return (a.astype(F32) + b.astype(F32)).astype(BF16)


def grads_kernel(
    vec, tab, wrt, bb, bi, rp,
    tok, dout, wqkv, wout, qkv, mixed, resid, gg, xr, gp, act, gh, pb, pg, pg0,
    block_o, ig_o, ar_o, kb_o, ki_o, lb_o, li_o, land_o,
    core_b, core_i, st1_b, st1_i, ar_core, ar_z, ar_xy1, ar_xy2, ar_t,
    ggr,
    c_send, c_recv, s1_send, s1_recv, s2_send, s2_recv, r_send, r_recv, g_send, g_recv,
    ac_send, ac_recv, az_send, az_recv, ax_send, ax_recv, zz_send, zz_recv, cc_send, cc_recv,
    l_sem, o_sem, f_sem,
):
    dp = lax.axis_index("dp")
    z = lax.axis_index("expert")
    y, x, c = dp // 4, lax.rem(dp // 2, 2), lax.rem(dp, 2)
    yx = y * 2 + x
    partner = (yx * 2 + (1 - c), z)
    flips = ((y * 2 + (1 - x)), ((1 - y) * 2 + x))
    across = (1 - y) * 2 + (1 - x)

    def remote(src, dst, ssem, rsem, target):
        return pltpu.make_async_remote_copy(
            src_ref=src, dst_ref=dst, send_sem=ssem, recv_sem=rsem, device_id=target, device_id_type=MESH
        )

    barrier = pltpu.get_barrier_semaphore()
    for target in [partner, (flips[0] * 2 + c, z), (flips[1] * 2 + c, z)]:
        pl.semaphore_signal(barrier, inc=1, device_id=target, device_id_type=MESH)
    for d in range(1, NZ):
        pl.semaphore_signal(barrier, inc=1, device_id=(dp, lax.rem(z + d, NZ)), device_id_type=MESH)
    pl.semaphore_wait(barrier, 6)

    def gate_copy(d):
        return remote(gg.at[lax.rem(z + d, NZ)], ggr.at[z], g_send.at[d - 1], g_recv.at[d - 1], (dp, lax.rem(z + d, NZ)))

    for d in range(1, NZ):
        gate_copy(d).start()
    own_gate = pltpu.make_async_copy(gg.at[z], ggr.at[z], l_sem.at[0])
    own_gate.start()

    def home(item, d):
        target = lax.rem(z + d, NZ)
        part = pg.at[target] if item == 0 else pb.at[item - 1, target]
        return remote(
            part, land_o.at[item, z], r_send.at[item, d - 1], r_recv.at[item, d - 1], (dp, target)
        )

    def arrived(item):
        for d in range(1, NZ):
            source = lax.rem(z + NZ - d, NZ)
            ref = land_o.at[item, source]
            remote(ref, ref, r_send.at[item, d - 1], r_recv.at[item, d - 1], (dp, source)).wait_recv()

    def load(quad, sources):
        copies = [pltpu.make_async_copy(ref, quad[i], l_sem.at[1 + i]) for i, ref in enumerate(sources)]
        for copy in copies:
            copy.start()
        for copy in copies:
            copy.wait()

    def load_item(quad, item):
        arrived(item)
        own = pg.at[z] if item == 0 else pb.at[item - 1, z]
        load(quad, [own] + [land_o.at[item, lax.rem(z + d, NZ)] for d in range(1, NZ)])

    def quad_sum(quad):
        parts = [ref[...].astype(F32) for ref in quad]
        return (parts[0] + parts[1]) + (parts[2] + parts[3])

    cores, lands1, lands2, keeps = (core_b, core_i), (st1_b, st1_i), (lb_o, li_o), (kb_o, ki_o)

    def core_copy(kind, e, src):
        return remote(src, cores[kind].at[e], c_send.at[kind, e], c_recv.at[kind, e], partner)

    def hop1(kind, e, slot):
        block = flips[kind] if slot == 0 else across
        return remote(
            cores[kind].at[e, block], lands1[kind].at[e, slot],
            s1_send.at[kind, e, slot], s1_recv.at[kind, e, slot], (flips[kind] * 2 + c, z),
        )

    def hop2(kind, e):
        return remote(
            cores[kind].at[e, flips[1 - kind]], lands2[kind].at[e],
            s2_send.at[kind, e], s2_recv.at[kind, e], (flips[1 - kind] * 2 + c, z),
        )

    def send1(kind, e):
        for slot in (1, 0):
            hop1(kind, e, slot).start()

    def turn(kind, e):
        ref = cores[kind]
        hop1(kind, e, 1).wait_recv()
        ref[e, flips[1 - kind]] = add_low(ref[e, flips[1 - kind]], lands1[kind][e, 1])
        hop2(kind, e).start()
        hop1(kind, e, 0).wait_recv()
        ref[e, yx] = add_low(ref[e, yx], lands1[kind][e, 0])
        keep(kind, e).start()

    def keep(kind, e):
        return pltpu.make_async_copy(cores[kind].at[e, yx], keeps[kind].at[e], f_sem.at[kind, e])

    for item in range(2):
        for d in range(1, NZ):
            home(item, d).start()

    V = pltpu.VMEM
    rows = MB * ROWS

    def attention_grads(one, gqkv_s, nor_s, gat_s, ext):
        def inside(wqkv_s, wout_s, qkv_s, tok_s, dout_s, res_s, gres, gm_s):
            loads = [
                pltpu.make_async_copy(src, dst, o_sem.at[4 + i])
                for i, (src, dst) in enumerate(
                    ((wqkv, wqkv_s), (wout, wout_s))
                )
            ]
            for copy in loads:
                copy.start()
            ext[...] = jnp.zeros_like(ext)
            qkv_s[T:KEYS, :] = jnp.zeros((KEYS - T, 3 * D), BF16)
            for d in range(1, NZ):
                gate_copy(d).wait_send()
                source = lax.rem(z + NZ - d, NZ)
                remote(ggr.at[source], ggr.at[source], g_send.at[d - 1], g_recv.at[d - 1], (dp, source)).wait_recv()
            own_gate.wait()
            for copy in loads:
                copy.wait()

            def image(mb, carry):
                quad = [gqkv_s.at[mb, :, i * D : (i + 1) * D] for i in range(3)] + [gm_s]

                @pl.when(mb == 0)
                def _():
                    load(quad, [pg0.at[p] for p in range(NZ)])

                @pl.when(mb == 1)
                def _():
                    load_item(quad, 0)

                fetches = [
                    pltpu.make_async_copy(src.at[mb], dst, o_sem.at[8 + i])
                    for i, (src, dst) in enumerate(((qkv, qkv_s.at[0:T]), (dout, dout_s), (tok, tok_s), (resid, res_s)))
                ]
                for fetch in fetches:
                    fetch.start()
                gates = jnp.concatenate([ggr[p, mb] for p in range(NZ)], axis=0)
                g = tab[mb] * gates
                probs = rp[mb]
                gl = (probs * (g - jnp.sum(probs * g, axis=0, keepdims=True))).astype(BF16)
                fetches[3].wait()
                n2, r2 = normal(res_s[...])
                inner = (n2 * vec[2:3] + vec[3:4]).astype(BF16)
                wr = dot(gl, inner)
                for p in range(NZ):
                    ext[8 + LOCAL * p : 8 + LOCAL * (p + 1), :] += wr[8 * p : 8 * p + LOCAL]
                gi = quad_sum(quad) + dot(gl, wrt[...], TN)
                ext[5:6, :] += jnp.sum(gi * n2, axis=0, keepdims=True)
                ext[6:7, :] += jnp.sum(gi, axis=0, keepdims=True)
                u = gi * vec[2:3]
                fetches[1].wait()
                grad = dout_s[...].astype(F32) + r2 * (
                    u - jnp.mean(u, -1, keepdims=True) - n2 * jnp.mean(u * n2, -1, keepdims=True)
                )

                @pl.when(mb == 1)
                def _():
                    pltpu.make_async_copy(gres, ig_o.at[0], o_sem.at[12]).wait()

                gres[...] = grad
                low = grad.astype(BF16)
                gat_s[mb] = low
                ext[4:5, :] += jnp.sum(low.astype(F32), axis=0, keepdims=True)
                gm_s[...] = dot(low, wout_s[...], NT).astype(BF16)
                fetches[0].wait()

                def heads(p, carry):
                    at = [pl.ds(pl.multiple_of(i * D + p * 128, 128), 128) for i in range(3)]
                    q, k, v = qkv_s[0:T, at[0]], qkv_s[:, at[1]], qkv_s[:, at[2]]
                    gm = gm_s[:, at[0]]
                    gq = jnp.zeros((T, 128), F32)
                    gk = jnp.zeros((KEYS, 128), F32)
                    gv = jnp.zeros((KEYS, 128), F32)
                    for which in (0, 1):
                        mask = half_mask(which)
                        km = k * mask
                        prob = attention_probs(dot(q, km, NT) * HEAD_DIM ** (-0.5))
                        gpr = dot(gm, v * mask, NT)
                        gs = (prob * (gpr - jnp.sum(prob * gpr, axis=-1, keepdims=True))).astype(BF16)
                        gq = gq + dot(gs, km)
                        gk = gk + dot(gs, q * mask, TN)
                        gv = gv + dot(prob.astype(BF16), gm * mask, TN)
                    gqkv_s[mb, :, at[0]] = (gq * HEAD_DIM ** (-0.5)).astype(BF16)
                    gqkv_s[mb, :, at[1]] = (gk[0:T] * HEAD_DIM ** (-0.5)).astype(BF16)
                    gqkv_s[mb, :, at[2]] = gv[0:T].astype(BF16)
                    return carry

                lax.fori_loop(0, PAIRS, heads, 0, unroll=2)
                for row, i in ((2, 0), (3, 2)):
                    ext[row : row + 1, :] += jnp.sum(
                        gqkv_s[mb, :, i * D : (i + 1) * D].astype(F32), axis=0, keepdims=True
                    )
                gn = dot(gqkv_s[mb], wqkv_s[...], NT)
                fetches[2].wait()
                n1, r1 = normal(tok_s[...].astype(F32))
                nor_s[mb] = (n1 * vec[0:1] + vec[1:2]).astype(BF16)
                ext[0:1, :] += jnp.sum(gn * n1, axis=0, keepdims=True)
                ext[1:2, :] += jnp.sum(gn, axis=0, keepdims=True)
                w = gn * vec[0:1]
                gres[...] += r1 * (
                    w - jnp.mean(w, -1, keepdims=True) - n1 * jnp.mean(w * n1, -1, keepdims=True)
                )
                pltpu.make_async_copy(gres, ig_o.at[mb], o_sem.at[12 + mb]).start()

                @pl.when(mb == 0)
                def _():
                    one(1)

                return carry

            lax.fori_loop(0, MB, image, 0)
            pltpu.make_async_copy(gres, ig_o.at[1], o_sem.at[13]).wait()

        pl.run_scoped(
            inside,
            V((D, 3 * D), BF16), V((D, D), BF16), V((KEYS, 3 * D), BF16), V((T, D), BF16), V((T, D), BF16),
            V((T, D), F32), V((T, D), F32), V((T, D), BF16),
        )

        def shared(a, mix_s):
            mix = pltpu.make_async_copy(mixed, mix_s, o_sem.at[4])
            mix.start()
            for zz in range(NZ):
                @pl.when(z == zz)
                def _():
                    at = 24 + 5 * LOCAL * zz
                    ext[at : at + LOCAL, :] = bb[...]
                    for f in range(4):
                        ext[at + LOCAL * (f + 1) : at + LOCAL * (f + 2), :] = bi[:, f * CHUNK : (f + 1) * CHUNK]
            for i in range(3):
                total = jnp.zeros((D, D), F32)
                for mb in range(MB):
                    total = total + dot(nor_s[mb], gqkv_s[mb, :, i * D : (i + 1) * D], TN)
                a[i * D : (i + 1) * D, :] = total.astype(BF16)
            mix.wait()
            total = jnp.zeros((D, D), F32)
            for mb in range(MB):
                total = total + dot(mix_s[mb], gat_s[mb], TN)
            a[3 * D : 4 * D, :] = total.astype(BF16)
            a[4 * D : TOTAL, :] = ext[...].astype(BF16)

            def share(side, zz):
                return pl.ds(pl.multiple_of((side * NZ + zz) * SHARE, 16), SHARE)

            def to_core(zz):
                return remote(a.at[share(1 - c, zz)], ar_core.at[zz], ac_send.at[zz], ac_recv.at[zz], partner)

            for zz in range(NZ):
                to_core(zz).start()
            for kind in (0, 1):
                turn(kind, 0)

            def along(flow, zz, slot):
                return remote(
                    a.at[share(c, zz)], ar_z.at[flow, slot], az_send.at[flow, slot], az_recv.at[flow, slot],
                    (dp, z - 1 if flow == 0 else z + 1),
                )

            for j in range(NZ):
                zz = j
                to_core(zz).wait_recv()
                a[share(c, zz), :] = add_low(a[share(c, zz), :], ar_core[zz])
            for j in range(NZ - 1):
                @pl.when(z == NZ - 1)
                def _():
                    along(0, j, j).start()

                @pl.when(z == 0)
                def _():
                    along(1, NZ - 1 - j, NZ - 2 - j).start()

            def sum_one(flow, dest, at):
                slot = dest if flow == 0 else dest - 1

                @pl.when(z == at)
                def _():
                    along(flow, dest, slot).wait_recv()
                    a[share(c, dest), :] = add_low(a[share(c, dest), :], ar_z[flow, slot])
                    if at != dest:
                        along(flow, dest, slot).start()

            for d in range(1, NZ):
                home(2, d).start()
            one(2)
            for kind in (0, 1):
                turn(kind, 1)
            for step, order in enumerate((
                ((0, 0, 2), (1, 3, 1)),
                ((0, 1, 2), (1, 3, 2), (1, 2, 1), (0, 0, 1)),
                ((0, 2, 2), (1, 2, 2), (1, 1, 1), (0, 1, 1), (0, 0, 0), (1, 3, 3)),
            )):
                for flow, dest, at in order:
                    sum_one(flow, dest, at)

            halves = (slice(0, 208), slice(208, SHARE))

            def cross(stage_no, half, src):
                dest = (ar_xy1, ar_xy2)[stage_no].at[halves[half]]
                way = half if stage_no == 0 else 1 - half
                return remote(
                    src, dest, ax_send.at[stage_no, half], ax_recv.at[stage_no, half], (flips[way] * 2 + c, z)
                )

            def mine(half):
                start_row = 0 if half == 0 else 208
                size = 208 if half == 0 else SHARE - 208
                return pl.ds(pl.multiple_of((c * NZ + z) * SHARE + start_row, 16), size)

            for half in (0, 1):
                cross(0, half, a.at[mine(half)]).start()
            for half in (0, 1):
                cross(0, half, a.at[mine(half)]).wait_recv()
                ar_t[halves[half], :] = add_low(a[mine(half), :], ar_xy1[halves[half], :])
                cross(1, half, ar_t.at[halves[half]]).start()
            one(3)
            for half in (0, 1):
                cross(1, half, ar_t.at[halves[half]]).wait()
                ar_t[halves[half], :] = add_low(ar_t[halves[half], :], ar_xy2[halves[half], :])
                cross(0, half, a.at[mine(half)]).wait_send()
            for zz in range(NZ):
                to_core(zz).wait_send()
                for flow in (0, 1):
                    slot = zz if flow == 0 else zz - 1
                    if 0 <= slot < NZ - 1:
                        goes = (z > zz) if flow == 0 else (z < zz)

                        @pl.when(goes)
                        def _():
                            along(flow, zz, slot).wait_send()

        pl.run_scoped(shared, V((TOTAL, D), BF16), V((MB, T, D), BF16))

    def body(wg_b, wg_i, act_s, gh_s, x_s, gp_s, xp):
        def fetch(e, which):
            pairs = ((act, act_s), (gp, gp_s), (xr, x_s), (gh, gh_s))
            return [
                pltpu.make_async_copy(pairs[i][0].at[e], pairs[i][1], o_sem.at[i]) for i in which
            ]

        def pull(e, which):
            for copy in fetch(e, which):
                copy.start()

        def ready(e, which):
            for copy in fetch(e, which):
                copy.wait()

        pull(0, (0, 1, 2, 3))

        def one(e):
            def back_block(k, side):
                at = pl.ds(pl.multiple_of((2 * k + side) * PART, 128), PART)
                return dot(act_s[:, at], gp_s[...], TN)

            ready(e, (0, 1))

            if e > 0:
                core_copy(0, e - 1, wg_b).wait_send()

            def other_b(k, carry):
                wg_b[k] = back_block(k, 1 - c).astype(BF16)
                return carry

            lax.fori_loop(0, 4, other_b, 0, unroll=2)
            core_copy(0, e, wg_b).start()
            ready(e, (2, 3))
            for side in (0, 1):
                for k in range(4):
                    band = (2 * k + side) * BAND
                    xp[side, :, k * BAND : (k + 1) * BAND] = x_s[:, band : band + BAND]

            if e > 0:
                core_copy(1, e - 1, wg_i).wait_send()

            def other_i(f, carry):
                at = pl.ds(pl.multiple_of(f * CHUNK, 128), CHUNK)
                grad = dot(xp[1 - c], gh_s[:, at], TN).astype(BF16)
                for k in range(4):
                    wg_i[k, :, at] = grad[k * BAND : (k + 1) * BAND]
                return carry

            lax.fori_loop(0, 4, other_i, 0, unroll=2)
            core_copy(1, e, wg_i).start()
            core_copy(0, e, wg_b).wait_recv()

            def own_b(k, carry):
                core_b[e, k] = (core_b[e, k].astype(F32) + back_block(k, c)).astype(BF16)
                return carry

            lax.fori_loop(0, 4, own_b, 0, unroll=2)

            send1(0, e)
            if e < LOCAL - 1:
                pull(e + 1, (0, 1))

            core_copy(1, e, wg_i).wait_recv()

            def own_i(f, carry):
                at = pl.ds(pl.multiple_of(f * CHUNK, 128), CHUNK)
                grad = dot(xp[c], gh_s[:, at], TN)
                for k in range(4):
                    core_i[e, k, :, at] = (
                        core_i[e, k, :, at].astype(F32) + grad[k * BAND : (k + 1) * BAND]
                    ).astype(BF16)
                return carry

            lax.fori_loop(0, 4, own_i, 0, unroll=2)

            send1(1, e)
            if e < LOCAL - 1:
                pull(e + 1, (2, 3))

        one(0)
        pl.run_scoped(
            functools.partial(attention_grads, one),
            V((MB, T, 3 * D), BF16), V((MB, T, D), BF16), V((MB, T, D), BF16), V((EXTRA, D), F32),
        )
        core_copy(0, LOCAL - 1, wg_b).wait_send()
        core_copy(1, LOCAL - 1, wg_i).wait_send()

    pl.run_scoped(
        body,
        V((4, PART, D), BF16), V((4, BAND, HIDDEN), BF16), V((rows, HIDDEN), BF16), V((rows, HIDDEN), BF16),
        V((rows, D), BF16), V((rows, D), BF16), V((2, rows, D // 2), BF16),
    )

    def place(zz):
        return ar_o.at[pl.ds(pl.multiple_of((c * NZ + zz) * SHARE, 16), SHARE)]

    own_share = pltpu.make_async_copy(ar_t, place(z), l_sem.at[6])
    own_share.start()

    def spread(up, h):
        source = z - h if up else z + h
        index = (0 if up else 1, h)
        return remote(
            ar_t if h == 0 else place(source), place(source), zz_send.at[index], zz_recv.at[index],
            (dp, z + 1 if up else z - 1),
        )

    def leaves(up, h):
        return jnp.logical_and(z - h >= 0, z + 1 < NZ) if up else jnp.logical_and(z + h < NZ, z >= 1)

    def to_partner(src, k, zz):
        return remote(src, place(zz), cc_send.at[k], cc_recv.at[k], partner)

    for up in (True, False):
        @pl.when(leaves(up, 0))
        def _():
            spread(up, 0).start()

    to_partner(ar_t, 0, z).start()
    def block_out(mb):
        def image_out(base, quad_s, low):
            quad = [quad_s.at[i] for i in range(NZ)]
            fetch = pltpu.make_async_copy(resid.at[mb], base, l_sem.at[5])
            fetch.start()
            load_item(quad, 1 + mb)
            fetch.wait()
            low[...] = (base[...] + quad_sum(quad)).astype(BF16)
            store = pltpu.make_async_copy(low, block_o.at[mb], l_sem.at[7])
            store.start()
            store.wait()

        pl.run_scoped(image_out, V((T, D), F32), V((NZ, T, D), BF16), V((T, D), BF16))

    block_out(0)
    for h in range(NZ - 1):
        for up in (True, False):
            source = z - h - 1 if up else z + h + 1

            @pl.when((z - h - 1 >= 0) if up else (z + h + 1 < NZ))
            def _():
                index = (0 if up else 1, h)
                remote(
                    place(source), place(source), zz_send.at[index], zz_recv.at[index],
                    (dp, z - 1 if up else z + 1),
                ).wait_recv()
                k = lax.rem(source - z + NZ, NZ)
                to_partner(place(source), k, source).start()

            if h + 1 < NZ - 1:
                @pl.when(leaves(up, h + 1))
                def _():
                    spread(up, h + 1).start()
        if h < 2:
            for kind in (0, 1):
                turn(kind, 2 + h)
    block_out(1)
    own_share.wait()
    for k in range(NZ):
        zz = lax.rem(z + k, NZ)
        src = ar_t if k == 0 else place(zz)
        to_partner(src, k, zz).wait_send()
        other = ar_o.at[pl.ds(pl.multiple_of(((1 - c) * NZ + zz) * SHARE, 16), SHARE)]
        remote(other, other, cc_send.at[k], cc_recv.at[k], partner).wait_recv()
    for h in range(NZ - 1):
        for up in (True, False):
            @pl.when(leaves(up, h))
            def _():
                spread(up, h).wait_send()
    for item in range(3):
        for d in range(1, NZ):
            home(item, d).wait_send()
    for kind in (0, 1):
        for e in range(LOCAL):
            for slot in (0, 1):
                hop1(kind, e, slot).wait_send()
            hop2(kind, e).wait()
            keep(kind, e).wait()


def grads_call(*operands):
    vm = pl.BlockSpec(memory_space=pltpu.VMEM)
    hb = pl.BlockSpec(memory_space=pl.ANY)
    S = jax.ShapeDtypeStruct
    V = pltpu.VMEM
    DMA = pltpu.SemaphoreType.DMA
    outs = [
        (S((MB, T, D), BF16), hb),
        (S((MB, T, D), F32), hb),
        (S((TOTAL, D), BF16), hb),
        (S((LOCAL, PART, D), BF16), hb),
        (S((LOCAL, BAND, HIDDEN), BF16), hb),
        (S((LOCAL, PART, D), BF16), hb),
        (S((LOCAL, BAND, HIDDEN), BF16), hb),
        (S((3, NZ, T, D), BF16), hb),
    ]
    return pl.pallas_call(
        grads_kernel,
        out_shape=[o[0] for o in outs],
        in_specs=[vm] * 6 + [hb] * 15,
        out_specs=[o[1] for o in outs],
        scratch_shapes=[
            V((LOCAL, 4, PART, D), BF16), V((LOCAL, 4, BAND, HIDDEN), BF16),
            V((LOCAL, 2, PART, D), BF16), V((LOCAL, 2, BAND, HIDDEN), BF16),
            V((NZ, SHARE, D), BF16), V((2, NZ - 1, SHARE, D), BF16),
            V((SHARE, D), BF16), V((SHARE, D), BF16), V((SHARE, D), BF16),
            V((NZ, MB, 8, T), F32),
            DMA((2, LOCAL)), DMA((2, LOCAL)), DMA((2, LOCAL, 2)), DMA((2, LOCAL, 2)), DMA((2, LOCAL)), DMA((2, LOCAL)),
            DMA((3, NZ - 1)), DMA((3, NZ - 1)), DMA((NZ - 1,)), DMA((NZ - 1,)),
            DMA((NZ,)), DMA((NZ,)), DMA((2, NZ - 1)), DMA((2, NZ - 1)), DMA((2, 2)), DMA((2, 2)),
            DMA((2, NZ - 1)), DMA((2, NZ - 1)), DMA((NZ,)), DMA((NZ,)),
            DMA((8,)), DMA((14,)), DMA((2, LOCAL)),
        ],
        compiler_params=pltpu.CompilerParams(
            collective_id=2, has_side_effects=True, vmem_limit_bytes=63 << 20
        ),
        name="grads",
    )(*operands)


def finish_kernel(
    ar, kb, ki, lb, li, block, ig,
    block_o, ig_o, g1_o, s1_o, qkv_o, qv_o, wout_o, bout_o, g2_o, s2_o, route_o, wi_o, bi_o, wb_o, bb_o,
    ar_s, kb_s, ki_s, lb_s, li_s, block_s, ig_s, wide, narrow, out_i, out_b, tall,
    in_sem, out_sem,
):
    dp = lax.axis_index("dp")
    z = lax.axis_index("expert")

    def fetch(src, dst, i):
        copy = pltpu.make_async_copy(src, dst, in_sem.at[i])
        copy.start()
        return copy

    back = [(fetch(kb.at[e], kb_s.at[e], e), fetch(lb.at[e], lb_s.at[e], 4 + e)) for e in range(LOCAL)]
    ahead = [(fetch(ki.at[e], ki_s.at[e], 8 + e), fetch(li.at[e], li_s.at[e], 12 + e)) for e in range(LOCAL)]
    dense = [
        fetch(ar.at[i * D : (i + 1) * D], ar_s.at[i * D : (i + 1) * D], 16 + i) for i in range(4)
    ]
    few = fetch(ar.at[4 * D : TOTAL], ar_s.at[4 * D : TOTAL], 20)
    rows_in = (fetch(block, block_s, 21), fetch(ig, ig_s, 22))
    sent = []

    def send(src, dst):
        copy = pltpu.make_async_copy(src, dst, out_sem.at[len(sent)])
        copy.start()
        sent.append(copy)

    for pairs, kept, landed, out, dst in ((back, kb_s, lb_s, out_b, wb_o), (ahead, ki_s, li_s, out_i, wi_o)):
        for e in range(LOCAL):
            for copy in pairs[e]:
                copy.wait()
            out[e] = kept[e].astype(F32) + landed[e].astype(F32)
            send(out.at[e], dst.at[e])
    for i in range(4):
        dense[i].wait()
        part = ar_s[i * D : (i + 1) * D, :].astype(F32)
        if i < 3:
            wide[i] = part
            send(wide.at[i], qkv_o.at[:, i * D : (i + 1) * D])
        else:
            narrow[...] = part
            send(narrow, wout_o)
    few.wait()
    low = ar_s[4 * D : TOTAL, :]
    ext = low.astype(F32)
    for row, ref in ((0, g1_o), (1, s1_o), (4, bout_o), (5, g2_o), (6, s2_o)):
        ref[...] = ext[row]
    qv_o[...] = ext[2:4]
    route_o[...] = ext[8 : 8 + NZ * LOCAL]

    def pick(first):
        at = lax.broadcasted_iota(jnp.int32, (8, EXTRA), 0) + first
        return dot((at == lax.broadcasted_iota(jnp.int32, (8, EXTRA), 1)).astype(F32).astype(BF16), low)

    base = 24 + 5 * LOCAL * z
    column = lax.broadcasted_iota(jnp.int32, (D, BAND), 1) + dp * BAND
    chosen = (column == lax.broadcasted_iota(jnp.int32, (D, BAND), 0)).astype(F32).astype(BF16)
    bb_o[...] = dot(pick(base).astype(BF16), chosen)[:LOCAL]
    rows = pick(base + LOCAL * (dp // 2 + 1))
    bi_o[...] = jnp.where(lax.rem(dp, 2) == 0, rows[:, :PART], rows[:, PART:])[:LOCAL]
    for copy in rows_in:
        copy.wait()
    for mb in range(MB):
        at = slice(mb * SEQ, (mb + 1) * SEQ)
        tall[at, :] = block_s[mb].astype(F32)[:SEQ]
        ig_o[at, :] = ig_s[mb, :SEQ, :]
    block_o[...] = tall[0 : MB * SEQ, :].astype(BF16)
    for copy in sent:
        copy.wait()


def finish_call(*operands):
    vm = pl.BlockSpec(memory_space=pltpu.VMEM)
    hb = pl.BlockSpec(memory_space=pl.ANY)
    S = jax.ShapeDtypeStruct
    V = pltpu.VMEM
    rows = MB * SEQ
    vector = (S((D,), F32), vm)
    outs = [
        (S((rows, D), BF16), vm),
        (S((rows, D), F32), vm),
        vector,
        vector,
        (S((D, 3 * D), F32), hb),
        (S((2, D), F32), vm),
        (S((D, D), F32), hb),
        vector,
        vector,
        vector,
        (S((NZ * LOCAL, D), F32), vm),
        (S((LOCAL, BAND, HIDDEN), F32), hb),
        (S((LOCAL, PART), F32), vm),
        (S((LOCAL, PART, D), F32), hb),
        (S((LOCAL, BAND), F32), vm),
    ]
    return pl.pallas_call(
        finish_kernel,
        out_shape=[o[0] for o in outs],
        in_specs=[hb] * 7,
        out_specs=[o[1] for o in outs],
        scratch_shapes=[
            V((TOTAL, D), BF16),
            V((LOCAL, PART, D), BF16), V((LOCAL, BAND, HIDDEN), BF16), V((LOCAL, PART, D), BF16), V((LOCAL, BAND, HIDDEN), BF16),
            V((MB, T, D), BF16), V((MB, T, D), F32), V((3, D, D), F32), V((D, D), F32),
            V((LOCAL, BAND, HIDDEN), F32), V((LOCAL, PART, D), F32), V((400, D), F32),
            pltpu.SemaphoreType.DMA((23,)), pltpu.SemaphoreType.DMA((12,)),
        ],
        compiler_params=pltpu.CompilerParams(vmem_limit_bytes=58 << 20),
        name="finish",
    )(*operands)

def fast_body(
    tokens, routes, gain_one, shift_one, w_qkv, qv_bias, w_out, out_bias, gain_two, shift_two,
    w_route, w_in, b_in, w_back, b_back, d_out,
):
    wrt = jnp.pad(w_route.T.reshape(NZ, LOCAL, D), ((0, 0), (0, 8 - LOCAL), (0, 0))).reshape(32, D)
    (vec, tab, tw, qkv, mixed, resid, rp, gg, bb, bi, dw, xr, gp, act, gh, pb, pg, pg0) = dispatch_call(
        tokens, d_out, routes, gain_one, shift_one, gain_two, shift_two, out_bias, qv_bias,
        w_qkv, w_out, wrt, b_in, b_back, w_in, w_back,
    )
    block, ig, ar, kb, ki, lb, li, _ = grads_call(
        vec, tab, wrt, bb, bi, rp, tw, dw, w_qkv, w_out, qkv, mixed, resid, gg, xr, gp, act, gh, pb, pg, pg0
    )
    out = list(finish_call(ar, kb, ki, lb, li, block, ig))
    out[10] = out[10].T
    return tuple(out)


def solution(mesh):
    fast = mesh.shape["dp"] == 8 and mesh.shape["expert"] == NZ
    return jax.shard_map(
        fast_body if fast else general_body,
        mesh=mesh,
        in_specs=(
            P(("dp", "expert"), None),
            P(("dp", "expert"), None),
            P(),
            P(),
            P(),
            P(),
            P(),
            P(),
            P(),
            P(),
            P(),
            P("expert", None, None),
            P("expert", None),
            P("expert", None, None),
            P("expert", None),
            P(("dp", "expert"), None),
        ),
        out_specs=(
            P(("dp", "expert"), None),
            P(("dp", "expert"), None),
            P(),
            P(),
            P(),
            P(),
            P(),
            P(),
            P(),
            P(),
            P(),
            P("expert", "dp", None),
            P("expert", "dp"),
            P("expert", "dp", None),
            P("expert", "dp"),
        ),
        check_vma=False,
    )
```

```python
import functools

import jax
import jax.numpy as jnp
from jax import lax
from jax.experimental import pallas as pl
from jax.experimental.pallas import tpu as pltpu
from jax.sharding import PartitionSpec as P

HEADS = 12
HEAD_DIM = 64
SEQ = 197
TOP = 2
MB = 2
ROWS_MB = 197
D = 768


HIGH = lax.Precision.HIGHEST
EPSILON = 1e-06


def layer_norm(value, gain, shift):
    center = value - jnp.mean(value, axis=-1, keepdims=True)
    spread = jnp.mean(center * center, axis=-1, keepdims=True)
    return center * lax.rsqrt(spread + EPSILON) * gain + shift


def route_soft(logits):
    return jax.nn.softmax(logits, axis=-1)


def general_body(
    tokens,
    routes,
    gain_one,
    shift_one,
    w_qkv,
    qv_bias,
    w_out,
    out_bias,
    gain_two,
    shift_two,
    w_route,
    w_in,
    b_in,
    w_back,
    b_back,
    d_out,
):
    groups = lax.axis_size("expert")
    local = w_in.shape[0]
    experts = groups * local
    width = tokens.shape[1]
    rows = ROWS_MB
    cap = 5 * rows * TOP // (3 * experts)
    images = rows // SEQ
    scale = HEAD_DIM ** (-0.5)
    expert_ids = jnp.arange(experts, dtype=jnp.int32)
    w_route_wide = w_route.astype(jnp.float32)
    acc_gain_one = jnp.zeros_like(gain_one)
    acc_shift_one = jnp.zeros_like(shift_one)
    acc_qkv = jnp.zeros(w_qkv.shape, jnp.float32)
    acc_qv = jnp.zeros_like(qv_bias)
    acc_out = jnp.zeros(w_out.shape, jnp.float32)
    acc_out_bias = jnp.zeros_like(out_bias)
    acc_gain_two = jnp.zeros_like(gain_two)
    acc_shift_two = jnp.zeros_like(shift_two)
    acc_route = jnp.zeros(w_route.shape, jnp.float32)
    acc_expert = None
    outputs = []
    input_grads = []
    for part in range(MB):
        x = tokens[part * rows : (part + 1) * rows].astype(jnp.float32)
        route = routes[part * rows : (part + 1) * rows]
        cotan = d_out[part * rows : (part + 1) * rows].astype(jnp.float32)
        normed, ln_one_pull = jax.vjp(layer_norm, x, gain_one, shift_one)
        normed_low = normed.astype(jnp.bfloat16)
        bias = jnp.concatenate([qv_bias[0], jnp.zeros_like(qv_bias[0]), qv_bias[1]])
        qkv = (jnp.dot(normed_low, w_qkv, preferred_element_type=jnp.float32) + bias).astype(
            jnp.bfloat16
        )
        query = qkv[:, :width].reshape(images, SEQ, HEADS, HEAD_DIM)
        keys = qkv[:, width : 2 * width].reshape(images, SEQ, HEADS, HEAD_DIM)
        values = qkv[:, 2 * width :].reshape(images, SEQ, HEADS, HEAD_DIM)
        scores = (
            jnp.einsum("ishd,ithd->ihst", query, keys, preferred_element_type=jnp.float32) * scale
        )
        log_total = jax.nn.logsumexp(scores, axis=-1, keepdims=True)
        probs_low = jnp.exp(scores - log_total).astype(jnp.bfloat16)
        mixed = jnp.einsum("ihst,ithd->ishd", probs_low, values, preferred_element_type=jnp.float32)
        mixed = mixed.reshape(rows, width).astype(jnp.bfloat16)
        resid = x + jnp.dot(mixed, w_out, preferred_element_type=jnp.float32) + out_bias
        inner, ln_two_pull = jax.vjp(layer_norm, resid, gain_two, shift_two)
        inner_low = inner.astype(jnp.bfloat16)
        logits = jnp.dot(inner_low, w_route, preferred_element_type=jnp.float32)
        route_probs, soft_pull = jax.vjp(route_soft, logits)
        choose = (route[:, :, None] == expert_ids[None, None, :]).astype(jnp.float32)
        gates = jnp.einsum("rke,re->rk", choose, route_probs, precision=HIGH)
        flat_ids = route.reshape(-1)
        table = (flat_ids[:, None] == expert_ids[None, :]).astype(jnp.int32)
        order = jnp.arange(rows * TOP, dtype=jnp.int32)
        earlier = (order[None, :] < order[:, None]).astype(jnp.bfloat16)
        before = jnp.dot(
            earlier, table.astype(jnp.bfloat16), preferred_element_type=jnp.float32
        ).astype(jnp.int32)
        slot = jnp.sum(before * table, axis=1)
        dest = flat_ids * cap + slot
        sending = (
            jnp.zeros((experts * cap, width), jnp.bfloat16)
            .at[dest]
            .set(jnp.repeat(inner_low, TOP, axis=0))
        )
        sending = sending.reshape(groups, local, cap, width)
        received = lax.all_to_all(sending, "expert", split_axis=0, concat_axis=0, tiled=True)
        hidden = jnp.einsum("secd,edf->secf", received, w_in, preferred_element_type=jnp.float32)
        hidden = hidden + b_in[None, :, None, :]
        active = jax.nn.gelu(hidden).astype(jnp.bfloat16)
        result = jnp.einsum("secf,efd->secd", active, w_back, preferred_element_type=jnp.float32)
        result = (result + b_back[None, :, None, :]).astype(jnp.bfloat16)
        returned = lax.all_to_all(result, "expert", split_axis=0, concat_axis=0, tiled=True)
        returned, kept_rows, kept_hidden = (returned, received, hidden)
        picked = (
            returned.reshape(experts * cap, width)[dest]
            .reshape(rows, TOP, width)
            .astype(jnp.float32)
        )
        block = resid + jnp.sum(gates[:, :, None] * picked, axis=1)
        outputs.append(block.astype(jnp.bfloat16))
        grad_gate = jnp.sum(picked * cotan[:, None, :], axis=2)
        grad_picked = (gates[:, :, None] * cotan[:, None, :]).astype(jnp.bfloat16)
        grad_send = (
            jnp.zeros((experts * cap, width), jnp.bfloat16)
            .at[dest]
            .set(grad_picked.reshape(rows * TOP, width))
        )
        grad_send = grad_send.reshape(groups, local, cap, width)
        grad_recv = lax.all_to_all(grad_send, "expert", split_axis=0, concat_axis=0, tiled=True)
        active, gelu_pull = jax.vjp(jax.nn.gelu, kept_hidden)
        active_low = active.astype(jnp.bfloat16)
        grad_active = jnp.einsum(
            "secd,efd->secf", grad_recv, w_back, preferred_element_type=jnp.float32
        )
        grad_hidden = gelu_pull(grad_active)[0].astype(jnp.bfloat16)
        step_w_back = jnp.einsum(
            "secf,secd->efd", active_low, grad_recv, preferred_element_type=jnp.float32
        )
        step_b_back = jnp.sum(grad_recv.astype(jnp.float32), axis=(0, 2))
        step_w_in = jnp.einsum(
            "secd,secf->edf", kept_rows, grad_hidden, preferred_element_type=jnp.float32
        )
        step_b_in = jnp.sum(grad_hidden.astype(jnp.float32), axis=(0, 2))
        grad_rows = jnp.einsum(
            "secf,edf->secd", grad_hidden, w_in, preferred_element_type=jnp.float32
        )
        grad_rows = grad_rows.astype(jnp.bfloat16)
        grad_back = lax.all_to_all(grad_rows, "expert", split_axis=0, concat_axis=0, tiled=True)
        shares = (step_w_in, step_b_in, step_w_back, step_b_back)
        if acc_expert is None:
            acc_expert = shares
        else:
            acc_expert = tuple((a + b for a, b in zip(acc_expert, shares)))
        grad_inner = jnp.sum(
            grad_back.reshape(experts * cap, width)[dest]
            .reshape(rows, TOP, width)
            .astype(jnp.float32),
            axis=1,
        )
        grad_probs = jnp.einsum("rk,rke->re", grad_gate, choose, precision=HIGH)
        grad_logits = soft_pull(grad_probs)[0]
        acc_route = acc_route + jnp.einsum(
            "rd,re->de", inner_low.astype(jnp.float32), grad_logits, precision=HIGH
        )
        grad_inner = grad_inner + jnp.einsum("re,de->rd", grad_logits, w_route_wide, precision=HIGH)
        grad_ln_two, grad_gain_two, grad_shift_two = ln_two_pull(grad_inner)
        acc_gain_two = acc_gain_two + grad_gain_two
        acc_shift_two = acc_shift_two + grad_shift_two
        grad_resid = cotan + grad_ln_two
        grad_att = grad_resid.astype(jnp.bfloat16)
        acc_out = acc_out + jnp.einsum(
            "rd,re->de", mixed, grad_att, preferred_element_type=jnp.float32
        )
        acc_out_bias = acc_out_bias + jnp.sum(grad_att.astype(jnp.float32), axis=0)
        grad_mixed = jnp.einsum("re,de->rd", grad_att, w_out, preferred_element_type=jnp.float32)
        grad_mixed = grad_mixed.astype(jnp.bfloat16).reshape(images, SEQ, HEADS, HEAD_DIM)
        again = (
            jnp.einsum("ishd,ithd->ihst", query, keys, preferred_element_type=jnp.float32) * scale
        )
        probs = jnp.exp(again - log_total)
        grad_probs_att = jnp.einsum(
            "ishd,ithd->ihst", grad_mixed, values, preferred_element_type=jnp.float32
        )
        row_total = jnp.sum(probs * grad_probs_att, axis=-1, keepdims=True)
        grad_scores = (probs * (grad_probs_att - row_total)).astype(jnp.bfloat16)
        grad_query = (
            jnp.einsum("ihst,ithd->ishd", grad_scores, keys, preferred_element_type=jnp.float32)
            * scale
        )
        grad_keys = (
            jnp.einsum("ihst,ishd->ithd", grad_scores, query, preferred_element_type=jnp.float32)
            * scale
        )
        grad_values = jnp.einsum(
            "ihst,ishd->ithd",
            probs.astype(jnp.bfloat16),
            grad_mixed,
            preferred_element_type=jnp.float32,
        )
        grad_qkv = jnp.concatenate(
            [
                grad_query.reshape(rows, width),
                grad_keys.reshape(rows, width),
                grad_values.reshape(rows, width),
            ],
            axis=1,
        ).astype(jnp.bfloat16)
        acc_qkv = acc_qkv + jnp.einsum(
            "rd,re->de", normed_low, grad_qkv, preferred_element_type=jnp.float32
        )
        column_sums = jnp.sum(grad_qkv.astype(jnp.float32), axis=0)
        acc_qv = acc_qv + jnp.stack([column_sums[:width], column_sums[2 * width :]])
        grad_normed = jnp.einsum("re,de->rd", grad_qkv, w_qkv, preferred_element_type=jnp.float32)
        grad_ln_one, grad_gain_one, grad_shift_one = ln_one_pull(grad_normed)
        acc_gain_one = acc_gain_one + grad_gain_one
        acc_shift_one = acc_shift_one + grad_shift_one
        input_grads.append(grad_resid + grad_ln_one)
    expert_grads = (
        lax.psum_scatter(
            acc_expert[0].astype(jnp.bfloat16), "dp", scatter_dimension=1, tiled=True
        ).astype(jnp.float32),
        lax.psum_scatter(
            acc_expert[1].astype(jnp.bfloat16), "dp", scatter_dimension=1, tiled=True
        ).astype(jnp.float32),
        lax.psum_scatter(
            acc_expert[2].astype(jnp.bfloat16), "dp", scatter_dimension=1, tiled=True
        ).astype(jnp.float32),
        lax.psum_scatter(
            acc_expert[3].astype(jnp.bfloat16), "dp", scatter_dimension=1, tiled=True
        ).astype(jnp.float32),
    )
    shared = (
        acc_gain_one,
        acc_shift_one,
        acc_qkv,
        acc_qv,
        acc_out,
        acc_out_bias,
        acc_gain_two,
        acc_shift_two,
        acc_route,
    )
    shared = lax.psum(
        (
            shared[0],
            shared[1],
            shared[2],
            shared[3],
            shared[4],
            shared[5],
            shared[6],
            shared[7],
            shared[8],
        ),
        ("dp", "expert"),
    )
    return (
        jnp.concatenate(outputs, axis=0),
        jnp.concatenate(input_grads, axis=0),
        shared[0],
        shared[1],
        shared[2],
        shared[3],
        shared[4],
        shared[5],
        shared[6],
        shared[7],
        shared[8],
        expert_grads[0],
        expert_grads[1],
        expert_grads[2],
        expert_grads[3],
    )


F32, BF16 = jnp.float32, jnp.bfloat16
NZ = 4
LOCAL = 4
PAIRS = HEADS // 2
T = 208
KEYS = 256
CAP = 41
CAP_ROWS = 48
PACKED = 176
ROWS = NZ * CAP_ROWS
CHUNK = 768
PIECE = 1536
PIECES = 4 * CHUNK // PIECE
MESH = pl.DeviceIdType.MESH
NT = (((1,), (1,)), ((), ()))
TN = (((0,), (0,)), ((), ()))


def dot(a, b, dims=(((1,), (0,)), ((), ()))):
    return lax.dot_general(a, b, dims, preferred_element_type=F32)


def normal(value):
    center = value - jnp.mean(value, axis=-1, keepdims=True)
    scale = lax.rsqrt(jnp.mean(center * center, axis=-1, keepdims=True) + EPSILON)
    return center * scale, scale


def half_mask(which):
    lane = lax.broadcasted_iota(jnp.int32, (1, 128), 1)
    return ((lane < 64) if which == 0 else (lane >= 64)).astype(F32).astype(BF16)


def attention_probs(scores):
    key = lax.broadcasted_iota(jnp.int32, scores.shape, 1)
    scores = jnp.where(key < SEQ, scores, -1e30)
    top = jnp.max(scores, axis=-1, keepdims=True)
    raised = jnp.exp(scores - top)
    return raised / jnp.sum(raised, axis=-1, keepdims=True)


def route_softmax(logits, real):
    logits = jnp.where(real, logits, -1e30)
    raised = jnp.exp(logits - jnp.max(logits, axis=0, keepdims=True))
    raised = jnp.where(real, raised, 0.0)
    return raised / jnp.sum(raised, axis=0, keepdims=True)


def pick_matrix(slots):
    index = lax.broadcasted_iota(jnp.int32, (CAP_ROWS, T), 0).astype(F32)
    return jnp.concatenate(
        [(index == slots[e : e + 1, :]).astype(F32) for e in range(LOCAL)], axis=0
    )


def dispatch_kernel(
    tok, dout, routes, v0, v1, v2, v3, v4, qv, wqkv, wout, wrt, b_in, b_back, w_in, w_back,
    vec, tab_o, tw_o, qkv_o, mixed_o, resid_o, rp_o, gg_o, bb_o, bi_o, dw_o, x_o, gp_o, act_o, gh_o, pb_o, pg_o, home_o,
    gi, gd, sl, sg, dense, qkv_s, mixed_s, inner_s, xs, gs, cs, rgs, ggs, wb1, wb2, act_st, gh_st, acc_o, acc_g,
    os_, grs, pb_s, pg_s,
    send_sem, recv_sem, d_sem, w_sem, st_sem, x_sem, p_sem, h_send, h_recv,
):
    dp = lax.axis_index("dp")
    z = lax.axis_index("expert")

    def item_ref(kind, source, mb):
        return (gd, sg, gi, sl)[kind].at[source, mb]

    def copy_of(up, kind, mb, h, source, target, packed):
        index = (0 if up else 1, kind * MB + mb, h)
        dst = item_ref(kind, source, mb)
        src = dst
        if packed:
            src, dst = dense.at[kind // 2, mb, h], dst.at[0:PACKED]
        return pltpu.make_async_remote_copy(
            src_ref=src, dst_ref=dst, send_sem=send_sem.at[index], recv_sem=recv_sem.at[index],
            device_id=(dp, target), device_id_type=MESH,
        )

    def hop(up, kind, mb, h, packed):
        return copy_of(up, kind, mb, h, z - h if up else z + h, z + 1 if up else z - 1, packed)

    def leaves(up, h):
        return jnp.logical_and(z - h >= 0, z + 1 < NZ) if up else jnp.logical_and(z + h < NZ, z >= 1)

    def arrives(up, h):
        return (z - h - 1 >= 0) if up else (z + h + 1 < NZ)

    def to_end(up):
        return (z + 1 == NZ - 1) if up else (z == 1)

    def at_end(up):
        return (z == NZ - 1) if up else (z == 0)

    def each(kind, condition, where, action):
        if kind in (0, 2):
            @pl.when(jnp.logical_and(condition, where))
            def _():
                action(True)

            @pl.when(jnp.logical_and(condition, jnp.logical_not(where)))
            def _():
                action(False)
        else:
            @pl.when(condition)
            def _():
                action(False)

    def start(kind, mb, h):
        for up in (True, False):
            def go(packed):
                if packed:
                    source = z - h if up else z + h
                    slots = sl[source, mb, NZ - 1 if up else 0]
                    row = lax.broadcasted_iota(jnp.int32, (PACKED, T), 0)
                    owner = row // CAP
                    wanted = jnp.full((PACKED, T), -5.0, F32)
                    for e in range(LOCAL):
                        wanted = jnp.where(owner == e, slots[e : e + 1, :], wanted)
                    chosen = (wanted == (row - owner * CAP).astype(F32)).astype(F32).astype(BF16)
                    dense[kind // 2, mb, h] = dot(chosen, item_ref(kind, source, mb)[...]).astype(BF16)
                hop(up, kind, mb, h, packed).start()

            each(kind, leaves(up, h), to_end(up), go)

    def pass_on(kind, mb, h):
        for up in (True, False):
            def take(packed):
                source = z - h - 1 if up else z + h + 1
                copy_of(up, kind, mb, h, source, z - 1 if up else z + 1, packed).wait_recv()

            each(kind, arrives(up, h), at_end(up), take)
        if h + 1 < NZ - 1:
            start(kind, mb, h + 1)

    def weights(n, slot):
        e = lax.rem(n, LOCAL * PIECES) // PIECES
        f = lax.rem(n, PIECES)
        cols = pl.ds(pl.multiple_of(f * PIECE, PIECE), PIECE)
        return (
            pltpu.make_async_copy(w_in.at[e, :, cols], wb1.at[slot], w_sem.at[0, slot]),
            pltpu.make_async_copy(w_back.at[e, cols, :], wb2.at[slot], w_sem.at[1, slot]),
        )

    for copy in weights(0, 0):
        copy.start()
    for ref in (gi, gd):
        for source in range(NZ):
            for mb in range(MB):
                ref[source, mb, PACKED:T, :] = jnp.zeros((T - PACKED, D), BF16)
    for row, ref in enumerate((v0, v1, v2, v3, v4)):
        vec[row : row + 1, :] = ref[...].reshape(1, D)
    vec[5:7, :] = qv[...]
    vec[7:8, :] = jnp.zeros((1, D), F32)
    lane = lax.broadcasted_iota(jnp.int32, (1, 32), 1)
    part = lax.rem(lane, 8)
    expert_of = jnp.where(part < LOCAL, (lane // 8) * LOCAL + part, -7)
    chosen_all = jnp.logical_or(routes[:, 0:1] == expert_of, routes[:, 1:2] == expert_of)
    chosen_all = chosen_all.astype(F32).astype(BF16)
    token = lax.broadcasted_iota(jnp.int32, (MB * SEQ, T), 0)
    column = lax.broadcasted_iota(jnp.int32, (MB * SEQ, T), 1)
    for mb in range(MB):
        here = jnp.logical_and(token == column + mb * SEQ, column < SEQ).astype(F32).astype(BF16)
        ahead = jnp.logical_and(token >= mb * SEQ, token < column + mb * SEQ).astype(F32).astype(BF16)
        table = dot(chosen_all, here, TN)
        tab_o[mb] = table
        slots = jnp.where(table > 0.5, dot(chosen_all, ahead, TN), -1.0)
        for p in range(NZ):
            sl[z, mb, p] = slots[8 * p : 8 * p + 8, :]
        tw_o[mb] = dot(here, tok[...], TN).astype(BF16)
        gd[z, mb] = dot(here, dout[...], TN).astype(BF16)
    barrier = pltpu.get_barrier_semaphore()
    for d in range(1, NZ):
        pl.semaphore_signal(barrier, inc=1, device_id=(dp, lax.rem(z + d, NZ)), device_id_type=MESH)
    pl.semaphore_wait(barrier, NZ - 1)
    start(3, 0, 0)
    start(0, 0, 0)
    start(3, 1, 0)
    own = [pltpu.make_async_copy(gd.at[z, mb], dw_o.at[mb], d_sem.at[mb]) for mb in range(MB)]
    for copy in own:
        copy.start()

    qkv_s[T:KEYS, :] = jnp.zeros((KEYS - T, 3 * D), BF16)
    bb_o[...] = jnp.zeros_like(bb_o)
    bi_o[...] = jnp.zeros_like(bi_o)

    def forward(mb, carry):
        x = tw_o[mb].astype(F32)
        normed = (normal(x)[0] * vec[0:1] + vec[1:2]).astype(BF16)
        for c in range(3):
            cols = slice(c * D, (c + 1) * D)
            part = dot(normed, wqkv[:, cols])
            if c != 1:
                row = 5 if c == 0 else 6
                part = part + vec[row : row + 1]
            qkv_s[0:T, cols] = part.astype(BF16)

        def heads(p, carry):
            at = [pl.ds(pl.multiple_of(c * D + p * 128, 128), 128) for c in range(3)]
            q, k, v = qkv_s[0:T, at[0]], qkv_s[:, at[1]], qkv_s[:, at[2]]
            mixed = jnp.zeros((T, 128), F32)
            for which in (0, 1):
                mask = half_mask(which)
                probs = attention_probs(dot(q, k * mask, NT) * HEAD_DIM ** (-0.5))
                mixed = mixed + dot(probs.astype(BF16), v * mask)
            mixed_s[:, at[0]] = mixed.astype(BF16)
            return carry

        lax.fori_loop(0, PAIRS, heads, 0, unroll=3)
        qkv_o[mb] = qkv_s[0:T, :]
        mixed_o[mb] = mixed_s[...]
        resid = x + dot(mixed_s[...], wout[...]) + vec[4:5]
        resid_o[mb] = resid
        inner = (normal(resid)[0] * vec[2:3] + vec[3:4]).astype(BF16)
        gi[z, mb] = inner
        real = lax.rem(lax.broadcasted_iota(jnp.int32, (32, T), 0), 8) < LOCAL
        probs = route_softmax(dot(wrt[...], inner, NT), real)
        rp_o[mb] = probs
        gates = tab_o[mb] * probs
        for p in range(NZ):
            sg[z, mb, p] = gates[8 * p : 8 * p + 8, :]

        @pl.when(mb == 0)
        def _():
            start(1, 0, 0)
            start(2, 0, 0)

        return carry

    lax.fori_loop(0, MB, forward, 0)
    middle = jnp.logical_and(z > 0, z < NZ - 1)

    @pl.when(jnp.logical_not(middle))
    def _():
        for kind in range(3):
            start(kind, 1, 0)

    for h in range(NZ - 1):
        for kind in (3, 0, 1, 2):
            pass_on(kind, 0, h)
        pass_on(3, 1, h)

    @pl.when(middle)
    def _():
        for kind in range(3):
            start(kind, 1, 0)

    def micro(mb, carry):
        @pl.when(mb == 1)
        def _():
            for kind in range(3):
                pass_on(kind, 1, 2)

        def spread(src, carry):
            pick = pick_matrix(sl[src, mb, z])
            gate = sg[src, mb, z]
            row = lax.broadcasted_iota(jnp.int32, (ROWS, T), 0)
            owner = row // CAP_ROWS
            place = row - owner * CAP_ROWS
            unpack = jnp.logical_and(
                place < CAP, lax.broadcasted_iota(jnp.int32, (ROWS, T), 1) == owner * CAP + place
            ).astype(F32)
            packed = jnp.logical_and(jnp.logical_or(z == 0, z == NZ - 1), src != z)
            low = jnp.where(packed, unpack, pick).astype(BF16)
            rows_x = dot(low, gi[src, mb]).astype(BF16)
            rows_c = dot(low, gd[src, mb])
            at = pl.ds(pl.multiple_of(mb * ROWS + src * CAP_ROWS, 16), CAP_ROWS)
            here = pl.ds(pl.multiple_of(src * CAP_ROWS, 16), CAP_ROWS)
            for e in range(LOCAL):
                part = slice(e * CAP_ROWS, (e + 1) * CAP_ROWS)
                gate_rows = jnp.sum(pick[part] * gate[e : e + 1, :], axis=1, keepdims=True)
                grad = (rows_c[part] * gate_rows).astype(BF16)
                xs[e, at, :] = rows_x[part]
                gs[e, at, :] = grad
                cs[e, here, :] = rows_c[part].astype(BF16)
                rgs[e, here, :] = jnp.broadcast_to(gate_rows, (CAP_ROWS, 128))
                bb_o[e : e + 1, :] += jnp.sum(grad.astype(F32), axis=0, keepdims=True)
            return carry

        lax.fori_loop(0, NZ, spread, 0)
        rows = pl.ds(pl.multiple_of(mb * ROWS, 16), ROWS)

        def expert(e, carry):
            acc_o[...] = jnp.zeros_like(acc_o)
            acc_g[...] = jnp.zeros_like(acc_g)

            def step(f, carry):
                n = (mb * LOCAL + e) * PIECES + f
                slot = lax.rem(n, 2)
                cols = pl.ds(pl.multiple_of(f * PIECE, PIECE), PIECE)

                @pl.when(n + 1 < LOCAL * PIECES * MB)
                def _():
                    for copy in weights(n + 1, 1 - slot):
                        copy.start()

                @pl.when(n >= 2)
                def _():
                    for copy in stores(n - 2, slot):
                        copy.wait()

                for copy in weights(n, slot):
                    copy.wait()
                hid = dot(xs[e, rows, :], wb1[slot]) + b_in[pl.ds(e, 1), cols]
                square = hid * hid
                bend = jnp.tanh(hid * (0.7978845608 + (0.7978845608 * 0.044715) * square))
                half = 0.5 + 0.5 * bend
                act = (hid * half).astype(BF16)
                slope = half + (0.5 * hid) * (1.0 - bend * bend) * (
                    0.7978845608 + (3 * 0.7978845608 * 0.044715) * square
                )

                act_st[slot] = act
                acc_o[...] += dot(act, wb2[slot])
                grad = (dot(gs[e, rows, :], wb2[slot], NT) * slope).astype(BF16)
                gh_st[slot] = grad
                acc_g[...] += dot(grad, wb1[slot], NT)
                bi_o[pl.ds(e, 1), cols] += jnp.sum(grad.astype(F32), axis=0, keepdims=True)
                for copy in stores(n, slot):
                    copy.start()
                return carry

            lax.fori_loop(0, PIECES, step, 0)
            out = (acc_o[...] + b_back[pl.ds(e, 1), :]).astype(BF16).astype(F32)
            gg = jnp.sum(out * cs[e].astype(F32), axis=1, keepdims=True)
            scaled = (out * rgs[e][:, 0:1]).astype(BF16)
            back = acc_g[...].astype(BF16)
            at = pl.ds(pl.multiple_of(e * CAP_ROWS, 16), CAP_ROWS)
            for src in range(NZ):
                part = slice(src * CAP_ROWS, (src + 1) * CAP_ROWS)
                os_[src, at, :] = scaled[part]
                grs[src, at, :] = back[part]
                ggs[src, at, :] = jnp.broadcast_to(gg[part], (CAP_ROWS, 128))

            @pl.when(jnp.logical_and(mb == 1, e == jnp.where(middle, 1, 0)))
            def _():
                for d in range(1, NZ):
                    sent_home(d).start()
                own_home().start()

            @pl.when(jnp.logical_and(mb == 0, e == 0))
            def _():
                for kind in range(3):
                    pass_on(kind, 1, 0)

            @pl.when(jnp.logical_and(mb == 0, e == 2))
            def _():
                for kind in range(3):
                    pass_on(kind, 1, 1)

            return carry

        def stores(n, slot):
            m = n // (LOCAL * PIECES)
            e = lax.rem(n, LOCAL * PIECES) // PIECES
            f = lax.rem(n, PIECES)
            at = (e, pl.ds(pl.multiple_of(m * ROWS, 16), ROWS), pl.ds(pl.multiple_of(f * PIECE, PIECE), PIECE))
            return (
                pltpu.make_async_copy(act_st.at[slot], act_o.at[at], st_sem.at[0, slot]),
                pltpu.make_async_copy(gh_st.at[slot], gh_o.at[at], st_sem.at[1, slot]),
            )

        lax.fori_loop(0, LOCAL, expert, 0)

        @pl.when(mb == 1)
        def _():
            for slot in (0, 1):
                for copy in stores(LOCAL * PIECES * MB - 2 + slot, slot):
                    copy.wait()

        @pl.when(mb == 1)
        def _():
            for src in range(NZ):
                kept(0, src).wait()
            for d in range(1, NZ):
                sent_home(d).wait_send()
            own_home().wait()

        def gather(src, carry):
            pick = pick_matrix(sl[src, mb, z])
            low = pick.astype(BF16)
            pb_s[src] = dot(low, os_[src], TN).astype(BF16)
            pg_s[src] = dot(low, grs[src], TN).astype(BF16)
            kept(mb, src).start()
            for e in range(LOCAL):
                part = slice(e * CAP_ROWS, (e + 1) * CAP_ROWS)
                gg_o[src, mb, e : e + 1, :] = jnp.sum(
                    pick[part] * ggs[src, part, 0:1], axis=0, keepdims=True
                )

            @pl.when(mb == 1)
            def _():
                kept_grad(src).start()

            return carry

        lax.fori_loop(0, NZ, gather, 0)

        @pl.when(mb == 1)
        def _():
            for src in range(NZ):
                kept(1, src).wait()
                kept_grad(src).wait()

        return carry

    def kept(mb, src):
        return pltpu.make_async_copy(pb_s.at[src], pb_o.at[mb, src], p_sem.at[0, src])

    def kept_grad(src):
        return pltpu.make_async_copy(pg_s.at[src], pg_o.at[src], p_sem.at[1, src])

    def sent_home(d):
        target = lax.rem(z + d, NZ)
        return pltpu.make_async_remote_copy(
            src_ref=pg_s.at[target], dst_ref=home_o.at[z], send_sem=h_send.at[d - 1], recv_sem=h_recv.at[d - 1],
            device_id=(dp, target), device_id_type=MESH,
        )

    def own_home():
        return pltpu.make_async_copy(pg_s.at[z], home_o.at[z], d_sem.at[MB])

    gg_o[...] = jnp.zeros_like(gg_o)
    lax.fori_loop(0, MB, micro, 0)
    last = (
        pltpu.make_async_copy(xs, x_o, x_sem.at[0]),
        pltpu.make_async_copy(gs, gp_o, x_sem.at[1]),
    )
    for copy in last:
        copy.start()
    for copy in last:
        copy.wait()
    for d in range(1, NZ):
        source = lax.rem(z + NZ - d, NZ)
        pltpu.make_async_remote_copy(
            src_ref=home_o.at[source], dst_ref=home_o.at[source], send_sem=h_send.at[d - 1],
            recv_sem=h_recv.at[d - 1], device_id=(dp, source), device_id_type=MESH,
        ).wait_recv()
    for copy in own:
        copy.wait()
    for mb in range(MB):
        for kind in range(4):
            for h in range(NZ - 1):
                for up in (True, False):
                    each(
                        kind, leaves(up, h), to_end(up),
                        lambda packed: hop(up, kind, mb, h, packed).wait_send(),
                    )


def dispatch_call(*operands):
    vm = pl.BlockSpec(memory_space=pltpu.VMEM)
    hb = pl.BlockSpec(memory_space=pl.ANY)
    S = jax.ShapeDtypeStruct
    rows = MB * ROWS
    outs = [
        (S((8, D), F32), vm),
        (S((MB, 32, T), F32), vm),
        (S((MB, T, D), BF16), vm),
        (S((MB, T, 3 * D), BF16), vm),
        (S((MB, T, D), BF16), vm),
        (S((MB, T, D), F32), vm),
        (S((MB, 32, T), F32), vm),
        (S((NZ, MB, 8, T), F32), vm),
        (S((LOCAL, D), F32), vm),
        (S((LOCAL, 4 * CHUNK), F32), vm),
        (S((MB, T, D), BF16), hb),
        (S((LOCAL, rows, D), BF16), hb),
        (S((LOCAL, rows, D), BF16), hb),
        (S((LOCAL, rows, 4 * CHUNK), BF16), hb),
        (S((LOCAL, rows, 4 * CHUNK), BF16), hb),
        (S((MB, NZ, T, D), BF16), hb),
        (S((NZ, T, D), BF16), hb),
        (S((NZ, T, D), BF16), hb),
    ]
    V = pltpu.VMEM
    DMA = pltpu.SemaphoreType.DMA
    return pl.pallas_call(
        dispatch_kernel,
        out_shape=[o[0] for o in outs],
        in_specs=[vm] * 14 + [hb] * 2,
        out_specs=[o[1] for o in outs],
        scratch_shapes=[
            V((NZ, MB, T, D), BF16), V((NZ, MB, T, D), BF16), V((NZ, MB, NZ, 8, T), F32), V((NZ, MB, NZ, 8, T), F32), V((2, MB, NZ - 1, PACKED, D), BF16),
            V((KEYS, 3 * D), BF16), V((T, D), BF16), V((8, 128), F32),
            V((LOCAL, rows, D), BF16), V((LOCAL, rows, D), BF16), V((LOCAL, ROWS, D), BF16),
            V((LOCAL, ROWS, 128), F32), V((NZ, ROWS, 128), F32),
            V((2, D, PIECE), BF16), V((2, PIECE, D), BF16),
            V((2, ROWS, PIECE), BF16), V((2, ROWS, PIECE), BF16),
            V((ROWS, D), F32), V((ROWS, D), F32),
            V((NZ, ROWS, D), BF16), V((NZ, ROWS, D), BF16),
            V((NZ, T, D), BF16), V((NZ, T, D), BF16),
            DMA((2, 4 * MB, NZ - 1)), DMA((2, 4 * MB, NZ - 1)), DMA((MB + 1,)), DMA((2, 2)), DMA((2, 2)),
            DMA((2,)), DMA((2, NZ)), DMA((NZ - 1,)), DMA((NZ - 1,)),
        ],
        compiler_params=pltpu.CompilerParams(
            collective_id=1, has_side_effects=True, vmem_limit_bytes=58 << 20
        ),
        name="dispatch",
    )(*operands)


HIDDEN = 4 * CHUNK
PART = HIDDEN // 8
BAND = D // 8
SHARE = 400
EXTRA = 128
TOTAL = 8 * SHARE


def add_low(a, b):
    return (a.astype(F32) + b.astype(F32)).astype(BF16)


def grads_kernel(
    vec, tab, wrt, bb, bi, rp,
    tok, dout, wqkv, wout, qkv, mixed, resid, gg, xr, gp, act, gh, pb, pg, pg0,
    block_o, ig_o, ar_o, kb_o, ki_o, lb_o, li_o, land_o,
    core_b, core_i, st1_b, st1_i, ar_core, ar_z, ar_xy1, ar_xy2, ar_t,
    ggr,
    c_send, c_recv, s1_send, s1_recv, s2_send, s2_recv, r_send, r_recv, g_send, g_recv,
    ac_send, ac_recv, az_send, az_recv, ax_send, ax_recv, zz_send, zz_recv, cc_send, cc_recv,
    l_sem, o_sem, f_sem,
):
    dp = lax.axis_index("dp")
    z = lax.axis_index("expert")
    y, x, c = dp // 4, lax.rem(dp // 2, 2), lax.rem(dp, 2)
    yx = y * 2 + x
    partner = (yx * 2 + (1 - c), z)
    flips = ((y * 2 + (1 - x)), ((1 - y) * 2 + x))
    across = (1 - y) * 2 + (1 - x)

    def remote(src, dst, ssem, rsem, target):
        return pltpu.make_async_remote_copy(
            src_ref=src, dst_ref=dst, send_sem=ssem, recv_sem=rsem, device_id=target, device_id_type=MESH
        )

    barrier = pltpu.get_barrier_semaphore()
    for target in [partner, (flips[0] * 2 + c, z), (flips[1] * 2 + c, z)]:
        pl.semaphore_signal(barrier, inc=1, device_id=target, device_id_type=MESH)
    for d in range(1, NZ):
        pl.semaphore_signal(barrier, inc=1, device_id=(dp, lax.rem(z + d, NZ)), device_id_type=MESH)
    pl.semaphore_wait(barrier, 6)

    def gate_copy(d):
        return remote(gg.at[lax.rem(z + d, NZ)], ggr.at[z], g_send.at[d - 1], g_recv.at[d - 1], (dp, lax.rem(z + d, NZ)))

    for d in range(1, NZ):
        gate_copy(d).start()
    own_gate = pltpu.make_async_copy(gg.at[z], ggr.at[z], l_sem.at[0])
    own_gate.start()

    def home(item, d):
        target = lax.rem(z + d, NZ)
        part = pg.at[target] if item == 0 else pb.at[item - 1, target]
        return remote(
            part, land_o.at[item, z], r_send.at[item, d - 1], r_recv.at[item, d - 1], (dp, target)
        )

    def arrived(item):
        for d in range(1, NZ):
            source = lax.rem(z + NZ - d, NZ)
            ref = land_o.at[item, source]
            remote(ref, ref, r_send.at[item, d - 1], r_recv.at[item, d - 1], (dp, source)).wait_recv()

    def load(quad, sources):
        copies = [pltpu.make_async_copy(ref, quad[i], l_sem.at[1 + i]) for i, ref in enumerate(sources)]
        for copy in copies:
            copy.start()
        for copy in copies:
            copy.wait()

    def load_item(quad, item):
        arrived(item)
        own = pg.at[z] if item == 0 else pb.at[item - 1, z]
        load(quad, [own] + [land_o.at[item, lax.rem(z + d, NZ)] for d in range(1, NZ)])

    def quad_sum(quad):
        parts = [ref[...].astype(F32) for ref in quad]
        return (parts[0] + parts[1]) + (parts[2] + parts[3])

    cores, lands1, lands2, keeps = (core_b, core_i), (st1_b, st1_i), (lb_o, li_o), (kb_o, ki_o)

    def core_copy(kind, e, src):
        return remote(src, cores[kind].at[e], c_send.at[kind, e], c_recv.at[kind, e], partner)

    def hop1(kind, e, slot):
        block = flips[kind] if slot == 0 else across
        return remote(
            cores[kind].at[e, block], lands1[kind].at[e, slot],
            s1_send.at[kind, e, slot], s1_recv.at[kind, e, slot], (flips[kind] * 2 + c, z),
        )

    def hop2(kind, e):
        return remote(
            cores[kind].at[e, flips[1 - kind]], lands2[kind].at[e],
            s2_send.at[kind, e], s2_recv.at[kind, e], (flips[1 - kind] * 2 + c, z),
        )

    def send1(kind, e):
        for slot in (1, 0):
            hop1(kind, e, slot).start()

    def turn(kind, e):
        ref = cores[kind]
        hop1(kind, e, 1).wait_recv()
        ref[e, flips[1 - kind]] = add_low(ref[e, flips[1 - kind]], lands1[kind][e, 1])
        hop2(kind, e).start()
        hop1(kind, e, 0).wait_recv()
        ref[e, yx] = add_low(ref[e, yx], lands1[kind][e, 0])
        keep(kind, e).start()

    def keep(kind, e):
        return pltpu.make_async_copy(cores[kind].at[e, yx], keeps[kind].at[e], f_sem.at[kind, e])

    for item in range(2):
        for d in range(1, NZ):
            home(item, d).start()

    V = pltpu.VMEM
    rows = MB * ROWS

    def attention_grads(one, gqkv_s, nor_s, gat_s, ext):
        def inside(wqkv_s, wout_s, qkv_s, tok_s, dout_s, res_s, gres, gm_s):
            loads = [
                pltpu.make_async_copy(src, dst, o_sem.at[4 + i])
                for i, (src, dst) in enumerate(
                    ((wqkv, wqkv_s), (wout, wout_s))
                )
            ]
            for copy in loads:
                copy.start()
            ext[...] = jnp.zeros_like(ext)
            qkv_s[T:KEYS, :] = jnp.zeros((KEYS - T, 3 * D), BF16)
            for d in range(1, NZ):
                gate_copy(d).wait_send()
                source = lax.rem(z + NZ - d, NZ)
                remote(ggr.at[source], ggr.at[source], g_send.at[d - 1], g_recv.at[d - 1], (dp, source)).wait_recv()
            own_gate.wait()
            for copy in loads:
                copy.wait()

            def image(mb, carry):
                quad = [gqkv_s.at[mb, :, i * D : (i + 1) * D] for i in range(3)] + [gm_s]

                @pl.when(mb == 0)
                def _():
                    load(quad, [pg0.at[p] for p in range(NZ)])

                @pl.when(mb == 1)
                def _():
                    load_item(quad, 0)

                fetches = [
                    pltpu.make_async_copy(src.at[mb], dst, o_sem.at[8 + i])
                    for i, (src, dst) in enumerate(((qkv, qkv_s.at[0:T]), (dout, dout_s), (tok, tok_s), (resid, res_s)))
                ]
                for fetch in fetches:
                    fetch.start()
                gates = jnp.concatenate([ggr[p, mb] for p in range(NZ)], axis=0)
                g = tab[mb] * gates
                probs = rp[mb]
                gl = (probs * (g - jnp.sum(probs * g, axis=0, keepdims=True))).astype(BF16)
                fetches[3].wait()
                n2, r2 = normal(res_s[...])
                inner = (n2 * vec[2:3] + vec[3:4]).astype(BF16)
                wr = dot(gl, inner)
                for p in range(NZ):
                    ext[8 + LOCAL * p : 8 + LOCAL * (p + 1), :] += wr[8 * p : 8 * p + LOCAL]
                gi = quad_sum(quad) + dot(gl, wrt[...], TN)
                ext[5:6, :] += jnp.sum(gi * n2, axis=0, keepdims=True)
                ext[6:7, :] += jnp.sum(gi, axis=0, keepdims=True)
                u = gi * vec[2:3]
                fetches[1].wait()
                grad = dout_s[...].astype(F32) + r2 * (
                    u - jnp.mean(u, -1, keepdims=True) - n2 * jnp.mean(u * n2, -1, keepdims=True)
                )

                @pl.when(mb == 1)
                def _():
                    pltpu.make_async_copy(gres, ig_o.at[0], o_sem.at[12]).wait()

                gres[...] = grad
                low = grad.astype(BF16)
                gat_s[mb] = low
                ext[4:5, :] += jnp.sum(low.astype(F32), axis=0, keepdims=True)
                gm_s[...] = dot(low, wout_s[...], NT).astype(BF16)
                fetches[0].wait()

                def heads(p, carry):
                    at = [pl.ds(pl.multiple_of(i * D + p * 128, 128), 128) for i in range(3)]
                    q, k, v = qkv_s[0:T, at[0]], qkv_s[:, at[1]], qkv_s[:, at[2]]
                    gm = gm_s[:, at[0]]
                    gq = jnp.zeros((T, 128), F32)
                    gk = jnp.zeros((KEYS, 128), F32)
                    gv = jnp.zeros((KEYS, 128), F32)
                    for which in (0, 1):
                        mask = half_mask(which)
                        km = k * mask
                        prob = attention_probs(dot(q, km, NT) * HEAD_DIM ** (-0.5))
                        gpr = dot(gm, v * mask, NT)
                        gs = (prob * (gpr - jnp.sum(prob * gpr, axis=-1, keepdims=True))).astype(BF16)
                        gq = gq + dot(gs, km)
                        gk = gk + dot(gs, q * mask, TN)
                        gv = gv + dot(prob.astype(BF16), gm * mask, TN)
                    gqkv_s[mb, :, at[0]] = (gq * HEAD_DIM ** (-0.5)).astype(BF16)
                    gqkv_s[mb, :, at[1]] = (gk[0:T] * HEAD_DIM ** (-0.5)).astype(BF16)
                    gqkv_s[mb, :, at[2]] = gv[0:T].astype(BF16)
                    return carry

                lax.fori_loop(0, PAIRS, heads, 0, unroll=2)
                for row, i in ((2, 0), (3, 2)):
                    ext[row : row + 1, :] += jnp.sum(
                        gqkv_s[mb, :, i * D : (i + 1) * D].astype(F32), axis=0, keepdims=True
                    )
                gn = dot(gqkv_s[mb], wqkv_s[...], NT)
                fetches[2].wait()
                n1, r1 = normal(tok_s[...].astype(F32))
                nor_s[mb] = (n1 * vec[0:1] + vec[1:2]).astype(BF16)
                ext[0:1, :] += jnp.sum(gn * n1, axis=0, keepdims=True)
                ext[1:2, :] += jnp.sum(gn, axis=0, keepdims=True)
                w = gn * vec[0:1]
                gres[...] += r1 * (
                    w - jnp.mean(w, -1, keepdims=True) - n1 * jnp.mean(w * n1, -1, keepdims=True)
                )
                pltpu.make_async_copy(gres, ig_o.at[mb], o_sem.at[12 + mb]).start()

                @pl.when(mb == 0)
                def _():
                    one(1)

                return carry

            lax.fori_loop(0, MB, image, 0)
            pltpu.make_async_copy(gres, ig_o.at[1], o_sem.at[13]).wait()

        pl.run_scoped(
            inside,
            V((D, 3 * D), BF16), V((D, D), BF16), V((KEYS, 3 * D), BF16), V((T, D), BF16), V((T, D), BF16),
            V((T, D), F32), V((T, D), F32), V((T, D), BF16),
        )

        def shared(a, mix_s):
            mix = pltpu.make_async_copy(mixed, mix_s, o_sem.at[4])
            mix.start()
            for zz in range(NZ):
                @pl.when(z == zz)
                def _():
                    at = 24 + 5 * LOCAL * zz
                    ext[at : at + LOCAL, :] = bb[...]
                    for f in range(4):
                        ext[at + LOCAL * (f + 1) : at + LOCAL * (f + 2), :] = bi[:, f * CHUNK : (f + 1) * CHUNK]
            for i in range(3):
                total = jnp.zeros((D, D), F32)
                for mb in range(MB):
                    total = total + dot(nor_s[mb], gqkv_s[mb, :, i * D : (i + 1) * D], TN)
                a[i * D : (i + 1) * D, :] = total.astype(BF16)
            mix.wait()
            total = jnp.zeros((D, D), F32)
            for mb in range(MB):
                total = total + dot(mix_s[mb], gat_s[mb], TN)
            a[3 * D : 4 * D, :] = total.astype(BF16)
            a[4 * D : TOTAL, :] = ext[...].astype(BF16)

            def share(side, zz):
                return pl.ds(pl.multiple_of((side * NZ + zz) * SHARE, 16), SHARE)

            def to_core(zz):
                return remote(a.at[share(1 - c, zz)], ar_core.at[zz], ac_send.at[zz], ac_recv.at[zz], partner)

            for zz in range(NZ):
                to_core(zz).start()
            for kind in (0, 1):
                turn(kind, 0)

            def along(flow, zz, slot):
                return remote(
                    a.at[share(c, zz)], ar_z.at[flow, slot], az_send.at[flow, slot], az_recv.at[flow, slot],
                    (dp, z - 1 if flow == 0 else z + 1),
                )

            for j in range(NZ):
                zz = j
                to_core(zz).wait_recv()
                a[share(c, zz), :] = add_low(a[share(c, zz), :], ar_core[zz])
            for j in range(NZ - 1):
                @pl.when(z == NZ - 1)
                def _():
                    along(0, j, j).start()

                @pl.when(z == 0)
                def _():
                    along(1, NZ - 1 - j, NZ - 2 - j).start()

            def sum_one(flow, dest, at):
                slot = dest if flow == 0 else dest - 1

                @pl.when(z == at)
                def _():
                    along(flow, dest, slot).wait_recv()
                    a[share(c, dest), :] = add_low(a[share(c, dest), :], ar_z[flow, slot])
                    if at != dest:
                        along(flow, dest, slot).start()

            for d in range(1, NZ):
                home(2, d).start()
            one(2)
            for kind in (0, 1):
                turn(kind, 1)
            for step, order in enumerate((
                ((0, 0, 2), (1, 3, 1)),
                ((0, 1, 2), (1, 3, 2), (1, 2, 1), (0, 0, 1)),
                ((0, 2, 2), (1, 2, 2), (1, 1, 1), (0, 1, 1), (0, 0, 0), (1, 3, 3)),
            )):
                for flow, dest, at in order:
                    sum_one(flow, dest, at)

            halves = (slice(0, 208), slice(208, SHARE))

            def cross(stage_no, half, src):
                dest = (ar_xy1, ar_xy2)[stage_no].at[halves[half]]
                way = half if stage_no == 0 else 1 - half
                return remote(
                    src, dest, ax_send.at[stage_no, half], ax_recv.at[stage_no, half], (flips[way] * 2 + c, z)
                )

            def mine(half):
                start_row = 0 if half == 0 else 208
                size = 208 if half == 0 else SHARE - 208
                return pl.ds(pl.multiple_of((c * NZ + z) * SHARE + start_row, 16), size)

            for half in (0, 1):
                cross(0, half, a.at[mine(half)]).start()
            for half in (0, 1):
                cross(0, half, a.at[mine(half)]).wait_recv()
                ar_t[halves[half], :] = add_low(a[mine(half), :], ar_xy1[halves[half], :])
                cross(1, half, ar_t.at[halves[half]]).start()
            one(3)
            for half in (0, 1):
                cross(1, half, ar_t.at[halves[half]]).wait()
                ar_t[halves[half], :] = add_low(ar_t[halves[half], :], ar_xy2[halves[half], :])
                cross(0, half, a.at[mine(half)]).wait_send()
            for zz in range(NZ):
                to_core(zz).wait_send()
                for flow in (0, 1):
                    slot = zz if flow == 0 else zz - 1
                    if 0 <= slot < NZ - 1:
                        goes = (z > zz) if flow == 0 else (z < zz)

                        @pl.when(goes)
                        def _():
                            along(flow, zz, slot).wait_send()

        pl.run_scoped(shared, V((TOTAL, D), BF16), V((MB, T, D), BF16))

    def body(wg_b, wg_i, act_s, gh_s, x_s, gp_s, xp):
        def fetch(e, which):
            pairs = ((act, act_s), (gp, gp_s), (xr, x_s), (gh, gh_s))
            return [
                pltpu.make_async_copy(pairs[i][0].at[e], pairs[i][1], o_sem.at[i]) for i in which
            ]

        def pull(e, which):
            for copy in fetch(e, which):
                copy.start()

        def ready(e, which):
            for copy in fetch(e, which):
                copy.wait()

        pull(0, (0, 1, 2, 3))

        def one(e):
            def back_block(k, side):
                at = pl.ds(pl.multiple_of((2 * k + side) * PART, 128), PART)
                return dot(act_s[:, at], gp_s[...], TN)

            ready(e, (0, 1))

            if e > 0:
                core_copy(0, e - 1, wg_b).wait_send()

            def other_b(k, carry):
                wg_b[k] = back_block(k, 1 - c).astype(BF16)
                return carry

            lax.fori_loop(0, 4, other_b, 0, unroll=2)
            core_copy(0, e, wg_b).start()
            ready(e, (2, 3))
            for side in (0, 1):
                for k in range(4):
                    band = (2 * k + side) * BAND
                    xp[side, :, k * BAND : (k + 1) * BAND] = x_s[:, band : band + BAND]

            if e > 0:
                core_copy(1, e - 1, wg_i).wait_send()

            def other_i(f, carry):
                at = pl.ds(pl.multiple_of(f * CHUNK, 128), CHUNK)
                grad = dot(xp[1 - c], gh_s[:, at], TN).astype(BF16)
                for k in range(4):
                    wg_i[k, :, at] = grad[k * BAND : (k + 1) * BAND]
                return carry

            lax.fori_loop(0, 4, other_i, 0, unroll=2)
            core_copy(1, e, wg_i).start()
            core_copy(0, e, wg_b).wait_recv()

            def own_b(k, carry):
                core_b[e, k] = (core_b[e, k].astype(F32) + back_block(k, c)).astype(BF16)
                return carry

            lax.fori_loop(0, 4, own_b, 0, unroll=2)

            send1(0, e)
            if e < LOCAL - 1:
                pull(e + 1, (0, 1))

            core_copy(1, e, wg_i).wait_recv()

            def own_i(f, carry):
                at = pl.ds(pl.multiple_of(f * CHUNK, 128), CHUNK)
                grad = dot(xp[c], gh_s[:, at], TN)
                for k in range(4):
                    core_i[e, k, :, at] = (
                        core_i[e, k, :, at].astype(F32) + grad[k * BAND : (k + 1) * BAND]
                    ).astype(BF16)
                return carry

            lax.fori_loop(0, 4, own_i, 0, unroll=2)

            send1(1, e)
            if e < LOCAL - 1:
                pull(e + 1, (2, 3))

        one(0)
        pl.run_scoped(
            functools.partial(attention_grads, one),
            V((MB, T, 3 * D), BF16), V((MB, T, D), BF16), V((MB, T, D), BF16), V((EXTRA, D), F32),
        )
        core_copy(0, LOCAL - 1, wg_b).wait_send()
        core_copy(1, LOCAL - 1, wg_i).wait_send()

    pl.run_scoped(
        body,
        V((4, PART, D), BF16), V((4, BAND, HIDDEN), BF16), V((rows, HIDDEN), BF16), V((rows, HIDDEN), BF16),
        V((rows, D), BF16), V((rows, D), BF16), V((2, rows, D // 2), BF16),
    )

    def place(zz):
        return ar_o.at[pl.ds(pl.multiple_of((c * NZ + zz) * SHARE, 16), SHARE)]

    own_share = pltpu.make_async_copy(ar_t, place(z), l_sem.at[6])
    own_share.start()

    def spread(up, h):
        source = z - h if up else z + h
        index = (0 if up else 1, h)
        return remote(
            ar_t if h == 0 else place(source), place(source), zz_send.at[index], zz_recv.at[index],
            (dp, z + 1 if up else z - 1),
        )

    def leaves(up, h):
        return jnp.logical_and(z - h >= 0, z + 1 < NZ) if up else jnp.logical_and(z + h < NZ, z >= 1)

    def to_partner(src, k, zz):
        return remote(src, place(zz), cc_send.at[k], cc_recv.at[k], partner)

    for up in (True, False):
        @pl.when(leaves(up, 0))
        def _():
            spread(up, 0).start()

    to_partner(ar_t, 0, z).start()
    def block_out(mb):
        def image_out(base, quad_s, low):
            quad = [quad_s.at[i] for i in range(NZ)]
            fetch = pltpu.make_async_copy(resid.at[mb], base, l_sem.at[5])
            fetch.start()
            load_item(quad, 1 + mb)
            fetch.wait()
            low[...] = (base[...] + quad_sum(quad)).astype(BF16)
            store = pltpu.make_async_copy(low, block_o.at[mb], l_sem.at[7])
            store.start()
            store.wait()

        pl.run_scoped(image_out, V((T, D), F32), V((NZ, T, D), BF16), V((T, D), BF16))

    block_out(0)
    for h in range(NZ - 1):
        for up in (True, False):
            source = z - h - 1 if up else z + h + 1

            @pl.when((z - h - 1 >= 0) if up else (z + h + 1 < NZ))
            def _():
                index = (0 if up else 1, h)
                remote(
                    place(source), place(source), zz_send.at[index], zz_recv.at[index],
                    (dp, z - 1 if up else z + 1),
                ).wait_recv()
                k = lax.rem(source - z + NZ, NZ)
                to_partner(place(source), k, source).start()

            if h + 1 < NZ - 1:
                @pl.when(leaves(up, h + 1))
                def _():
                    spread(up, h + 1).start()
        if h < 2:
            for kind in (0, 1):
                turn(kind, 2 + h)
        if h == 1:
            block_out(1)
    own_share.wait()
    for k in range(NZ):
        zz = lax.rem(z + k, NZ)
        src = ar_t if k == 0 else place(zz)
        to_partner(src, k, zz).wait_send()
        other = ar_o.at[pl.ds(pl.multiple_of(((1 - c) * NZ + zz) * SHARE, 16), SHARE)]
        remote(other, other, cc_send.at[k], cc_recv.at[k], partner).wait_recv()
    for h in range(NZ - 1):
        for up in (True, False):
            @pl.when(leaves(up, h))
            def _():
                spread(up, h).wait_send()
    for item in range(3):
        for d in range(1, NZ):
            home(item, d).wait_send()
    for kind in (0, 1):
        for e in range(LOCAL):
            for slot in (0, 1):
                hop1(kind, e, slot).wait_send()
            hop2(kind, e).wait()
            keep(kind, e).wait()


def grads_call(*operands):
    vm = pl.BlockSpec(memory_space=pltpu.VMEM)
    hb = pl.BlockSpec(memory_space=pl.ANY)
    S = jax.ShapeDtypeStruct
    V = pltpu.VMEM
    DMA = pltpu.SemaphoreType.DMA
    outs = [
        (S((MB, T, D), BF16), hb),
        (S((MB, T, D), F32), hb),
        (S((TOTAL, D), BF16), hb),
        (S((LOCAL, PART, D), BF16), hb),
        (S((LOCAL, BAND, HIDDEN), BF16), hb),
        (S((LOCAL, PART, D), BF16), hb),
        (S((LOCAL, BAND, HIDDEN), BF16), hb),
        (S((3, NZ, T, D), BF16), hb),
    ]
    return pl.pallas_call(
        grads_kernel,
        out_shape=[o[0] for o in outs],
        in_specs=[vm] * 6 + [hb] * 15,
        out_specs=[o[1] for o in outs],
        scratch_shapes=[
            V((LOCAL, 4, PART, D), BF16), V((LOCAL, 4, BAND, HIDDEN), BF16),
            V((LOCAL, 2, PART, D), BF16), V((LOCAL, 2, BAND, HIDDEN), BF16),
            V((NZ, SHARE, D), BF16), V((2, NZ - 1, SHARE, D), BF16),
            V((SHARE, D), BF16), V((SHARE, D), BF16), V((SHARE, D), BF16),
            V((NZ, MB, 8, T), F32),
            DMA((2, LOCAL)), DMA((2, LOCAL)), DMA((2, LOCAL, 2)), DMA((2, LOCAL, 2)), DMA((2, LOCAL)), DMA((2, LOCAL)),
            DMA((3, NZ - 1)), DMA((3, NZ - 1)), DMA((NZ - 1,)), DMA((NZ - 1,)),
            DMA((NZ,)), DMA((NZ,)), DMA((2, NZ - 1)), DMA((2, NZ - 1)), DMA((2, 2)), DMA((2, 2)),
            DMA((2, NZ - 1)), DMA((2, NZ - 1)), DMA((NZ,)), DMA((NZ,)),
            DMA((8,)), DMA((14,)), DMA((2, LOCAL)),
        ],
        compiler_params=pltpu.CompilerParams(
            collective_id=2, has_side_effects=True, vmem_limit_bytes=63 << 20
        ),
        name="grads",
    )(*operands)


def finish_kernel(
    ar, kb, ki, lb, li, block, ig,
    block_o, ig_o, g1_o, s1_o, qkv_o, qv_o, wout_o, bout_o, g2_o, s2_o, route_o, wi_o, bi_o, wb_o, bb_o,
    ar_s, kb_s, ki_s, lb_s, li_s, block_s, ig_s, wide, narrow, out_i, out_b, tall,
    in_sem, out_sem,
):
    dp = lax.axis_index("dp")
    z = lax.axis_index("expert")

    def fetch(src, dst, i):
        copy = pltpu.make_async_copy(src, dst, in_sem.at[i])
        copy.start()
        return copy

    back = [(fetch(kb.at[e], kb_s.at[e], e), fetch(lb.at[e], lb_s.at[e], 4 + e)) for e in range(LOCAL)]
    ahead = [(fetch(ki.at[e], ki_s.at[e], 8 + e), fetch(li.at[e], li_s.at[e], 12 + e)) for e in range(LOCAL)]
    dense = [
        fetch(ar.at[i * D : (i + 1) * D], ar_s.at[i * D : (i + 1) * D], 16 + i) for i in range(4)
    ]
    few = fetch(ar.at[4 * D : TOTAL], ar_s.at[4 * D : TOTAL], 20)
    rows_in = (fetch(block, block_s, 21), fetch(ig, ig_s, 22))
    sent = []

    def send(src, dst):
        copy = pltpu.make_async_copy(src, dst, out_sem.at[len(sent)])
        copy.start()
        sent.append(copy)

    for pairs, kept, landed, out, dst in ((back, kb_s, lb_s, out_b, wb_o), (ahead, ki_s, li_s, out_i, wi_o)):
        for e in range(LOCAL):
            for copy in pairs[e]:
                copy.wait()
            out[e] = kept[e].astype(F32) + landed[e].astype(F32)
            send(out.at[e], dst.at[e])
    for i in range(4):
        dense[i].wait()
        part = ar_s[i * D : (i + 1) * D, :].astype(F32)
        if i < 3:
            wide[i] = part
            send(wide.at[i], qkv_o.at[:, i * D : (i + 1) * D])
        else:
            narrow[...] = part
            send(narrow, wout_o)
    few.wait()
    low = ar_s[4 * D : TOTAL, :]
    ext = low.astype(F32)
    for row, ref in ((0, g1_o), (1, s1_o), (4, bout_o), (5, g2_o), (6, s2_o)):
        ref[...] = ext[row]
    qv_o[...] = ext[2:4]
    route_o[...] = ext[8 : 8 + NZ * LOCAL]

    def pick(first):
        at = lax.broadcasted_iota(jnp.int32, (8, EXTRA), 0) + first
        return dot((at == lax.broadcasted_iota(jnp.int32, (8, EXTRA), 1)).astype(F32).astype(BF16), low)

    base = 24 + 5 * LOCAL * z
    column = lax.broadcasted_iota(jnp.int32, (D, BAND), 1) + dp * BAND
    chosen = (column == lax.broadcasted_iota(jnp.int32, (D, BAND), 0)).astype(F32).astype(BF16)
    bb_o[...] = dot(pick(base).astype(BF16), chosen)[:LOCAL]
    rows = pick(base + LOCAL * (dp // 2 + 1))
    bi_o[...] = jnp.where(lax.rem(dp, 2) == 0, rows[:, :PART], rows[:, PART:])[:LOCAL]
    for copy in rows_in:
        copy.wait()
    for mb in range(MB):
        at = slice(mb * SEQ, (mb + 1) * SEQ)
        tall[at, :] = block_s[mb].astype(F32)[:SEQ]
        ig_o[at, :] = ig_s[mb, :SEQ, :]
    block_o[...] = tall[0 : MB * SEQ, :].astype(BF16)
    for copy in sent:
        copy.wait()


def finish_call(*operands):
    vm = pl.BlockSpec(memory_space=pltpu.VMEM)
    hb = pl.BlockSpec(memory_space=pl.ANY)
    S = jax.ShapeDtypeStruct
    V = pltpu.VMEM
    rows = MB * SEQ
    vector = (S((D,), F32), vm)
    outs = [
        (S((rows, D), BF16), vm),
        (S((rows, D), F32), vm),
        vector,
        vector,
        (S((D, 3 * D), F32), hb),
        (S((2, D), F32), vm),
        (S((D, D), F32), hb),
        vector,
        vector,
        vector,
        (S((NZ * LOCAL, D), F32), vm),
        (S((LOCAL, BAND, HIDDEN), F32), hb),
        (S((LOCAL, PART), F32), vm),
        (S((LOCAL, PART, D), F32), hb),
        (S((LOCAL, BAND), F32), vm),
    ]
    return pl.pallas_call(
        finish_kernel,
        out_shape=[o[0] for o in outs],
        in_specs=[hb] * 7,
        out_specs=[o[1] for o in outs],
        scratch_shapes=[
            V((TOTAL, D), BF16),
            V((LOCAL, PART, D), BF16), V((LOCAL, BAND, HIDDEN), BF16), V((LOCAL, PART, D), BF16), V((LOCAL, BAND, HIDDEN), BF16),
            V((MB, T, D), BF16), V((MB, T, D), F32), V((3, D, D), F32), V((D, D), F32),
            V((LOCAL, BAND, HIDDEN), F32), V((LOCAL, PART, D), F32), V((400, D), F32),
            pltpu.SemaphoreType.DMA((23,)), pltpu.SemaphoreType.DMA((12,)),
        ],
        compiler_params=pltpu.CompilerParams(vmem_limit_bytes=58 << 20),
        name="finish",
    )(*operands)

def fast_body(
    tokens, routes, gain_one, shift_one, w_qkv, qv_bias, w_out, out_bias, gain_two, shift_two,
    w_route, w_in, b_in, w_back, b_back, d_out,
):
    wrt = jnp.pad(w_route.T.reshape(NZ, LOCAL, D), ((0, 0), (0, 8 - LOCAL), (0, 0))).reshape(32, D)
    (vec, tab, tw, qkv, mixed, resid, rp, gg, bb, bi, dw, xr, gp, act, gh, pb, pg, pg0) = dispatch_call(
        tokens, d_out, routes, gain_one, shift_one, gain_two, shift_two, out_bias, qv_bias,
        w_qkv, w_out, wrt, b_in, b_back, w_in, w_back,
    )
    block, ig, ar, kb, ki, lb, li, _ = grads_call(
        vec, tab, wrt, bb, bi, rp, tw, dw, w_qkv, w_out, qkv, mixed, resid, gg, xr, gp, act, gh, pb, pg, pg0
    )
    out = list(finish_call(ar, kb, ki, lb, li, block, ig))
    out[10] = out[10].T
    return tuple(out)


def solution(mesh):
    fast = mesh.shape["dp"] == 8 and mesh.shape["expert"] == NZ
    return jax.shard_map(
        fast_body if fast else general_body,
        mesh=mesh,
        in_specs=(
            P(("dp", "expert"), None),
            P(("dp", "expert"), None),
            P(),
            P(),
            P(),
            P(),
            P(),
            P(),
            P(),
            P(),
            P(),
            P("expert", None, None),
            P("expert", None),
            P("expert", None, None),
            P("expert", None),
            P(("dp", "expert"), None),
        ),
        out_specs=(
            P(("dp", "expert"), None),
            P(("dp", "expert"), None),
            P(),
            P(),
            P(),
            P(),
            P(),
            P(),
            P(),
            P(),
            P(),
            P("expert", "dp", None),
            P("expert", "dp"),
            P("expert", "dp", None),
            P("expert", "dp"),
        ),
        check_vma=False,
    )
```
